32 devices in a mesh: rows: 16 (over z, x, core), seq: 2 (over y).
Axes of the slice: x: 2, y: 2, z: 4, core: 2. Of those that a mesh axis runs over, the one named last changes fastest.
Arguments:
- block_input: bfloat16 [64, 2048, 768], P('rows', 'seq'), may hold values from -6 to 6
- segment_ids: int32 [64, 2048], P('rows', 'seq'), may hold values from 0 to 3, as said below
- norm1_gain: float32 [768], replicated, may hold values from 0.1 to 1.9
- norm1_shift: float32 [768], replicated, may hold values from -3 to 3
- qkv_weight: bfloat16 [768, 2304], replicated, may hold values from -0.21875 to 0.21875
- qv_bias: float32 [1536], replicated, may hold values from -3 to 3
- proj_weight: bfloat16 [768, 768], replicated, may hold values from -6 to 6
- proj_bias: float32 [768], replicated, may hold values from -3 to 3
- norm2_gain: float32 [768], replicated, may hold values from 0.1 to 1.9
- norm2_shift: float32 [768], replicated, may hold values from -3 to 3
- fc_weight: bfloat16 [768, 3072], replicated, may hold values from -0.21875 to 0.21875
- fc_bias: float32 [3072], replicated, may hold values from -3 to 3
- out_weight: bfloat16 [3072, 768], replicated, may hold values from -0.3125 to 0.3125
- out_bias: float32 [768], replicated, may hold values from -3 to 3
- out_cotangent: bfloat16 [64, 2048, 768], P('rows', 'seq'), may hold values from -6 to 6
Outputs:
- layer_output: bfloat16 [64, 2048, 768], P('rows', 'seq')
- input_grad: float32 [64, 2048, 768], P('rows', 'seq')
- grad_norm1_gain: float32 [768], replicated
- grad_norm1_shift: float32 [768], replicated
- grad_qkv_weight: float32 [768, 2304], replicated
- grad_qv_bias: float32 [1536], replicated
- grad_proj_weight: float32 [768, 768], replicated
- grad_proj_bias: float32 [768], replicated
- grad_norm2_gain: float32 [768], replicated
- grad_norm2_shift: float32 [768], replicated
- grad_fc_weight: float32 [768, 3072], replicated
- grad_fc_bias: float32 [3072], replicated
- grad_out_weight: float32 [3072, 768], replicated
- grad_out_bias: float32 [768], replicated
The draws below stay inside these ranges and needn't reach their ends.
Inputs may be any that keep to these rules, and one draw needn't show every extreme that they name: `segment_ids`: along each row the ids never fall; every row holds documents 0, 1 and 2 in that order, then padding marked 3 that ends the row.
All inputs are finite; a program needn't handle non-finite values.
Results may differ from the reference program's by a relative error of at most 0.02.
Values may be sent and summed in bfloat16 or wider, within the bound.
A program may use at most 576 MiB of HBM per device.

```python
import jax
import jax.numpy as jnp
from jax import lax

D = 768
HEADS = 12
HEAD_DIM = 64
FF = 3072
ROW_LEN = 2048
GROUP = 1024
ROWS = 64


def draw_segment_ids(key, part):
    key = jax.random.fold_in(key, 7)
    first_key, second_key, third_key = jax.random.split(key, 3)
    begin_long = 1 + jax.random.randint(first_key, (ROWS, 1), 0, GROUP - 1)
    end_long = ROW_LEN - GROUP + 1 + jax.random.randint(second_key, (ROWS, 1), 0, GROUP - 2)
    raw_draw = jax.random.randint(third_key, (ROWS, 1), 0, 1048576)
    pad_start = end_long + 1 + raw_draw % (ROW_LEN - end_long - 1)
    slot_index = jnp.arange(ROW_LEN)[None, :]
    return (slot_index >= begin_long).astype(jnp.int32) + (slot_index >= end_long).astype(jnp.int32) + (slot_index >= pad_start).astype(jnp.int32)


def with_spikes(array, key, source, target, shards_of, factor):
    def block_of(position):
        return (jnp.arange(array.shape[position]) // (array.shape[position] // shards_of)).reshape((-1,) + (1,) * (array.ndim - 1 - position))

    one_side = jax.random.permutation(key, shards_of)[block_of(target)]
    far = (block_of(target) + shards_of // 2) % shards_of
    return jnp.where((block_of(source) == one_side) | (block_of(source) == far), factor * array, array)


def levels(stream_key, dims, pieces, least, largest):
    level = 1.0
    for position, blocks in pieces:
        heights = jax.random.uniform(jax.random.fold_in(jax.random.fold_in(stream_key, 6), position), (blocks,), jnp.float32, least / len(pieces), largest / len(pieces))
        level = level * jnp.repeat(jnp.exp(heights), dims[position] // blocks).reshape((-1,) + (1,) * (len(dims) - 1 - position))
    return level


def gaussian(rng, dims, scale, bound, cuts=(), held_as=jnp.bfloat16):
    entries = jax.random.normal(rng, dims, jnp.float32) * scale
    if len(cuts) > 0:
        entries = levels(rng, dims, cuts, -0.22, 0.18) * entries
    return jnp.clip(entries, min=-bound, max=bound).astype(held_as)


def noise_with(key, shape, deviation, most, cuts, heavy, kind=jnp.bfloat16):
    drawn = deviation * jax.random.normal(key, shape, jnp.float32)
    if cuts:
        drawn = drawn * levels(key, shape, cuts, -0.22, 0.18)
    return jnp.clip(with_spikes(drawn, jax.random.fold_in(key, 3), *heavy), -most, most).astype(kind)


def setup_inputs(seed: int = 0) -> dict:
    splits = jax.random.split(jax.random.key(seed), 16)
    block_input = gaussian(splits[0], (ROWS, ROW_LEN, D), 1.0, 6.0, ((0, 16), (1, 2)))
    segment_ids = draw_segment_ids(jax.random.fold_in(splits[15], 71), 0)
    norm1_gain = jnp.clip(1.0 + 0.18 * jax.random.normal(splits[2], (D,), jnp.float32), 0.1, 1.9)
    norm1_shift = gaussian(splits[3], (D,), 0.5, 3.0, (), jnp.float32)
    qkv_weight = gaussian(splits[4], (D, 3 * D), D ** -0.5, 0.21875)
    qv_bias = gaussian(splits[5], (2 * D,), 0.5, 3.0, (), jnp.float32)
    proj_weight = gaussian(splits[6], (D, D), 1 ** -0.5, 6.0)
    proj_bias = gaussian(splits[7], (D,), 0.5, 3.0, (), jnp.float32)
    norm2_gain = jnp.clip(1.0 + 0.18 * jax.random.normal(splits[8], (D,), jnp.float32), 0.1, 1.9)
    norm2_shift = gaussian(splits[9], (D,), 0.5, 3.0, (), jnp.float32)
    fc_weight = gaussian(splits[10], (D, FF), D ** -0.5, 0.21875)
    fc_bias = gaussian(splits[11], (FF,), 0.5, 3.0, (), jnp.float32)
    out_weight = gaussian(splits[12], (FF, D), (FF // 8) ** -0.5, 0.3125)
    out_bias = gaussian(splits[13], (D,), 0.5, 3.0, (), jnp.float32)
    out_cotangent = noise_with(splits[14], (ROWS, ROW_LEN, D), 1.0, 6.0, ((0, 16), (1, 2)), (0, 2, 16, 2.0))
    return {"block_input": block_input, "segment_ids": segment_ids, "norm1_gain": norm1_gain, "norm1_shift": norm1_shift, "qkv_weight": qkv_weight, "qv_bias": qv_bias, "proj_weight": proj_weight, "proj_bias": proj_bias, "norm2_gain": norm2_gain, "norm2_shift": norm2_shift, "fc_weight": fc_weight, "fc_bias": fc_bias, "out_weight": out_weight, "out_bias": out_bias, "out_cotangent": out_cotangent}


BRANCH = 12 ** (-0.5)
EPSILON = 1e-05
PADDING = 3
NEGATIVE = -1e+30

@jax.custom_vjp
def low(v):
    return lax.optimization_barrier(v.astype(jnp.bfloat16)).astype(jnp.float32)

@jax.custom_vjp
def low_back(v):
    return v

def low_keep(v):
    return (low(v), None)

def low_pass(kept, grad):
    return (grad,)

def back_keep(v):
    return (v, None)

def back_low(kept, grad):
    return (low(grad),)
low.defvjp(low_keep, low_pass)
low_back.defvjp(back_keep, back_low)

def matmul(left, right):
    return jnp.dot(left, right, precision=lax.Precision.HIGHEST, preferred_element_type=jnp.float32)

def layer_norm(values, scale_gain, shift_bias):
    center = values - lax.optimization_barrier(jnp.mean(values, axis=-1, keepdims=True))
    variance = lax.optimization_barrier(jnp.mean(center * center, axis=-1, keepdims=True))
    return center * lax.rsqrt(variance + EPSILON) * scale_gain + shift_bias

def row_block(params, row_input, row_segments):
    norm1_gain, norm1_shift, qkv_weight, qv_bias, proj_weight, proj_bias, norm2_gain, norm2_shift, fc_weight, fc_bias, out_weight, out_bias = params
    length = row_input.shape[0]
    slot_index = jnp.arange(length)
    allowed = (row_segments[:, None] == row_segments[None, :]) & (slot_index[None, :] <= slot_index[:, None]) & ((row_segments[None, :] != PADDING) | (slot_index[None, :] == slot_index[:, None]))
    normed_one = low(layer_norm(row_input, norm1_gain, norm1_shift))
    mixed_qkv = matmul(normed_one, qkv_weight)
    queries = low_back(low(mixed_qkv[:, :D] + qv_bias[:D])).reshape(length, HEADS, HEAD_DIM)
    key_rows = low_back(low(mixed_qkv[:, D:2 * D])).reshape(length, HEADS, HEAD_DIM)
    value_rows = low_back(low(mixed_qkv[:, 2 * D:] + qv_bias[D:])).reshape(length, HEADS, HEAD_DIM)
    scores = low_back(jnp.einsum('qhd,khd->hqk', queries, key_rows, precision=lax.Precision.HIGHEST)) * HEAD_DIM ** (-0.5)
    scores = jnp.where(allowed[None], scores, NEGATIVE)
    probs_low = low(jax.nn.softmax(scores, axis=-1))
    attended = jnp.einsum('hqk,khd->qhd', probs_low, value_rows, precision=lax.Precision.HIGHEST).reshape(length, D)
    attended_low = low_back(low(attended))
    branch_one = low_back(matmul(attended_low, proj_weight) + proj_bias)
    middle = row_input + BRANCH * branch_one
    normed_two = low(layer_norm(middle, norm2_gain, norm2_shift))
    hidden_pre = low_back(matmul(normed_two, fc_weight) + fc_bias)
    hidden_act = low(jax.nn.gelu(hidden_pre, approximate=True))
    branch_two = low_back(matmul(hidden_act, out_weight) + out_bias)
    return middle + BRANCH * branch_two

def reference(block_input, segment_ids, norm1_gain, norm1_shift, qkv_weight, qv_bias, proj_weight, proj_bias, norm2_gain, norm2_shift, fc_weight, fc_bias, out_weight, out_bias, out_cotangent):
    params = tuple((member.astype(jnp.float32) for member in (norm1_gain, norm1_shift, qkv_weight, qv_bias, proj_weight, proj_bias, norm2_gain, norm2_shift, fc_weight, fc_bias, out_weight, out_bias)))
    inputs = block_input.astype(jnp.float32)

    def forward(row_inputs, weights):

        def row_step(row_pair):
            return row_block(weights, row_pair[0], row_pair[1])
        return lax.map(jax.checkpoint(row_step), (row_inputs, segment_ids))
    output, pullback = jax.vjp(forward, inputs, params)
    input_grad, param_grads = pullback(out_cotangent.astype(jnp.float32))
    return (output.astype(jnp.bfloat16), input_grad, param_grads[0], param_grads[1], param_grads[2], param_grads[3], param_grads[4], param_grads[5], param_grads[6], param_grads[7], param_grads[8], param_grads[9], param_grads[10], param_grads[11])
```

```python
from functools import partial

import jax
import jax.numpy as jnp
from jax import lax
from jax.experimental import pallas as pl
from jax.experimental.pallas import tpu as pltpu
from jax.sharding import PartitionSpec as P

HEADS = 12
HEAD_DIM = 64


BRANCH = 12 ** (-0.5)
EPSILON = 1e-05
PADDING = 3.0
NEGATIVE = -1e30
block_keys = 256


def layer_norm(values, scale_gain, shift_bias):
    center = values - jnp.mean(values, axis=-1, keepdims=True)
    variance = jnp.mean(center * center, axis=-1, keepdims=True)
    return center * lax.rsqrt(variance + EPSILON) * scale_gain + shift_bias


def allowed_pairs(query_segments, key_segments, query_slots, key_slots):
    same_doc = query_segments[:, :, None] == key_segments[:, None, :]
    causal = key_slots[None, None, :] <= query_slots[None, :, None]
    itself = key_slots[None, None, :] == query_slots[None, :, None]
    unpadded = key_segments[:, None, :] != PADDING
    return (same_doc & causal & (unpadded | itself))[:, None]


def split_heads(block_rows):
    return block_rows.reshape(block_rows.shape[0], block_rows.shape[1], HEADS, HEAD_DIM)


def fold_blocks(block_step, running, piece_tuple):
    piece_len = piece_tuple[0].shape[1]

    def one_block(block_index, held_state):
        offset = block_index * block_keys
        sub_tuple = tuple(
            (lax.dynamic_slice_in_dim(member, offset, block_keys, 1) for member in piece_tuple)
        )
        return block_step(held_state, sub_tuple, offset)

    return lax.fori_loop(0, piece_len // block_keys, one_block, running)


def keep_same(running):
    return running


def local(
    block_input,
    segment_ids,
    norm1_gain,
    norm1_shift,
    qkv_weight,
    qv_bias,
    proj_weight,
    proj_bias,
    norm2_gain,
    norm2_shift,
    fc_weight,
    fc_bias,
    out_weight,
    out_bias,
    out_cotangent,
):
    row_count, local_len, model_width = block_input.shape
    tokens = row_count * local_len
    full_len = local_len * lax.axis_size("seq")
    my_first = lax.axis_index("seq") * local_len
    query_slots = my_first + jnp.arange(local_len)
    my_segments = segment_ids.astype(jnp.bfloat16)
    my_seg_float = segment_ids.astype(jnp.float32)
    score_scale = HEAD_DIM ** (-0.5)
    inputs = block_input.astype(jnp.float32).reshape(tokens, model_width)
    normed_one = layer_norm(inputs, norm1_gain, norm1_shift).astype(jnp.bfloat16)
    mixed_qkv = jnp.dot(normed_one, qkv_weight, preferred_element_type=jnp.float32)
    query_flat = (
        (mixed_qkv[:, :model_width] + qv_bias[:model_width])
        .astype(jnp.bfloat16)
        .reshape(row_count, local_len, model_width)
    )
    key_rows = (
        mixed_qkv[:, model_width : 2 * model_width]
        .astype(jnp.bfloat16)
        .reshape(row_count, local_len, model_width)
    )
    value_rows = (
        (mixed_qkv[:, 2 * model_width :] + qv_bias[model_width:])
        .astype(jnp.bfloat16)
        .reshape(row_count, local_len, model_width)
    )
    queries = split_heads(query_flat)

    def attend_block(running, sub_tuple, first_slot):
        key_piece, value_piece, seg_piece = sub_tuple
        piece_len = key_piece.shape[1]
        key_slots = first_slot + jnp.arange(piece_len)
        seg_float = seg_piece.astype(jnp.float32)
        skipped = (first_slot > my_first + local_len - 1) | (
            jnp.max(seg_float) < jnp.min(my_seg_float)
        )

        def attend_update(state):
            running_max, running_sum, running_out = state
            scores = (
                jnp.einsum(
                    "rqhd,rkhd->rhqk",
                    queries,
                    split_heads(key_piece),
                    preferred_element_type=jnp.float32,
                )
                * score_scale
            )
            allowed = allowed_pairs(my_seg_float, seg_float, query_slots, key_slots)
            masked = jnp.where(allowed, scores, NEGATIVE)
            new_max = jnp.maximum(running_max, jnp.max(masked, axis=-1))
            prob_block = jnp.where(allowed, jnp.exp(scores - new_max[..., None]), 0.0)
            factor = jnp.exp(running_max - new_max)
            new_sum = running_sum * factor + jnp.sum(prob_block, axis=-1)
            added_part = jnp.einsum(
                "rhqk,rkhd->rqhd",
                prob_block.astype(jnp.bfloat16),
                split_heads(value_piece),
                preferred_element_type=jnp.float32,
            )
            new_out = running_out * jnp.transpose(factor, (0, 2, 1))[..., None] + added_part
            return (new_max, new_sum, new_out)

        return lax.cond(skipped, keep_same, attend_update, running)

    start_state = (
        jnp.full((row_count, HEADS, local_len), NEGATIVE, jnp.float32),
        jnp.zeros((row_count, HEADS, local_len), jnp.float32),
        jnp.zeros((row_count, local_len, HEADS, HEAD_DIM), jnp.float32),
    )
    running_max, running_sum, running_out = fold_blocks(
        attend_block,
        start_state,
        (
            lax.all_gather(key_rows, "seq", axis=1, tiled=True),
            lax.all_gather(value_rows, "seq", axis=1, tiled=True),
            lax.all_gather(my_segments, "seq", axis=1, tiled=True),
        ),
    )
    log_total = running_max + jnp.log(running_sum)
    attended_heads = running_out / jnp.transpose(running_sum, (0, 2, 1))[..., None]
    attended_low = attended_heads.reshape(tokens, model_width).astype(jnp.bfloat16)
    branch_one = jnp.dot(attended_low, proj_weight, preferred_element_type=jnp.float32) + proj_bias
    middle = inputs + BRANCH * branch_one
    normed_two = layer_norm(middle, norm2_gain, norm2_shift).astype(jnp.bfloat16)
    hidden_pre = jnp.dot(normed_two, fc_weight, preferred_element_type=jnp.float32) + fc_bias
    hidden_act = jax.nn.gelu(hidden_pre, approximate=True).astype(jnp.bfloat16)
    branch_two = jnp.dot(hidden_act, out_weight, preferred_element_type=jnp.float32) + out_bias
    layer_output = (
        (middle + BRANCH * branch_two)
        .astype(jnp.bfloat16)
        .reshape(row_count, local_len, model_width)
    )
    flat_cot = out_cotangent.reshape(tokens, model_width).astype(jnp.float32)
    grad_two = (BRANCH * flat_cot).astype(jnp.bfloat16)
    grad_out_weight = jnp.einsum(
        "tf,td->fd", hidden_act, grad_two, preferred_element_type=jnp.float32
    )
    grad_out_bias = jnp.sum(grad_two.astype(jnp.float32), axis=0)
    grad_act = jnp.einsum("td,fd->tf", grad_two, out_weight, preferred_element_type=jnp.float32)
    gelu_value, gelu_pull = jax.vjp(partial(jax.nn.gelu, approximate=True), hidden_pre)
    grad_pre = gelu_pull(grad_act)[0].astype(jnp.bfloat16)
    grad_fc_weight = jnp.einsum(
        "td,tf->df", normed_two, grad_pre, preferred_element_type=jnp.float32
    )
    grad_fc_bias = jnp.sum(grad_pre.astype(jnp.float32), axis=0)
    grad_normed_two = jnp.einsum(
        "tf,df->td", grad_pre, fc_weight, preferred_element_type=jnp.float32
    )
    norm_value, norm_pull = jax.vjp(layer_norm, middle, norm2_gain, norm2_shift)
    grad_inner, grad_norm2_gain, grad_norm2_shift = norm_pull(grad_normed_two)
    grad_middle = flat_cot + grad_inner
    grad_one = (BRANCH * grad_middle).astype(jnp.bfloat16)
    grad_proj_weight = jnp.einsum(
        "td,te->de", attended_low, grad_one, preferred_element_type=jnp.float32
    )
    grad_proj_bias = jnp.sum(grad_one.astype(jnp.float32), axis=0)
    grad_attended_flat = (
        jnp.einsum("te,de->td", grad_one, proj_weight, preferred_element_type=jnp.float32)
        .astype(jnp.bfloat16)
        .reshape(row_count, local_len, model_width)
    )
    grad_attended = split_heads(grad_attended_flat)
    grad_delta = jnp.einsum("rqhd,rqhd->rhq", grad_attended.astype(jnp.float32), attended_heads)

    def back_block(running, sub_tuple, first_slot):
        key_piece, value_piece, seg_piece = sub_tuple
        piece_len = key_piece.shape[1]
        key_slots = first_slot + jnp.arange(piece_len)
        seg_float = seg_piece.astype(jnp.float32)
        skipped = (first_slot > my_first + local_len - 1) | (
            jnp.max(seg_float) < jnp.min(my_seg_float)
        )

        def back_update(state):
            grad_query, grad_full = state
            key_heads = split_heads(key_piece)
            value_heads = split_heads(value_piece)
            scores = (
                jnp.einsum(
                    "rqhd,rkhd->rhqk", queries, key_heads, preferred_element_type=jnp.float32
                )
                * score_scale
            )
            allowed = allowed_pairs(my_seg_float, seg_float, query_slots, key_slots)
            prob_block = jnp.where(allowed, jnp.exp(scores - log_total[..., None]), 0.0)
            grad_probs = jnp.einsum(
                "rqhd,rkhd->rhqk", grad_attended, value_heads, preferred_element_type=jnp.float32
            )
            grad_scores = (score_scale * prob_block * (grad_probs - grad_delta[..., None])).astype(
                jnp.bfloat16
            )
            new_query = grad_query + jnp.einsum(
                "rhqk,rkhd->rqhd", grad_scores, key_heads, preferred_element_type=jnp.float32
            )
            grad_keys = jnp.einsum(
                "rhqk,rqhd->rkhd", grad_scores, queries, preferred_element_type=jnp.float32
            ).reshape(row_count, piece_len, model_width)
            grad_values = jnp.einsum(
                "rhqk,rqhd->rkhd",
                prob_block.astype(jnp.bfloat16),
                grad_attended,
                preferred_element_type=jnp.float32,
            ).reshape(row_count, piece_len, model_width)
            held_part = lax.dynamic_slice_in_dim(grad_full, first_slot, piece_len, 2)
            new_full = lax.dynamic_update_slice_in_dim(
                grad_full, held_part + jnp.stack((grad_keys, grad_values)), first_slot, 2
            )
            return (new_query, new_full)

        return lax.cond(skipped, keep_same, back_update, running)

    back_start = (
        jnp.zeros((row_count, local_len, HEADS, HEAD_DIM), jnp.float32),
        jnp.zeros((2, row_count, full_len, model_width), jnp.float32),
    )
    grad_query, grad_full = fold_blocks(
        back_block,
        back_start,
        (
            lax.all_gather(key_rows, "seq", axis=1, tiled=True),
            lax.all_gather(value_rows, "seq", axis=1, tiled=True),
            lax.all_gather(my_segments, "seq", axis=1, tiled=True),
        ),
    )
    grad_pairs = lax.psum_scatter(
        grad_full.astype(jnp.bfloat16), "seq", scatter_dimension=2, tiled=True
    ).astype(jnp.float32)
    grad_query_low = grad_query.reshape(row_count, local_len, model_width).astype(jnp.bfloat16)
    grad_key_low = grad_pairs[0].astype(jnp.bfloat16)
    grad_value_low = grad_pairs[1].astype(jnp.bfloat16)
    grad_qkv_low = jnp.concatenate((grad_query_low, grad_key_low, grad_value_low), axis=-1).reshape(
        tokens, 3 * model_width
    )
    grad_qkv_weight = jnp.einsum(
        "td,te->de", normed_one, grad_qkv_low, preferred_element_type=jnp.float32
    )
    grad_qv_bias = jnp.concatenate(
        (
            jnp.sum(grad_query_low.astype(jnp.float32), axis=(0, 1)),
            jnp.sum(grad_value_low.astype(jnp.float32), axis=(0, 1)),
        )
    )
    grad_normed_one = jnp.einsum(
        "te,de->td", grad_qkv_low, qkv_weight, preferred_element_type=jnp.float32
    )
    first_value, first_pull = jax.vjp(layer_norm, inputs, norm1_gain, norm1_shift)
    grad_first, grad_norm1_gain, grad_norm1_shift = first_pull(grad_normed_one)
    input_grad = (grad_middle + grad_first).reshape(row_count, local_len, model_width)
    local_grads = (
        grad_norm1_gain,
        grad_norm1_shift,
        grad_qkv_weight,
        grad_qv_bias,
        grad_proj_weight,
        grad_proj_bias,
        grad_norm2_gain,
        grad_norm2_shift,
        grad_fc_weight,
        grad_fc_bias,
        grad_out_weight,
        grad_out_bias,
    )
    shares = (
        lax.psum_scatter(
            local_grads[0].astype(jnp.bfloat16), "rows", scatter_dimension=0, tiled=True
        ).astype(jnp.float32),
        lax.psum_scatter(
            local_grads[1].astype(jnp.bfloat16), "rows", scatter_dimension=0, tiled=True
        ).astype(jnp.float32),
        lax.psum_scatter(
            local_grads[2].astype(jnp.bfloat16), "rows", scatter_dimension=0, tiled=True
        ).astype(jnp.float32),
        lax.psum_scatter(
            local_grads[3].astype(jnp.bfloat16), "rows", scatter_dimension=0, tiled=True
        ).astype(jnp.float32),
        lax.psum_scatter(
            local_grads[4].astype(jnp.bfloat16), "rows", scatter_dimension=0, tiled=True
        ).astype(jnp.float32),
        lax.psum_scatter(
            local_grads[5].astype(jnp.bfloat16), "rows", scatter_dimension=0, tiled=True
        ).astype(jnp.float32),
        lax.psum_scatter(
            local_grads[6].astype(jnp.bfloat16), "rows", scatter_dimension=0, tiled=True
        ).astype(jnp.float32),
        lax.psum_scatter(
            local_grads[7].astype(jnp.bfloat16), "rows", scatter_dimension=0, tiled=True
        ).astype(jnp.float32),
        lax.psum_scatter(
            local_grads[8].astype(jnp.bfloat16), "rows", scatter_dimension=0, tiled=True
        ).astype(jnp.float32),
        lax.psum_scatter(
            local_grads[9].astype(jnp.bfloat16), "rows", scatter_dimension=0, tiled=True
        ).astype(jnp.float32),
        lax.psum_scatter(
            local_grads[10].astype(jnp.bfloat16), "rows", scatter_dimension=0, tiled=True
        ).astype(jnp.float32),
        lax.psum_scatter(
            local_grads[11].astype(jnp.bfloat16), "rows", scatter_dimension=0, tiled=True
        ).astype(jnp.float32),
    )
    shares = (
        lax.psum(shares[0].astype(jnp.bfloat16), "seq").astype(jnp.float32),
        lax.psum(shares[1].astype(jnp.bfloat16), "seq").astype(jnp.float32),
        lax.psum(shares[2].astype(jnp.bfloat16), "seq").astype(jnp.float32),
        lax.psum(shares[3].astype(jnp.bfloat16), "seq").astype(jnp.float32),
        lax.psum(shares[4].astype(jnp.bfloat16), "seq").astype(jnp.float32),
        lax.psum(shares[5].astype(jnp.bfloat16), "seq").astype(jnp.float32),
        lax.psum(shares[6].astype(jnp.bfloat16), "seq").astype(jnp.float32),
        lax.psum(shares[7].astype(jnp.bfloat16), "seq").astype(jnp.float32),
        lax.psum(shares[8].astype(jnp.bfloat16), "seq").astype(jnp.float32),
        lax.psum(shares[9].astype(jnp.bfloat16), "seq").astype(jnp.float32),
        lax.psum(shares[10].astype(jnp.bfloat16), "seq").astype(jnp.float32),
        lax.psum(shares[11].astype(jnp.bfloat16), "seq").astype(jnp.float32),
    )
    totals = (
        lax.all_gather(shares[0].astype(jnp.bfloat16), "rows", axis=0, tiled=True).astype(
            jnp.float32
        ),
        lax.all_gather(shares[1].astype(jnp.bfloat16), "rows", axis=0, tiled=True).astype(
            jnp.float32
        ),
        lax.all_gather(shares[2].astype(jnp.bfloat16), "rows", axis=0, tiled=True).astype(
            jnp.float32
        ),
        lax.all_gather(shares[3].astype(jnp.bfloat16), "rows", axis=0, tiled=True).astype(
            jnp.float32
        ),
        lax.all_gather(shares[4].astype(jnp.bfloat16), "rows", axis=0, tiled=True).astype(
            jnp.float32
        ),
        lax.all_gather(shares[5].astype(jnp.bfloat16), "rows", axis=0, tiled=True).astype(
            jnp.float32
        ),
        lax.all_gather(shares[6].astype(jnp.bfloat16), "rows", axis=0, tiled=True).astype(
            jnp.float32
        ),
        lax.all_gather(shares[7].astype(jnp.bfloat16), "rows", axis=0, tiled=True).astype(
            jnp.float32
        ),
        lax.all_gather(shares[8].astype(jnp.bfloat16), "rows", axis=0, tiled=True).astype(
            jnp.float32
        ),
        lax.all_gather(shares[9].astype(jnp.bfloat16), "rows", axis=0, tiled=True).astype(
            jnp.float32
        ),
        lax.all_gather(shares[10].astype(jnp.bfloat16), "rows", axis=0, tiled=True).astype(
            jnp.float32
        ),
        lax.all_gather(shares[11].astype(jnp.bfloat16), "rows", axis=0, tiled=True).astype(
            jnp.float32
        ),
    )
    return (layer_output, input_grad) + tuple(totals)


MIB = 1 << 20
LOG2E = 1.4426950408889634
GELU_C = 0.7978845608028654
GELU_A = 0.044715
BLOCK = 256
f32 = jnp.float32
bf16 = jnp.bfloat16


def dot_nn(a, b):
    return lax.dot_general(a, b, (((1,), (0,)), ((), ())), preferred_element_type=f32)


def dot_nt(a, b):
    return lax.dot_general(a, b, (((1,), (1,)), ((), ())), preferred_element_type=f32)


def norm_parts(values):
    center = values - jnp.mean(values, axis=-1, keepdims=True)
    variance = jnp.mean(center * center, axis=-1, keepdims=True)
    inverse = lax.rsqrt(variance + EPSILON)
    return center * inverse, inverse


def row_sums(values):
    rows, cols = values.shape
    return jnp.sum(values.reshape(rows // 8, 8, cols), axis=0)


def whole(shape):
    return pl.BlockSpec(shape, lambda *_: (0,) * len(shape), pipeline_mode=pl.Buffered(1))


def call(kernel, name, grid, in_specs, out_specs, out_shape, scratch, flops, moved, vmem, prefetch=0):
    return pl.pallas_call(
        kernel,
        out_shape=out_shape,
        grid_spec=pltpu.PrefetchScalarGridSpec(
            num_scalar_prefetch=prefetch,
            grid=grid,
            in_specs=in_specs,
            out_specs=out_specs,
            scratch_shapes=scratch,
        ),
        compiler_params=pltpu.CompilerParams(vmem_limit_bytes=vmem * MIB),
        cost_estimate=pl.CostEstimate(flops=flops, bytes_accessed=moved, transcendentals=0),
        name=name,
    )


def qkv_kernel(x_ref, gain_ref, shift_ref, w_ref, bias_ref, q_ref, k_ref, v_ref, kt_ref, vt_ref):
    width = x_ref.shape[1]
    hat, _ = norm_parts(x_ref[...].astype(f32))
    normed = (hat * gain_ref[...] + shift_ref[...]).astype(bf16)
    q_ref[...] = (dot_nn(normed, w_ref[:, :width]) + bias_ref[:, :width]).astype(bf16)
    keys = dot_nn(normed, w_ref[:, width : 2 * width])
    k_ref[...] = keys.astype(bf16)
    kt_ref[...] = jnp.transpose(keys).astype(bf16)
    values = dot_nn(normed, w_ref[:, 2 * width :]) + bias_ref[:, width:]
    v_ref[...] = values.astype(bf16)
    vt_ref[...] = jnp.transpose(values).astype(bf16)


def project_qkv(x, gain, shift, weight, bias):
    tokens, width = x.shape
    tile = 512
    flat = pl.BlockSpec((tile, width), lambda t: (t, 0))
    turned = pl.BlockSpec((width, tile), lambda t: (0, t))
    return call(
        qkv_kernel,
        "qkv_forward",
        (tokens // tile,),
        [flat, whole((1, width)), whole((1, width)), whole(weight.shape), whole((1, 2 * width))],
        [flat, flat, flat, turned, turned],
        [jax.ShapeDtypeStruct((tokens, width), bf16)] * 3
        + [jax.ShapeDtypeStruct((width, tokens), bf16)] * 2,
        [],
        2 * tokens * width * 3 * width,
        tokens * width * 12 + weight.size * 2,
        60,
    )(x, gain[None], shift[None], weight, bias[None])


def attend_kernel(low_ref, start_ref, q_ref, k_ref, vt_ref, att_ref, lse_ref):
    row = pl.program_id(0)
    length = q_ref.shape[0]
    blocks = length // BLOCK
    scale = HEAD_DIM**-0.5 * LOG2E
    lanes = lax.broadcasted_iota(jnp.int32, (BLOCK, 2 * HEAD_DIM), 1)
    slots = lax.broadcasted_iota(jnp.int32, (BLOCK, BLOCK), 0)
    query_iota = lax.broadcasted_iota(jnp.int32, (BLOCK, BLOCK), 1)

    def query_block(qb, _):
        q_at = pl.ds(pl.multiple_of(qb * BLOCK, BLOCK), BLOCK)
        queries = q_ref[q_at, :]
        heads = [
            jnp.where(lanes < HEAD_DIM, queries, jnp.zeros_like(queries)),
            jnp.where(lanes >= HEAD_DIM, queries, jnp.zeros_like(queries)),
        ]
        start = start_ref[0, :, q_at]

        def scored(kb, extra):
            k_at = pl.ds(pl.multiple_of(kb * BLOCK, BLOCK), BLOCK)
            keys = k_ref[k_at, :]
            allowed = slots >= start - kb * BLOCK
            if extra is not None:
                allowed = allowed & extra
            return k_at, [
                jnp.where(allowed, dot_nt(keys, heads[h]) * scale, NEGATIVE) for h in range(2)
            ]

        k_at, scores = scored(qb, slots <= query_iota)
        state = []
        for h in range(2):
            top = jnp.max(scores[h], axis=0, keepdims=True)
            probs = jnp.exp2(scores[h] - top)
            total = jnp.sum(probs, axis=0, keepdims=True)
            out = dot_nn(vt_ref[pl.ds(h * HEAD_DIM, HEAD_DIM), k_at], probs.astype(bf16))
            state += [top, total, out]

        def key_block(kb, state):
            k_at, scores = scored(kb, None)
            fresh = []
            for h in range(2):
                top, total, out = state[3 * h : 3 * h + 3]
                new_top = jnp.maximum(top, jnp.max(scores[h], axis=0, keepdims=True))
                probs = jnp.exp2(scores[h] - new_top)
                factor = jnp.exp2(top - new_top)
                total = total * factor + jnp.sum(probs, axis=0, keepdims=True)
                out = out * factor + dot_nn(
                    vt_ref[pl.ds(h * HEAD_DIM, HEAD_DIM), k_at], probs.astype(bf16)
                )
                fresh += [new_top, total, out]
            return tuple(fresh)

        state = lax.fori_loop(low_ref[row * blocks + qb], qb, key_block, tuple(state))
        outs = []
        for h in range(2):
            top, total, out = state[3 * h : 3 * h + 3]
            outs.append(out / total)
            lse_ref[0, h : h + 1, q_at] = top + jnp.log2(total)
        att_ref[q_at, :] = jnp.transpose(jnp.concatenate(outs, axis=0)).astype(bf16)
        return 0

    lax.fori_loop(0, blocks, query_block, 0)


def attend(low, start, q, k, vt, rows):
    tokens, width = q.shape
    length = tokens // rows
    pairs = width // (2 * HEAD_DIM)
    flat = pl.BlockSpec((length, 2 * HEAD_DIM), lambda r, p, *_: (r, p))
    turned = pl.BlockSpec((2 * HEAD_DIM, length), lambda r, p, *_: (p, r))
    return call(
        attend_kernel,
        "attention_forward",
        (rows, pairs),
        [pl.BlockSpec((1, 1, length), lambda r, p, *_: (r, 0, 0)), flat, flat, turned],
        [flat, pl.BlockSpec((1, 2, length), lambda r, p, *_: (p, 0, r))],
        [
            jax.ShapeDtypeStruct((tokens, width), bf16),
            jax.ShapeDtypeStruct((pairs, 2, tokens), f32),
        ],
        [],
        2 * tokens * length * width,
        tokens * width * 8,
        60,
        prefetch=1,
    )(low, start, q, k, vt)


def attend_back_kernel(
    high_ref, start_ref, q_ref, k_ref, kt_ref, v_ref, do_ref, lse_ref, delta_ref,
    dq_ref, dk_ref, dv_ref, q0, q1, do0, do1, dqt,
):
    row = pl.program_id(0)
    length = q_ref.shape[0]
    blocks = length // BLOCK
    scale = HEAD_DIM**-0.5 * LOG2E
    lanes = lax.broadcasted_iota(jnp.int32, (length, 2 * HEAD_DIM), 1)
    zero = jnp.zeros((length, 2 * HEAD_DIM), bf16)
    queries = q_ref[...]
    q0[...] = jnp.where(lanes < HEAD_DIM, queries, zero)
    q1[...] = jnp.where(lanes >= HEAD_DIM, queries, zero)
    grads = do_ref[...]
    do0[...] = jnp.where(lanes < HEAD_DIM, grads, zero)
    do1[...] = jnp.where(lanes >= HEAD_DIM, grads, zero)
    dqt[...] = jnp.zeros_like(dqt)
    slots = lax.broadcasted_iota(jnp.int32, (BLOCK, BLOCK), 0)
    query_iota = lax.broadcasted_iota(jnp.int32, (BLOCK, BLOCK), 1)

    def key_block(kb, _):
        k_at = pl.ds(pl.multiple_of(kb * BLOCK, BLOCK), BLOCK)
        keys = k_ref[k_at, :]
        values = v_ref[k_at, :]

        def visit(qb, extra):
            q_at = pl.ds(pl.multiple_of(qb * BLOCK, BLOCK), BLOCK)
            allowed = slots >= start_ref[0, :, q_at] - kb * BLOCK
            if extra is not None:
                allowed = allowed & extra
            dk = dv = None
            for h, (qh, doh) in enumerate(((q0, do0), (q1, do1))):
                q_head = qh[q_at, :]
                do_head = doh[q_at, :]
                scores = dot_nt(keys, q_head) * scale
                probs = jnp.where(allowed, jnp.exp2(scores - lse_ref[0, h : h + 1, q_at]), 0.0)
                grad_probs = dot_nt(values, do_head)
                grad_scores = (probs * (grad_probs - delta_ref[0, h : h + 1, q_at])).astype(bf16)
                dv_part = dot_nn(probs.astype(bf16), do_head)
                dk_part = dot_nn(grad_scores, q_head)
                dk = dk_part if dk is None else dk + dk_part
                dv = dv_part if dv is None else dv + dv_part
                at = pl.ds(h * HEAD_DIM, HEAD_DIM)
                dqt[at, q_at] += dot_nn(kt_ref[at, k_at], grad_scores)
            return dk, dv

        def query_block(qb, state):
            dk, dv = visit(qb, None)
            return state[0] + dk, state[1] + dv

        dk, dv = lax.fori_loop(
            kb + 1, high_ref[row * blocks + kb] + 1, query_block, visit(kb, slots <= query_iota)
        )
        dk_ref[k_at, :] = (dk * HEAD_DIM**-0.5).astype(bf16)
        dv_ref[k_at, :] = dv.astype(bf16)
        return 0

    lax.fori_loop(0, blocks, key_block, 0)

    def turn(qb, _):
        q_at = pl.ds(pl.multiple_of(qb * BLOCK, BLOCK), BLOCK)
        dq_ref[q_at, :] = (jnp.transpose(dqt[:, q_at]) * HEAD_DIM**-0.5).astype(bf16)
        return 0

    lax.fori_loop(0, blocks, turn, 0)


def attend_back(high, start, q, k, kt, v, do, lse, delta, rows):
    tokens, width = q.shape
    length = tokens // rows
    pairs = width // (2 * HEAD_DIM)
    flat = pl.BlockSpec((length, 2 * HEAD_DIM), lambda r, p, *_: (r, p))
    turned = pl.BlockSpec((2 * HEAD_DIM, length), lambda r, p, *_: (p, r))
    lined = pl.BlockSpec((1, 2, length), lambda r, p, *_: (p, 0, r))
    return call(
        attend_back_kernel,
        "attention_backward",
        (rows, pairs),
        [pl.BlockSpec((1, 1, length), lambda r, p, *_: (r, 0, 0)), flat, flat, turned, flat, flat, lined, lined],
        [flat, flat, flat],
        [jax.ShapeDtypeStruct((tokens, width), bf16)] * 3,
        [pltpu.VMEM((length, 2 * HEAD_DIM), bf16)] * 4 + [pltpu.VMEM((2 * HEAD_DIM, length), f32)],
        5 * tokens * length * width,
        tokens * width * 16,
        60,
        prefetch=1,
    )(high, start, q, k, kt, v, do, lse, delta)


def mlp_kernel(
    x_ref, att_ref, cot_ref, proj_ref, projb_ref, gain_ref, shift_ref, fc_ref, fcb_ref, out_ref, outb_ref,
    pick_ref,
    y_ref, gm_ref, do_ref, delta_ref, dfc_ref, doutt_ref, dproj_ref, small_ref, dfcb_ref,
    dfc, doutt, dproj, sums, dfcb, stage, sem,
):
    step = pl.program_id(0)
    steps = pl.num_programs(0)
    tile, width = x_ref.shape
    hidden = fc_ref.shape[1]
    chunk = 768

    @pl.when(step == 0)
    def _():
        dfc[...] = jnp.zeros_like(dfc)
        doutt[...] = jnp.zeros_like(doutt)
        dproj[...] = jnp.zeros_like(dproj)
        sums[...] = jnp.zeros_like(sums)
        dfcb[...] = jnp.zeros_like(dfcb)

    att = att_ref[...]
    middle = x_ref[...].astype(f32) + BRANCH * (dot_nn(att, proj_ref[...]) + projb_ref[...])
    hat, inverse = norm_parts(middle)
    normed_f = hat * gain_ref[...] + shift_ref[...]
    normed = normed_f.astype(bf16)
    normed_t = jnp.transpose(normed_f).astype(bf16)
    cot = cot_ref[...].astype(f32)
    grad_two = (BRANCH * cot).astype(bf16)
    grad_two_f = grad_two.astype(f32)
    grad_two_t = jnp.transpose(grad_two_f).astype(bf16)
    branch = jnp.zeros((tile, width), f32)
    grad_normed = jnp.zeros((tile, width), f32)
    for at in range(0, hidden, chunk):
        cols = pl.ds(at, chunk)
        pre = dot_nn(normed, fc_ref[:, cols]) + fcb_ref[:, cols]
        square = pre * pre
        half = 0.5 + 0.5 * jnp.tanh(pre * (GELU_C + GELU_C * GELU_A * square))
        act = pre * half
        slope = half + act * (1.0 - half) * (2.0 * GELU_C + 6.0 * GELU_C * GELU_A * square)
        act = act.astype(bf16)
        grad_pre_f = dot_nt(grad_two, out_ref[cols, :]) * slope
        grad_pre = grad_pre_f.astype(bf16)
        branch += dot_nn(act, out_ref[cols, :])
        grad_normed += dot_nt(grad_pre, fc_ref[:, cols])
        dfc[:, cols] += dot_nn(normed_t, grad_pre)
        doutt[:, cols] += dot_nn(grad_two_t, act)
        dfcb[:, cols] += row_sums(grad_pre.astype(f32))
    y_ref[...] = (middle + BRANCH * (branch + outb_ref[...])).astype(bf16)
    scaled = grad_normed * gain_ref[...]
    mean_one = jnp.mean(scaled, axis=-1, keepdims=True)
    mean_two = jnp.mean(scaled * hat, axis=-1, keepdims=True)
    grad_middle = cot + inverse * (scaled - mean_one - hat * mean_two)
    gm_ref[...] = grad_middle
    grad_one_f = BRANCH * grad_middle
    grad_one = grad_one_f.astype(bf16)
    grad_att = dot_nt(grad_one, proj_ref[...]).astype(bf16)
    do_ref[...] = grad_att
    dproj[...] += dot_nn(jnp.transpose(att.astype(f32)).astype(bf16), grad_one)
    product = grad_att.astype(f32) * att.astype(f32)
    upper = product.astype(bf16)
    lower = (product - upper.astype(f32)).astype(bf16)
    delta = dot_nt(pick_ref[...], upper) + dot_nt(pick_ref[...], lower)
    for pair in range(delta_ref.shape[0]):
        delta_ref[pair] = delta[2 * pair : 2 * pair + 2, :]
    sums[0:8, :] += row_sums(grad_normed * hat)
    sums[8:16, :] += row_sums(grad_normed)
    sums[16:24, :] += row_sums(grad_two_f)
    sums[24:32, :] += row_sums(grad_one.astype(f32))

    @pl.when(step == steps - 1)
    def _():
        for source, target in ((dfc, dfc_ref), (doutt, doutt_ref)):
            stage[...] = source[...].astype(bf16)
            copy = pltpu.make_async_copy(stage, target, sem)
            copy.start()
            copy.wait()
        dproj_ref[...] = dproj[...].astype(bf16)
        small_ref[...] = sums[...]
        dfcb_ref[...] = dfcb[...]


def feed_forward(x, att, cot, proj_weight, proj_bias, gain, shift, fc_weight, fc_bias, out_weight, out_bias):
    tokens, width = x.shape
    hidden = fc_weight.shape[1]
    heads = width // HEAD_DIM
    tile = 256
    pick = (jnp.arange(16)[:, None] == jnp.arange(width)[None, :] // HEAD_DIM).astype(bf16)
    flat = pl.BlockSpec((tile, width), lambda t: (t, 0))
    return call(
        mlp_kernel,
        "feed_forward",
        (tokens // tile,),
        [flat, flat, flat, whole((width, width)), whole((1, width)), whole((1, width)), whole((1, width)),
         whole(fc_weight.shape), whole((1, hidden)), whole(out_weight.shape), whole((1, width)), whole((16, width))],
        [flat, flat, flat, pl.BlockSpec((heads // 2, 2, tile), lambda t: (0, 0, t)),
         pl.BlockSpec(memory_space=pl.ANY), pl.BlockSpec(memory_space=pl.ANY),
         whole((width, width)), whole((32, width)), whole((8, hidden))],
        [
            jax.ShapeDtypeStruct((tokens, width), bf16),
            jax.ShapeDtypeStruct((tokens, width), f32),
            jax.ShapeDtypeStruct((tokens, width), bf16),
            jax.ShapeDtypeStruct((heads // 2, 2, tokens), f32),
            jax.ShapeDtypeStruct((width, hidden), bf16),
            jax.ShapeDtypeStruct((width, hidden), bf16),
            jax.ShapeDtypeStruct((width, width), bf16),
            jax.ShapeDtypeStruct((32, width), f32),
            jax.ShapeDtypeStruct((8, hidden), f32),
        ],
        [
            pltpu.VMEM((width, hidden), f32),
            pltpu.VMEM((width, hidden), f32),
            pltpu.VMEM((width, width), f32),
            pltpu.VMEM((32, width), f32),
            pltpu.VMEM((8, hidden), f32),
            pltpu.VMEM((width, hidden), bf16),
            pltpu.SemaphoreType.DMA,
        ],
        2 * tokens * width * (3 * width + 6 * hidden),
        tokens * width * 14,
        62,
    )(x, att, cot, proj_weight, proj_bias[None], gain[None], shift[None], fc_weight, fc_bias[None],
      out_weight, out_bias[None], pick)


def qkv_weight_kernel(x_ref, gain_ref, shift_ref, dq_ref, dk_ref, dv_ref, dw_ref, small_ref, acc, sums):
    step = pl.program_id(0)
    width = x_ref.shape[1]

    @pl.when(step == 0)
    def _():
        acc[...] = jnp.zeros_like(acc)
        sums[...] = jnp.zeros_like(sums)

    hat, _ = norm_parts(x_ref[...].astype(f32))
    normed_t = jnp.transpose(hat * gain_ref[...] + shift_ref[...]).astype(bf16)
    for i, ref in enumerate((dq_ref, dk_ref, dv_ref)):
        acc[:, i * width : (i + 1) * width] += dot_nn(normed_t, ref[...])
    sums[0:8, :] += row_sums(dq_ref[...].astype(f32))
    sums[8:16, :] += row_sums(dv_ref[...].astype(f32))

    @pl.when(step == pl.num_programs(0) - 1)
    def _():
        dw_ref[...] = acc[...].astype(bf16)
        small_ref[...] = sums[...]


def qkv_weight_back(x, gain, shift, dq, dk, dv):
    tokens, width = x.shape
    tile = 512
    flat = pl.BlockSpec((tile, width), lambda t: (t, 0))
    return call(
        qkv_weight_kernel,
        "qkv_weight_gradient",
        (tokens // tile,),
        [flat, whole((1, width)), whole((1, width)), flat, flat, flat],
        [whole((width, 3 * width)), whole((16, width))],
        [jax.ShapeDtypeStruct((width, 3 * width), bf16), jax.ShapeDtypeStruct((16, width), f32)],
        [pltpu.VMEM((width, 3 * width), f32), pltpu.VMEM((16, width), f32)],
        2 * tokens * width * 3 * width,
        tokens * width * 8,
        60,
    )(x, gain[None], shift[None], dq, dk, dv)


def qkv_input_kernel(x_ref, gain_ref, w_ref, dq_ref, dk_ref, dv_ref, gm_ref, dx_ref, small_ref, sums):
    step = pl.program_id(0)
    width = x_ref.shape[1]

    @pl.when(step == 0)
    def _():
        sums[...] = jnp.zeros_like(sums)

    hat, inverse = norm_parts(x_ref[...].astype(f32))
    grad_normed = (
        dot_nt(dq_ref[...], w_ref[:, :width])
        + dot_nt(dk_ref[...], w_ref[:, width : 2 * width])
        + dot_nt(dv_ref[...], w_ref[:, 2 * width :])
    )
    scaled = grad_normed * gain_ref[...]
    mean_one = jnp.mean(scaled, axis=-1, keepdims=True)
    mean_two = jnp.mean(scaled * hat, axis=-1, keepdims=True)
    dx_ref[...] = gm_ref[...] + inverse * (scaled - mean_one - hat * mean_two)
    sums[0:8, :] += row_sums(grad_normed * hat)
    sums[8:16, :] += row_sums(grad_normed)

    @pl.when(step == pl.num_programs(0) - 1)
    def _():
        small_ref[...] = sums[...]


def qkv_input_back(x, gain, weight, dq, dk, dv, grad_middle):
    tokens, width = x.shape
    tile = 512
    flat = pl.BlockSpec((tile, width), lambda t: (t, 0))
    return call(
        qkv_input_kernel,
        "qkv_input_gradient",
        (tokens // tile,),
        [flat, whole((1, width)), whole(weight.shape), flat, flat, flat, flat],
        [flat, whole((16, width))],
        [jax.ShapeDtypeStruct((tokens, width), f32), jax.ShapeDtypeStruct((16, width), f32)],
        [pltpu.VMEM((16, width), f32)],
        2 * tokens * width * 3 * width,
        tokens * width * 16,
        60,
    )(x, gain[None], weight, dq, dk, dv, grad_middle)


def to_rows(mine):
    me = lax.axis_index("seq")
    half = mine.shape[0] // 2
    kept = lax.dynamic_slice_in_dim(mine, me * half, half, 0)
    sent = lax.dynamic_slice_in_dim(mine, (1 - me) * half, half, 0)
    got = lax.ppermute(sent, "seq", [(0, 1), (1, 0)])
    first = jnp.where(me == 0, kept, got)
    second = jnp.where(me == 0, got, kept)
    return jnp.concatenate((first, second), axis=1)


def from_rows(rows, dtype):
    me = lax.axis_index("seq")
    length = rows.shape[1] // 2
    kept = lax.dynamic_slice_in_dim(rows, me * length, length, 1)
    sent = lax.dynamic_slice_in_dim(rows, (1 - me) * length, length, 1).astype(bf16)
    got = lax.ppermute(sent, "seq", [(0, 1), (1, 0)]).astype(dtype)
    return jnp.concatenate((jnp.where(me == 0, kept, got), jnp.where(me == 0, got, kept)), axis=0)


def row_local(
    block_input, segment_ids, norm1_gain, norm1_shift, qkv_weight, qv_bias, proj_weight, proj_bias,
    norm2_gain, norm2_shift, fc_weight, fc_bias, out_weight, out_bias, out_cotangent,
):
    width = block_input.shape[-1]
    segments = to_rows(segment_ids)
    x = to_rows(block_input)
    rows, length, _ = x.shape
    tokens = rows * length
    cot = to_rows(out_cotangent)
    slot = jnp.arange(length, dtype=jnp.int32)[None]
    ends = [jnp.sum((segments <= doc).astype(jnp.int32), axis=1, keepdims=True) for doc in range(2)]
    start = jnp.where(
        segments == 0, 0, jnp.where(segments == 1, ends[0], jnp.where(segments == 2, ends[1], slot))
    )
    low_block = start[:, ::BLOCK] // BLOCK
    blocks = length // BLOCK
    high_block = jnp.sum(
        (low_block[:, None, :] <= jnp.arange(blocks)[None, :, None]).astype(jnp.int32), axis=2
    ) - 1
    start = start[:, None, :]
    low_block = low_block.reshape(-1)
    high_block = high_block.reshape(-1)
    x = x.reshape(tokens, width)
    cot = cot.reshape(tokens, width)
    q, k, v, kt, vt = project_qkv(x, norm1_gain, norm1_shift, qkv_weight, qv_bias)
    att, lse = attend(low_block, start, q, k, vt, rows)
    y, grad_middle, grad_att, delta, dfc, doutt, dproj, small_two, dfcb = feed_forward(
        x, att, cot, proj_weight, proj_bias, norm2_gain, norm2_shift, fc_weight, fc_bias, out_weight, out_bias
    )
    both = ("rows", "seq")
    dfc, doutt, dproj = lax.psum((dfc, doutt, dproj), both)
    layer_output = from_rows(y.reshape(rows, length, width), bf16)
    dq, dk, dv = attend_back(high_block, start, q, k, kt, v, grad_att, lse, delta, rows)
    dqkv, small_qv = qkv_weight_back(x, norm1_gain, norm1_shift, dq, dk, dv)
    dqkv = lax.psum(dqkv, both)
    dx, small_one = qkv_input_back(x, norm1_gain, qkv_weight, dq, dk, dv, grad_middle)
    input_grad = from_rows(dx.reshape(rows, length, width), f32)
    small = jnp.concatenate((small_two, small_qv, small_one), axis=0)
    small = jnp.sum(small.reshape(-1, 8, width), axis=1)
    small = jnp.concatenate((small.reshape(-1), jnp.sum(dfcb, axis=0)))
    small = lax.psum(small, both)
    line = lambda i, n=1: small[i * width : (i + n) * width]
    return (
        layer_output,
        input_grad,
        line(6),
        line(7),
        dqkv.astype(f32),
        line(4, 2),
        dproj.astype(f32),
        line(3),
        line(0),
        line(1),
        dfc.astype(f32),
        small[8 * width :],
        jnp.transpose(doutt).astype(f32),
        line(2),
    )


def solution(mesh):
    rows_spec = P("rows", "seq", None)
    in_specs = (rows_spec, P("rows", "seq")) + (P(),) * 12 + (rows_spec,)
    out_specs = (rows_spec, rows_spec) + (P(),) * 12
    body = row_local if mesh.shape["seq"] == 2 else local
    return jax.shard_map(body, mesh=mesh, in_specs=in_specs, out_specs=out_specs, check_vma=False)
```

```python
from functools import partial, reduce

import jax
import jax.numpy as jnp
from jax import lax
from jax.experimental import pallas as pl
from jax.experimental.pallas import tpu as pltpu
from jax.sharding import PartitionSpec as P

HEADS = 12
HEAD_DIM = 64


BRANCH = 12 ** (-0.5)
EPSILON = 1e-05
PADDING = 3.0
NEGATIVE = -1e30
block_keys = 256


def layer_norm(values, scale_gain, shift_bias):
    center = values - jnp.mean(values, axis=-1, keepdims=True)
    variance = jnp.mean(center * center, axis=-1, keepdims=True)
    return center * lax.rsqrt(variance + EPSILON) * scale_gain + shift_bias


def allowed_pairs(query_segments, key_segments, query_slots, key_slots):
    same_doc = query_segments[:, :, None] == key_segments[:, None, :]
    causal = key_slots[None, None, :] <= query_slots[None, :, None]
    itself = key_slots[None, None, :] == query_slots[None, :, None]
    unpadded = key_segments[:, None, :] != PADDING
    return (same_doc & causal & (unpadded | itself))[:, None]


def split_heads(block_rows):
    return block_rows.reshape(block_rows.shape[0], block_rows.shape[1], HEADS, HEAD_DIM)


def fold_blocks(block_step, running, piece_tuple):
    piece_len = piece_tuple[0].shape[1]

    def one_block(block_index, held_state):
        offset = block_index * block_keys
        sub_tuple = tuple(
            (lax.dynamic_slice_in_dim(member, offset, block_keys, 1) for member in piece_tuple)
        )
        return block_step(held_state, sub_tuple, offset)

    return lax.fori_loop(0, piece_len // block_keys, one_block, running)


def keep_same(running):
    return running


def local(
    block_input,
    segment_ids,
    norm1_gain,
    norm1_shift,
    qkv_weight,
    qv_bias,
    proj_weight,
    proj_bias,
    norm2_gain,
    norm2_shift,
    fc_weight,
    fc_bias,
    out_weight,
    out_bias,
    out_cotangent,
):
    row_count, local_len, model_width = block_input.shape
    tokens = row_count * local_len
    full_len = local_len * lax.axis_size("seq")
    my_first = lax.axis_index("seq") * local_len
    query_slots = my_first + jnp.arange(local_len)
    my_segments = segment_ids.astype(jnp.bfloat16)
    my_seg_float = segment_ids.astype(jnp.float32)
    score_scale = HEAD_DIM ** (-0.5)
    inputs = block_input.astype(jnp.float32).reshape(tokens, model_width)
    normed_one = layer_norm(inputs, norm1_gain, norm1_shift).astype(jnp.bfloat16)
    mixed_qkv = jnp.dot(normed_one, qkv_weight, preferred_element_type=jnp.float32)
    query_flat = (
        (mixed_qkv[:, :model_width] + qv_bias[:model_width])
        .astype(jnp.bfloat16)
        .reshape(row_count, local_len, model_width)
    )
    key_rows = (
        mixed_qkv[:, model_width : 2 * model_width]
        .astype(jnp.bfloat16)
        .reshape(row_count, local_len, model_width)
    )
    value_rows = (
        (mixed_qkv[:, 2 * model_width :] + qv_bias[model_width:])
        .astype(jnp.bfloat16)
        .reshape(row_count, local_len, model_width)
    )
    queries = split_heads(query_flat)

    def attend_block(running, sub_tuple, first_slot):
        key_piece, value_piece, seg_piece = sub_tuple
        piece_len = key_piece.shape[1]
        key_slots = first_slot + jnp.arange(piece_len)
        seg_float = seg_piece.astype(jnp.float32)
        skipped = (first_slot > my_first + local_len - 1) | (
            jnp.max(seg_float) < jnp.min(my_seg_float)
        )

        def attend_update(state):
            running_max, running_sum, running_out = state
            scores = (
                jnp.einsum(
                    "rqhd,rkhd->rhqk",
                    queries,
                    split_heads(key_piece),
                    preferred_element_type=jnp.float32,
                )
                * score_scale
            )
            allowed = allowed_pairs(my_seg_float, seg_float, query_slots, key_slots)
            masked = jnp.where(allowed, scores, NEGATIVE)
            new_max = jnp.maximum(running_max, jnp.max(masked, axis=-1))
            prob_block = jnp.where(allowed, jnp.exp(scores - new_max[..., None]), 0.0)
            factor = jnp.exp(running_max - new_max)
            new_sum = running_sum * factor + jnp.sum(prob_block, axis=-1)
            added_part = jnp.einsum(
                "rhqk,rkhd->rqhd",
                prob_block.astype(jnp.bfloat16),
                split_heads(value_piece),
                preferred_element_type=jnp.float32,
            )
            new_out = running_out * jnp.transpose(factor, (0, 2, 1))[..., None] + added_part
            return (new_max, new_sum, new_out)

        return lax.cond(skipped, keep_same, attend_update, running)

    start_state = (
        jnp.full((row_count, HEADS, local_len), NEGATIVE, jnp.float32),
        jnp.zeros((row_count, HEADS, local_len), jnp.float32),
        jnp.zeros((row_count, local_len, HEADS, HEAD_DIM), jnp.float32),
    )
    running_max, running_sum, running_out = fold_blocks(
        attend_block,
        start_state,
        (
            lax.all_gather(key_rows, "seq", axis=1, tiled=True),
            lax.all_gather(value_rows, "seq", axis=1, tiled=True),
            lax.all_gather(my_segments, "seq", axis=1, tiled=True),
        ),
    )
    log_total = running_max + jnp.log(running_sum)
    attended_heads = running_out / jnp.transpose(running_sum, (0, 2, 1))[..., None]
    attended_low = attended_heads.reshape(tokens, model_width).astype(jnp.bfloat16)
    branch_one = jnp.dot(attended_low, proj_weight, preferred_element_type=jnp.float32) + proj_bias
    middle = inputs + BRANCH * branch_one
    normed_two = layer_norm(middle, norm2_gain, norm2_shift).astype(jnp.bfloat16)
    hidden_pre = jnp.dot(normed_two, fc_weight, preferred_element_type=jnp.float32) + fc_bias
    hidden_act = jax.nn.gelu(hidden_pre, approximate=True).astype(jnp.bfloat16)
    branch_two = jnp.dot(hidden_act, out_weight, preferred_element_type=jnp.float32) + out_bias
    layer_output = (
        (middle + BRANCH * branch_two)
        .astype(jnp.bfloat16)
        .reshape(row_count, local_len, model_width)
    )
    flat_cot = out_cotangent.reshape(tokens, model_width).astype(jnp.float32)
    grad_two = (BRANCH * flat_cot).astype(jnp.bfloat16)
    grad_out_weight = jnp.einsum(
        "tf,td->fd", hidden_act, grad_two, preferred_element_type=jnp.float32
    )
    grad_out_bias = jnp.sum(grad_two.astype(jnp.float32), axis=0)
    grad_act = jnp.einsum("td,fd->tf", grad_two, out_weight, preferred_element_type=jnp.float32)
    gelu_value, gelu_pull = jax.vjp(partial(jax.nn.gelu, approximate=True), hidden_pre)
    grad_pre = gelu_pull(grad_act)[0].astype(jnp.bfloat16)
    grad_fc_weight = jnp.einsum(
        "td,tf->df", normed_two, grad_pre, preferred_element_type=jnp.float32
    )
    grad_fc_bias = jnp.sum(grad_pre.astype(jnp.float32), axis=0)
    grad_normed_two = jnp.einsum(
        "tf,df->td", grad_pre, fc_weight, preferred_element_type=jnp.float32
    )
    norm_value, norm_pull = jax.vjp(layer_norm, middle, norm2_gain, norm2_shift)
    grad_inner, grad_norm2_gain, grad_norm2_shift = norm_pull(grad_normed_two)
    grad_middle = flat_cot + grad_inner
    grad_one = (BRANCH * grad_middle).astype(jnp.bfloat16)
    grad_proj_weight = jnp.einsum(
        "td,te->de", attended_low, grad_one, preferred_element_type=jnp.float32
    )
    grad_proj_bias = jnp.sum(grad_one.astype(jnp.float32), axis=0)
    grad_attended_flat = (
        jnp.einsum("te,de->td", grad_one, proj_weight, preferred_element_type=jnp.float32)
        .astype(jnp.bfloat16)
        .reshape(row_count, local_len, model_width)
    )
    grad_attended = split_heads(grad_attended_flat)
    grad_delta = jnp.einsum("rqhd,rqhd->rhq", grad_attended.astype(jnp.float32), attended_heads)

    def back_block(running, sub_tuple, first_slot):
        key_piece, value_piece, seg_piece = sub_tuple
        piece_len = key_piece.shape[1]
        key_slots = first_slot + jnp.arange(piece_len)
        seg_float = seg_piece.astype(jnp.float32)
        skipped = (first_slot > my_first + local_len - 1) | (
            jnp.max(seg_float) < jnp.min(my_seg_float)
        )

        def back_update(state):
            grad_query, grad_full = state
            key_heads = split_heads(key_piece)
            value_heads = split_heads(value_piece)
            scores = (
                jnp.einsum(
                    "rqhd,rkhd->rhqk", queries, key_heads, preferred_element_type=jnp.float32
                )
                * score_scale
            )
            allowed = allowed_pairs(my_seg_float, seg_float, query_slots, key_slots)
            prob_block = jnp.where(allowed, jnp.exp(scores - log_total[..., None]), 0.0)
            grad_probs = jnp.einsum(
                "rqhd,rkhd->rhqk", grad_attended, value_heads, preferred_element_type=jnp.float32
            )
            grad_scores = (score_scale * prob_block * (grad_probs - grad_delta[..., None])).astype(
                jnp.bfloat16
            )
            new_query = grad_query + jnp.einsum(
                "rhqk,rkhd->rqhd", grad_scores, key_heads, preferred_element_type=jnp.float32
            )
            grad_keys = jnp.einsum(
                "rhqk,rqhd->rkhd", grad_scores, queries, preferred_element_type=jnp.float32
            ).reshape(row_count, piece_len, model_width)
            grad_values = jnp.einsum(
                "rhqk,rqhd->rkhd",
                prob_block.astype(jnp.bfloat16),
                grad_attended,
                preferred_element_type=jnp.float32,
            ).reshape(row_count, piece_len, model_width)
            held_part = lax.dynamic_slice_in_dim(grad_full, first_slot, piece_len, 2)
            new_full = lax.dynamic_update_slice_in_dim(
                grad_full, held_part + jnp.stack((grad_keys, grad_values)), first_slot, 2
            )
            return (new_query, new_full)

        return lax.cond(skipped, keep_same, back_update, running)

    back_start = (
        jnp.zeros((row_count, local_len, HEADS, HEAD_DIM), jnp.float32),
        jnp.zeros((2, row_count, full_len, model_width), jnp.float32),
    )
    grad_query, grad_full = fold_blocks(
        back_block,
        back_start,
        (
            lax.all_gather(key_rows, "seq", axis=1, tiled=True),
            lax.all_gather(value_rows, "seq", axis=1, tiled=True),
            lax.all_gather(my_segments, "seq", axis=1, tiled=True),
        ),
    )
    grad_pairs = lax.psum_scatter(
        grad_full.astype(jnp.bfloat16), "seq", scatter_dimension=2, tiled=True
    ).astype(jnp.float32)
    grad_query_low = grad_query.reshape(row_count, local_len, model_width).astype(jnp.bfloat16)
    grad_key_low = grad_pairs[0].astype(jnp.bfloat16)
    grad_value_low = grad_pairs[1].astype(jnp.bfloat16)
    grad_qkv_low = jnp.concatenate((grad_query_low, grad_key_low, grad_value_low), axis=-1).reshape(
        tokens, 3 * model_width
    )
    grad_qkv_weight = jnp.einsum(
        "td,te->de", normed_one, grad_qkv_low, preferred_element_type=jnp.float32
    )
    grad_qv_bias = jnp.concatenate(
        (
            jnp.sum(grad_query_low.astype(jnp.float32), axis=(0, 1)),
            jnp.sum(grad_value_low.astype(jnp.float32), axis=(0, 1)),
        )
    )
    grad_normed_one = jnp.einsum(
        "te,de->td", grad_qkv_low, qkv_weight, preferred_element_type=jnp.float32
    )
    first_value, first_pull = jax.vjp(layer_norm, inputs, norm1_gain, norm1_shift)
    grad_first, grad_norm1_gain, grad_norm1_shift = first_pull(grad_normed_one)
    input_grad = (grad_middle + grad_first).reshape(row_count, local_len, model_width)
    local_grads = (
        grad_norm1_gain,
        grad_norm1_shift,
        grad_qkv_weight,
        grad_qv_bias,
        grad_proj_weight,
        grad_proj_bias,
        grad_norm2_gain,
        grad_norm2_shift,
        grad_fc_weight,
        grad_fc_bias,
        grad_out_weight,
        grad_out_bias,
    )
    shares = (
        lax.psum_scatter(
            local_grads[0].astype(jnp.bfloat16), "rows", scatter_dimension=0, tiled=True
        ).astype(jnp.float32),
        lax.psum_scatter(
            local_grads[1].astype(jnp.bfloat16), "rows", scatter_dimension=0, tiled=True
        ).astype(jnp.float32),
        lax.psum_scatter(
            local_grads[2].astype(jnp.bfloat16), "rows", scatter_dimension=0, tiled=True
        ).astype(jnp.float32),
        lax.psum_scatter(
            local_grads[3].astype(jnp.bfloat16), "rows", scatter_dimension=0, tiled=True
        ).astype(jnp.float32),
        lax.psum_scatter(
            local_grads[4].astype(jnp.bfloat16), "rows", scatter_dimension=0, tiled=True
        ).astype(jnp.float32),
        lax.psum_scatter(
            local_grads[5].astype(jnp.bfloat16), "rows", scatter_dimension=0, tiled=True
        ).astype(jnp.float32),
        lax.psum_scatter(
            local_grads[6].astype(jnp.bfloat16), "rows", scatter_dimension=0, tiled=True
        ).astype(jnp.float32),
        lax.psum_scatter(
            local_grads[7].astype(jnp.bfloat16), "rows", scatter_dimension=0, tiled=True
        ).astype(jnp.float32),
        lax.psum_scatter(
            local_grads[8].astype(jnp.bfloat16), "rows", scatter_dimension=0, tiled=True
        ).astype(jnp.float32),
        lax.psum_scatter(
            local_grads[9].astype(jnp.bfloat16), "rows", scatter_dimension=0, tiled=True
        ).astype(jnp.float32),
        lax.psum_scatter(
            local_grads[10].astype(jnp.bfloat16), "rows", scatter_dimension=0, tiled=True
        ).astype(jnp.float32),
        lax.psum_scatter(
            local_grads[11].astype(jnp.bfloat16), "rows", scatter_dimension=0, tiled=True
        ).astype(jnp.float32),
    )
    shares = (
        lax.psum(shares[0].astype(jnp.bfloat16), "seq").astype(jnp.float32),
        lax.psum(shares[1].astype(jnp.bfloat16), "seq").astype(jnp.float32),
        lax.psum(shares[2].astype(jnp.bfloat16), "seq").astype(jnp.float32),
        lax.psum(shares[3].astype(jnp.bfloat16), "seq").astype(jnp.float32),
        lax.psum(shares[4].astype(jnp.bfloat16), "seq").astype(jnp.float32),
        lax.psum(shares[5].astype(jnp.bfloat16), "seq").astype(jnp.float32),
        lax.psum(shares[6].astype(jnp.bfloat16), "seq").astype(jnp.float32),
        lax.psum(shares[7].astype(jnp.bfloat16), "seq").astype(jnp.float32),
        lax.psum(shares[8].astype(jnp.bfloat16), "seq").astype(jnp.float32),
        lax.psum(shares[9].astype(jnp.bfloat16), "seq").astype(jnp.float32),
        lax.psum(shares[10].astype(jnp.bfloat16), "seq").astype(jnp.float32),
        lax.psum(shares[11].astype(jnp.bfloat16), "seq").astype(jnp.float32),
    )
    totals = (
        lax.all_gather(shares[0].astype(jnp.bfloat16), "rows", axis=0, tiled=True).astype(
            jnp.float32
        ),
        lax.all_gather(shares[1].astype(jnp.bfloat16), "rows", axis=0, tiled=True).astype(
            jnp.float32
        ),
        lax.all_gather(shares[2].astype(jnp.bfloat16), "rows", axis=0, tiled=True).astype(
            jnp.float32
        ),
        lax.all_gather(shares[3].astype(jnp.bfloat16), "rows", axis=0, tiled=True).astype(
            jnp.float32
        ),
        lax.all_gather(shares[4].astype(jnp.bfloat16), "rows", axis=0, tiled=True).astype(
            jnp.float32
        ),
        lax.all_gather(shares[5].astype(jnp.bfloat16), "rows", axis=0, tiled=True).astype(
            jnp.float32
        ),
        lax.all_gather(shares[6].astype(jnp.bfloat16), "rows", axis=0, tiled=True).astype(
            jnp.float32
        ),
        lax.all_gather(shares[7].astype(jnp.bfloat16), "rows", axis=0, tiled=True).astype(
            jnp.float32
        ),
        lax.all_gather(shares[8].astype(jnp.bfloat16), "rows", axis=0, tiled=True).astype(
            jnp.float32
        ),
        lax.all_gather(shares[9].astype(jnp.bfloat16), "rows", axis=0, tiled=True).astype(
            jnp.float32
        ),
        lax.all_gather(shares[10].astype(jnp.bfloat16), "rows", axis=0, tiled=True).astype(
            jnp.float32
        ),
        lax.all_gather(shares[11].astype(jnp.bfloat16), "rows", axis=0, tiled=True).astype(
            jnp.float32
        ),
    )
    return (layer_output, input_grad) + tuple(totals)


MIB = 1 << 20
LOG2E = 1.4426950408889634
GELU_C = 0.7978845608028654
GELU_A = 0.044715
BLOCK = 256
f32 = jnp.float32
bf16 = jnp.bfloat16


def dot_nn(a, b):
    return lax.dot_general(a, b, (((1,), (0,)), ((), ())), preferred_element_type=f32)


def dot_tn(a, b):
    return lax.dot_general(a, b, (((0,), (0,)), ((), ())), preferred_element_type=f32)


def dot_nt(a, b):
    return lax.dot_general(a, b, (((1,), (1,)), ((), ())), preferred_element_type=f32)


def norm_parts(values):
    center = values - jnp.mean(values, axis=-1, keepdims=True)
    variance = jnp.mean(center * center, axis=-1, keepdims=True)
    inverse = lax.rsqrt(variance + EPSILON)
    return center * inverse, inverse


def row_sums(values):
    rows, cols = values.shape
    return jnp.sum(values.reshape(rows // 8, 8, cols), axis=0)


def whole(shape):
    return pl.BlockSpec(shape, lambda *_: (0,) * len(shape), pipeline_mode=pl.Buffered(1))


def call(
    kernel, name, grid, in_specs, out_specs, out_shape, scratch, flops, moved, vmem, prefetch=1, aliases=None
):
    return pl.pallas_call(
        kernel,
        out_shape=out_shape,
        grid_spec=pltpu.PrefetchScalarGridSpec(
            num_scalar_prefetch=prefetch,
            grid=grid,
            in_specs=in_specs,
            out_specs=out_specs,
            scratch_shapes=scratch,
        ),
        compiler_params=pltpu.CompilerParams(vmem_limit_bytes=vmem * MIB),
        cost_estimate=pl.CostEstimate(flops=flops, bytes_accessed=moved, transcendentals=0),
        input_output_aliases=aliases or {},
        name=name,
    )


TILE = 512
LIMIT = 2.0**100


class Place:
    def __init__(self, rows, half_len):
        self.rows, self.per = rows, half_len // TILE
        self.phase = rows * self.per
        self.steps = 2 * self.phase

    def own(self, t, me):
        return me[0] * self.phase + jnp.minimum(t, self.phase - 1), 0

    def got(self, t, me):
        return jnp.maximum(t - self.phase, 0), 0

    def slot(self, t, me):
        late = t // self.phase
        half = jnp.where(late == 0, me[0], 1 - me[0])
        at = t - late * self.phase
        return (at // self.per) * 2 * self.per + half * self.per + at % self.per

    def turned(self, t, me):
        return 0, self.slot(t, me)


def either(step, phase, own_ref, got_ref):
    return jnp.where(step < phase, own_ref[...], got_ref[...])


def qkv_kernel(me_ref, x_ref, gain_ref, shift_ref, w_ref, bias_ref, *refs):
    width = x_ref.shape[1]
    hat, _ = norm_parts(x_ref[...].astype(f32))
    normed = (hat * gain_ref[...] + shift_ref[...]).astype(bf16)
    for i, ref in enumerate(refs[-3:]):
        part = dot_nt(w_ref[i * width : (i + 1) * width, :], normed)
        if i != 1:
            part = part + bias_ref[i * width : (i + 1) * width, :]
        ref[...] = part.astype(bf16)


def project_qkv(me, x, params, place, first, count, got, earlier, after):
    width = x.shape[1]
    tokens = place.steps * TILE
    index = (lambda t, me: (t, 0)) if got else (lambda t, me: place.own(t + first, me))
    turned = pl.BlockSpec((width, TILE), lambda t, me: place.turned(t + first, me))
    anywhere = pl.BlockSpec(memory_space=pl.ANY)
    extra = list(earlier) + list(after)
    return call(
        qkv_kernel,
        "qkv_forward",
        (count,),
        [pl.BlockSpec((TILE, width), index)]
        + [whole(p.shape) for p in params]
        + [anywhere] * len(extra),
        [turned] * 3,
        [jax.ShapeDtypeStruct((width, tokens), bf16)] * 3,
        [],
        2 * count * TILE * width * 3 * width,
        count * TILE * width * 8 + width * width * 6,
        60,
        aliases={6 + i: i for i in range(len(earlier))},
    )(me, x, *params, *extra)


def attend_kernel(low_ref, start_ref, qt_ref, kt_ref, vt_ref, *refs, row):
    att_ref, lse_ref, acc, base, bias = refs[-5:]
    width, length = qt_ref.shape
    heads = width // HEAD_DIM
    pad = HEAD_DIM + 16
    blocks = length // BLOCK
    scale = HEAD_DIM**-0.5 * LOG2E
    slots = lax.broadcasted_iota(jnp.int32, (BLOCK, BLOCK), 0)
    query_iota = lax.broadcasted_iota(jnp.int32, (BLOCK, BLOCK), 1)
    ones = jnp.ones((16, BLOCK), bf16)

    def at(i):
        return pl.ds(pl.multiple_of(i * BLOCK, BLOCK), BLOCK)

    def head_rows(h):
        return slice(h * HEAD_DIM, (h + 1) * HEAD_DIM)

    def acc_rows(h):
        return slice(h * pad, (h + 1) * pad)

    def total(h):
        return acc[h * pad + HEAD_DIM : h * pad + HEAD_DIM + 1, :]

    def score(h, qb, kb):
        return dot_tn(kt_ref[head_rows(h), at(kb)], qt_ref[head_rows(h), at(qb)])

    def weigh(h, kb, probs):
        return dot_nn(jnp.concatenate((vt_ref[head_rows(h), at(kb)], ones), axis=0), probs)

    def set_bias(qb, kb):
        allowed = (slots >= start_ref[0, :, at(qb)] - kb * BLOCK) & (
            slots + (kb - qb) * BLOCK <= query_iota
        )
        bias[...] = jnp.where(allowed, 0.0, NEGATIVE)

    def query_block(qb, carry):
        low = low_ref[row * blocks + qb]
        for h in range(heads):
            own = qt_ref[head_rows(h), at(qb)].astype(f32) * kt_ref[head_rows(h), at(qb)].astype(f32)
            base[h : h + 1, :] = jnp.sum(own, axis=0, keepdims=True) * scale
        acc[...] = jnp.zeros_like(acc)

        def fast(kb, carry):
            set_bias(qb, kb)

            def finish(h, probs):
                acc[acc_rows(h), :] += weigh(h, kb, probs)

            ahead = [score(h, qb, kb) for h in range(min(3, heads))]
            waiting = []
            for h in range(heads):
                scores = ahead.pop(0)
                if h + 3 < heads:
                    ahead.append(score(h + 3, qb, kb))
                probs = jnp.exp2(scores * scale + (bias[...] - base[h : h + 1, :]))
                waiting.append((h, probs.astype(bf16)))
                if len(waiting) > 1:
                    finish(*waiting.pop(0))
            finish(*waiting[0])
            return carry

        lax.fori_loop(low, qb + 1, fast, 0)
        largest = reduce(jnp.maximum, [total(h) for h in range(heads)])

        @pl.when(jnp.logical_not(jnp.max(largest) < LIMIT))
        def _():
            base[...] = jnp.full_like(base, NEGATIVE)
            acc[...] = jnp.zeros_like(acc)

            def safe(kb, carry):
                set_bias(qb, kb)
                for h in range(heads):
                    scores = score(h, qb, kb) * scale + bias[...]
                    old = base[h : h + 1, :]
                    top = jnp.maximum(old, jnp.max(scores, axis=0, keepdims=True))
                    base[h : h + 1, :] = top
                    probs = jnp.exp2(scores - top).astype(bf16)
                    acc[acc_rows(h), :] = acc[acc_rows(h), :] * jnp.exp2(old - top) + weigh(h, kb, probs)
                return carry

            lax.fori_loop(low, qb + 1, safe, 0)

        for h in range(heads):
            out = acc[h * pad : h * pad + HEAD_DIM, :]
            att_ref[head_rows(h), at(qb)] = (out / total(h)).astype(bf16)
            lse_ref[h // 2, h % 2 : h % 2 + 1, at(qb)] = base[h : h + 1, :] + jnp.log2(total(h))
        return carry

    lax.fori_loop(0, blocks, query_block, 0)


def attend(low, start, qt, kt, vt, row, length, earlier):
    width, tokens = qt.shape
    heads = width // HEAD_DIM
    turned = pl.BlockSpec((width, length), lambda i, low: (0, row))
    lined = pl.BlockSpec((heads // 2, 2, length), lambda i, low: (0, 0, row))
    return call(
        partial(attend_kernel, row=row),
        "attention_forward",
        (1,),
        [pl.BlockSpec((1, 1, length), lambda i, low: (row, 0, 0)), turned, turned, turned]
        + [pl.BlockSpec(memory_space=pl.ANY)] * len(earlier),
        [turned, lined],
        [
            jax.ShapeDtypeStruct((width, tokens), bf16),
            jax.ShapeDtypeStruct((heads // 2, 2, tokens), f32),
        ],
        [
            pltpu.VMEM((heads * (HEAD_DIM + 16), BLOCK), f32),
            pltpu.VMEM((16, BLOCK), f32),
            pltpu.VMEM((BLOCK, BLOCK), f32),
        ],
        2 * length * length * width,
        length * width * 8,
        60,
        aliases={5 + i: i for i in range(len(earlier))},
    )(low, start, qt, kt, vt, *earlier)


def attend_back_kernel(
    high_ref, start_ref, qt_ref, kt_ref, vt_ref, dot_ref, lse_ref, delta_ref,
    dqt_ref, dkt_ref, dvt_ref, dq, dk, dv, bias,
):
    row = pl.program_id(0)
    width, length = qt_ref.shape
    heads = width // HEAD_DIM
    blocks = length // BLOCK
    scale = HEAD_DIM**-0.5 * LOG2E
    slots = lax.broadcasted_iota(jnp.int32, (BLOCK, BLOCK), 0)
    query_iota = lax.broadcasted_iota(jnp.int32, (BLOCK, BLOCK), 1)
    dq[...] = jnp.zeros_like(dq)

    def at(i):
        return pl.ds(pl.multiple_of(i * BLOCK, BLOCK), BLOCK)

    def key_block(kb, carry):
        k_at = at(kb)

        def visit(qb, first):
            q_at = at(qb)
            allowed = slots >= start_ref[0, :, q_at] - kb * BLOCK
            if first:
                allowed = allowed & (slots <= query_iota)
            bias[...] = jnp.where(allowed, 0.0, NEGATIVE)

            def begin(h):
                rows = slice(h * HEAD_DIM, (h + 1) * HEAD_DIM)
                return (
                    dot_tn(kt_ref[rows, k_at], qt_ref[rows, q_at]),
                    dot_tn(vt_ref[rows, k_at], dot_ref[rows, q_at]),
                )

            def finish(h, probs, grad_scores):
                rows = slice(h * HEAD_DIM, (h + 1) * HEAD_DIM)
                dv_new = dot_nt(dot_ref[rows, q_at], probs)
                dk_new = dot_nt(qt_ref[rows, q_at], grad_scores)
                dv[rows, :] = dv_new if first else dv[rows, :] + dv_new
                dk[rows, :] = dk_new if first else dk[rows, :] + dk_new
                dq[rows, q_at] += dot_nn(kt_ref[rows, k_at], grad_scores)

            ahead = [begin(0)]
            waiting = []
            for h in range(heads):
                scores, grad_probs = ahead.pop(0)
                if h + 1 < heads:
                    ahead.append(begin(h + 1))
                line = (h // 2, slice(h % 2, h % 2 + 1), q_at)
                probs = jnp.exp2(scores * scale + (bias[...] - lse_ref[line]))
                grad_scores = (probs * (grad_probs - delta_ref[line])).astype(bf16)
                waiting.append((h, probs.astype(bf16), grad_scores))
                if len(waiting) > 1:
                    finish(*waiting.pop(0))
            finish(*waiting[0])

        visit(kb, True)

        def later(qb, carry):
            visit(qb, False)
            return carry

        lax.fori_loop(kb + 1, high_ref[row * blocks + kb] + 1, later, 0)
        dkt_ref[:, k_at] = (dk[...] * HEAD_DIM**-0.5).astype(bf16)
        dvt_ref[:, k_at] = dv[...].astype(bf16)
        return carry

    lax.fori_loop(0, blocks, key_block, 0)
    dqt_ref[...] = (dq[...] * HEAD_DIM**-0.5).astype(bf16)


def attend_back(high, start, qt, kt, vt, dot, lse, delta, rows):
    width, tokens = qt.shape
    length = tokens // rows
    heads = width // HEAD_DIM
    turned = pl.BlockSpec((width, length), lambda r, high: (0, r))
    lined = pl.BlockSpec((heads // 2, 2, length), lambda r, high: (0, 0, r))
    return call(
        attend_back_kernel,
        "attention_backward",
        (rows,),
        [pl.BlockSpec((1, 1, length), lambda r, high: (r, 0, 0)), turned, turned, turned, turned, lined, lined],
        [turned] * 3,
        [jax.ShapeDtypeStruct((width, tokens), bf16)] * 3,
        [
            pltpu.VMEM((width, length), f32),
            pltpu.VMEM((width, BLOCK), f32),
            pltpu.VMEM((width, BLOCK), f32),
            pltpu.VMEM((BLOCK, BLOCK), f32),
        ],
        5 * tokens * length * width,
        tokens * width * 14,
        62,
    )(high, start, qt, kt, vt, dot, lse, delta)


def mlp_kernel(
    me_ref, x_ref, xg_ref, cot_ref, cotg_ref, att_ref, proj_ref, projb_ref, gain_ref, shift_ref, fc_ref, fcb_ref,
    out_ref, outb_ref,
    kept_ref, sent_ref, gm_ref, do_ref, delta_ref, dfc_ref, dout_ref, dproj_ref, small_ref, dfcb_ref,
    dfc, doutt, dproj, sums, dfcb, stage, sem,
):
    step = pl.program_id(0)
    steps = pl.num_programs(0)
    phase = steps // 2
    tile, width = x_ref.shape
    hidden = fc_ref.shape[1]
    chunk = 768

    @pl.when(step == 0)
    def _():
        dfc[...] = jnp.zeros_like(dfc)
        doutt[...] = jnp.zeros_like(doutt)
        dproj[...] = jnp.zeros_like(dproj)
        sums[...] = jnp.zeros_like(sums)
        dfcb[...] = jnp.zeros_like(dfcb)

    att_t = att_ref[...]
    x = either(step, phase, x_ref, xg_ref).astype(f32)
    middle = x + BRANCH * (dot_tn(att_t, proj_ref[...]) + projb_ref[...])
    hat, inverse = norm_parts(middle)
    normed = (hat * gain_ref[...] + shift_ref[...]).astype(bf16)
    normed_t = jnp.transpose(normed)
    cot = either(step, phase, cot_ref, cotg_ref).astype(f32)
    grad_two = (BRANCH * cot).astype(bf16)
    grad_two_t = jnp.transpose(grad_two)
    branch = jnp.zeros((tile, width), f32)
    grad_normed = jnp.zeros((tile, width), f32)
    for at in range(0, hidden, chunk):
        cols = slice(at, at + chunk)
        pre = dot_nn(normed, fc_ref[:, cols]) + fcb_ref[:, cols]
        grad_act = dot_nt(grad_two, out_ref[cols, :])
        square = pre * pre
        half = 0.5 + 0.5 * jnp.tanh(pre * (GELU_C + GELU_C * GELU_A * square))
        act = pre * half
        slope = half + act * (1.0 - half) * (2.0 * GELU_C + 6.0 * GELU_C * GELU_A * square)
        act = act.astype(bf16)
        grad_pre = (grad_act * slope).astype(bf16)
        branch += dot_nn(act, out_ref[cols, :])
        grad_normed += dot_nt(grad_pre, fc_ref[:, cols])
        dfc[:, cols] += dot_nn(normed_t, grad_pre)
        doutt[:, cols] += dot_nn(grad_two_t, act)
        dfcb[:, cols] += row_sums(grad_pre.astype(f32))
    y = (middle + BRANCH * (branch + outb_ref[...])).astype(bf16)

    @pl.when(step < phase)
    def _():
        kept_ref[...] = y

    @pl.when(step >= phase)
    def _():
        sent_ref[...] = y

    scaled = grad_normed * gain_ref[...]
    mean_one = jnp.mean(scaled, axis=-1, keepdims=True)
    mean_two = jnp.mean(scaled * hat, axis=-1, keepdims=True)
    grad_middle = cot + inverse * (scaled - mean_one - hat * mean_two)
    gm_ref[...] = grad_middle.astype(bf16)
    grad_one = (BRANCH * grad_middle).astype(bf16)
    dproj[...] += dot_nn(att_t, grad_one)
    grad_att = dot_nt(proj_ref[...], grad_one).astype(bf16)
    do_ref[...] = grad_att
    product = grad_att.astype(f32) * att_t.astype(f32)
    for h in range(width // HEAD_DIM):
        part = product[h * HEAD_DIM : (h + 1) * HEAD_DIM, :]
        delta_ref[h // 2, h % 2 : h % 2 + 1, :] = jnp.sum(part, axis=0, keepdims=True)
    sums[0:8, :] += row_sums(grad_normed * hat)
    sums[8:16, :] += row_sums(grad_normed)
    sums[16:24, :] += row_sums(grad_two.astype(f32))
    sums[24:32, :] += row_sums(grad_one.astype(f32))

    @pl.when(step == steps - 1)
    def _():
        for at in range(0, hidden, chunk):
            cols = slice(at, at + chunk)
            stage[...] = dfc[:, cols].astype(bf16)
            copy = pltpu.make_async_copy(stage, dfc_ref.at[:, cols], sem)
            copy.start()
            copy.wait()
            stage[...] = jnp.transpose(doutt[:, cols].astype(bf16))
            copy = pltpu.make_async_copy(stage, dout_ref.at[cols, :], sem)
            copy.start()
            copy.wait()
        dproj_ref[...] = dproj[...].astype(bf16)
        small_ref[...] = sums[...]
        dfcb_ref[...] = dfcb[...]


def feed_forward(
    me, x, x_got, cot, cot_got, att, place, proj_weight, proj_bias, gain, shift, fc_weight, fc_bias, out_weight, out_bias
):
    width, tokens = att.shape
    hidden = fc_weight.shape[1]
    heads = width // HEAD_DIM
    own = pl.BlockSpec((TILE, width), place.own)
    got = pl.BlockSpec((TILE, width), place.got)
    turned = pl.BlockSpec((width, TILE), place.turned)
    plain = pl.BlockSpec((TILE, width), lambda t, me: (t, 0))
    anywhere = pl.BlockSpec(memory_space=pl.ANY)
    return call(
        mlp_kernel,
        "feed_forward",
        (place.steps,),
        [own, got, own, got, turned, whole((width, width)), whole((1, width)), whole((1, width)), whole((1, width)),
         whole(fc_weight.shape), whole((1, hidden)), whole(out_weight.shape), whole((1, width))],
        [own, got, plain, turned,
         pl.BlockSpec((heads // 2, 2, TILE), lambda t, me: (0, 0, place.slot(t, me))),
         anywhere, anywhere, whole((width, width)), whole((32, width)), whole((8, hidden))],
        [
            jax.ShapeDtypeStruct((tokens, width), bf16),
            jax.ShapeDtypeStruct((tokens // 2, width), bf16),
            jax.ShapeDtypeStruct((tokens, width), bf16),
            jax.ShapeDtypeStruct((width, tokens), bf16),
            jax.ShapeDtypeStruct((heads // 2, 2, tokens), f32),
            jax.ShapeDtypeStruct((width, hidden), bf16),
            jax.ShapeDtypeStruct((hidden, width), bf16),
            jax.ShapeDtypeStruct((width, width), bf16),
            jax.ShapeDtypeStruct((32, width), f32),
            jax.ShapeDtypeStruct((8, hidden), f32),
        ],
        [
            pltpu.VMEM((width, hidden), f32),
            pltpu.VMEM((width, hidden), f32),
            pltpu.VMEM((width, width), f32),
            pltpu.VMEM((32, width), f32),
            pltpu.VMEM((8, hidden), f32),
            pltpu.VMEM((width, 768), bf16),
            pltpu.SemaphoreType.DMA,
        ],
        2 * tokens * width * (3 * width + 6 * hidden),
        tokens * width * 14,
        63,
    )(me, x, x_got, cot, cot_got, att, proj_weight, proj_bias[None], gain[None], shift[None], fc_weight, fc_bias[None],
      out_weight, out_bias[None])


def qkv_weight_kernel(
    me_ref, x_ref, xg_ref, gain_ref, shift_ref, dq_ref, dk_ref, dv_ref, dw_ref, small_ref, acc, sums
):
    step = pl.program_id(0)
    steps = pl.num_programs(0)
    width = x_ref.shape[1]

    @pl.when(step == 0)
    def _():
        acc[...] = jnp.zeros_like(acc)
        sums[...] = jnp.zeros_like(sums)

    hat, _ = norm_parts(either(step, steps // 2, x_ref, xg_ref).astype(f32))
    normed_t = jnp.transpose((hat * gain_ref[...] + shift_ref[...]).astype(bf16))
    for i, ref in enumerate((dq_ref, dk_ref, dv_ref)):
        acc[i * width : (i + 1) * width, :] += dot_nt(normed_t, ref[...])
    for i, ref in enumerate((dq_ref, dv_ref)):
        part = ref[...].astype(f32)
        sums[i] += sum(part[:, j : j + 128] for j in range(0, part.shape[1], 128))

    @pl.when(step == steps - 1)
    def _():
        dw_ref[...] = acc[...].astype(bf16)
        small_ref[...] = sums[...]


def qkv_weight_back(me, x, x_got, place, gain, shift, dq, dk, dv):
    width, tokens = dq.shape
    turned = pl.BlockSpec((width, TILE), place.turned)
    return call(
        qkv_weight_kernel,
        "qkv_weight_gradient",
        (place.steps,),
        [pl.BlockSpec((TILE, width), place.own), pl.BlockSpec((TILE, width), place.got),
         whole((1, width)), whole((1, width)), turned, turned, turned],
        [whole((3 * width, width)), whole((2, width, 128))],
        [jax.ShapeDtypeStruct((3 * width, width), bf16), jax.ShapeDtypeStruct((2, width, 128), f32)],
        [pltpu.VMEM((3 * width, width), f32), pltpu.VMEM((2, width, 128), f32)],
        2 * tokens * width * 3 * width,
        tokens * width * 8,
        60,
    )(me, x, x_got, gain[None], shift[None], dq, dk, dv)


def qkv_input_kernel(
    me_ref, x_ref, xg_ref, gain_ref, w_ref, dq_ref, dk_ref, dv_ref, gm_ref, kept_ref, sent_ref, small_ref, sums
):
    step = pl.program_id(0)
    steps = pl.num_programs(0)
    width = x_ref.shape[1]

    @pl.when(step == 0)
    def _():
        sums[...] = jnp.zeros_like(sums)

    hat, inverse = norm_parts(either(step, steps // 2, x_ref, xg_ref).astype(f32))
    grad_normed = jnp.transpose(
        dot_nn(w_ref[:, :width], dq_ref[...])
        + dot_nn(w_ref[:, width : 2 * width], dk_ref[...])
        + dot_nn(w_ref[:, 2 * width :], dv_ref[...])
    )
    scaled = grad_normed * gain_ref[...]
    mean_one = jnp.mean(scaled, axis=-1, keepdims=True)
    mean_two = jnp.mean(scaled * hat, axis=-1, keepdims=True)
    grad_x = gm_ref[...].astype(f32) + inverse * (scaled - mean_one - hat * mean_two)

    @pl.when(step < steps // 2)
    def _():
        kept_ref[...] = grad_x

    @pl.when(step >= steps // 2)
    def _():
        sent_ref[...] = grad_x.astype(bf16)

    sums[0:8, :] += row_sums(grad_normed * hat)
    sums[8:16, :] += row_sums(grad_normed)

    @pl.when(step == steps - 1)
    def _():
        small_ref[...] = sums[...]


def qkv_input_back(me, x, x_got, place, gain, weight, dq, dk, dv, grad_middle):
    width, tokens = dq.shape
    own = pl.BlockSpec((TILE, width), place.own)
    got = pl.BlockSpec((TILE, width), place.got)
    turned = pl.BlockSpec((width, TILE), place.turned)
    return call(
        qkv_input_kernel,
        "qkv_input_gradient",
        (place.steps,),
        [own, got, whole((1, width)), whole(weight.shape), turned, turned, turned,
         pl.BlockSpec((TILE, width), lambda t, me: (t, 0))],
        [own, got, whole((16, width))],
        [
            jax.ShapeDtypeStruct((tokens, width), f32),
            jax.ShapeDtypeStruct((tokens // 2, width), bf16),
            jax.ShapeDtypeStruct((16, width), f32),
        ],
        [pltpu.VMEM((16, width), f32)],
        2 * tokens * width * 3 * width,
        tokens * width * 16,
        60,
    )(me, x, x_got, gain[None], weight, dq, dk, dv, grad_middle)


MESH = pl.DeviceIdType.MESH
PARTS = 6


def bits_of(rows):
    bits = [("rows", 1 << i) for i in range(rows.bit_length() - 1)]
    return bits[0], bits[1:2] + [("seq", 1)] + bits[2:], [("seq", 1)] + bits[2:] + bits[1:2]


def bit_value(bit):
    axis, weight = bit
    return lax.rem(lax.div(lax.axis_index(axis), weight), 2)


def partner(bit):
    axis, weight = bit
    return {axis: lax.axis_index(axis) + weight * (1 - 2 * bit_value(bit))}


def reduce_kernel(
    rows, one_ref, two_ref, small_ref, out_ref, small_out_ref,
    buf, full, core_recv, recv, lines, line_recv, sems, core_sems, line_sems, local_sem,
):
    core, order_a, order_b = bits_of(rows)
    stages = len(order_a)
    total = buf.shape[0]
    part = total // 2 // PARTS
    orders = [order_b if p % 3 == 1 else order_a for p in range(PARTS)]

    barrier = pltpu.get_barrier_semaphore()
    for bit in [core] + order_a:
        pl.semaphore_signal(barrier, inc=1, device_id=partner(bit), device_id_type=MESH)
    split = one_ref.shape[0]
    loads = [
        pltpu.make_async_copy(one_ref, buf.at[pl.ds(0, split)], local_sem.at[0]),
        pltpu.make_async_copy(two_ref, buf.at[pl.ds(split, total - split)], local_sem.at[1]),
    ]
    for load in loads:
        load.start()
    lines[0] = small_ref[...]
    for load in loads:
        load.wait()
    pl.semaphore_wait(barrier, stages + 1)

    def ds(start, size):
        return pl.ds(pl.multiple_of(start, 16), size)

    def send(source, target, pair, bit):
        copy = pltpu.make_async_remote_copy(
            src_ref=source,
            dst_ref=target,
            send_sem=pair.at[0],
            recv_sem=pair.at[1],
            device_id=partner(bit),
            device_id_type=MESH,
        )
        copy.start()
        return copy

    line_bits = [core] + order_a

    def line_send(k):
        return send(lines.at[k], line_recv.at[k], line_sems.at[k], line_bits[k])

    def line_next(k, copy):
        copy.wait_recv()
        lines[k + 1] = lines[k] + line_recv[k]
        return copy

    sent = []
    mine = bit_value(core)
    copies = []
    for p in range(PARTS):
        other = (1 - mine) * (total // 2) + p * part
        copies.append(send(buf.at[ds(other, part)], core_recv.at[pl.ds(p * part, part)], core_sems.at[0, p], core))
    line = line_send(0)
    offsets = []
    for p in range(PARTS):
        copies[p].wait_recv()
        sent.append(copies[p])
        at = mine * (total // 2) + p * part
        offsets.append(at)
        buf[ds(at, part), :] = (
            buf[ds(at, part), :].astype(f32) + core_recv[p * part : (p + 1) * part, :].astype(f32)
        ).astype(bf16)
        copies[p] = None

    def halve(p, s):
        half = part >> (s + 1)
        bit = orders[p][s]
        value = bit_value(bit)
        base = part - (part >> s)
        copy = send(
            buf.at[ds(offsets[p] + (1 - value) * half, half)],
            recv.at[p, pl.ds(base, half)],
            sems.at[0, p, s],
            bit,
        )
        offsets[p] = offsets[p] + value * half
        return copy

    def settle(p, s, copy):
        half = part >> (s + 1)
        base = part - (part >> s)
        copy.wait_recv()
        sent.append(copy)
        rows_at = ds(offsets[p], half)
        total_now = buf[rows_at, :].astype(f32) + recv[p, base : base + half, :].astype(f32)
        return rows_at, total_now.astype(bf16)

    copies = [halve(p, 0) for p in range(PARTS)]
    line = line_next(0, line)
    sent.append(line)
    line = line_send(1)
    for s in range(1, stages):
        for p in range(PARTS):
            at, value = settle(p, s - 1, copies[p])
            buf[at, :] = value
            copies[p] = halve(p, s)
        line = line_next(s, line)
        sent.append(line)
        line = line_send(s + 1)

    def double(p, s):
        size = part >> (s + 1)
        bit = orders[p][s]
        at = ds(offsets[p], size)
        copy = send(full.at[at], full.at[at], sems.at[1, p, s], bit)
        offsets[p] = offsets[p] - bit_value(bit) * size
        return copy

    for p in range(PARTS):
        at, value = settle(p, stages - 1, copies[p])
        full[at, :] = value
        copies[p] = double(p, stages - 1)
    line = line_next(stages, line)
    sent.append(line)
    small_out_ref[...] = lines[stages + 1]
    for s in reversed(range(stages - 1)):
        for p in range(PARTS):
            copies[p].wait_recv()
            sent.append(copies[p])
            copies[p] = double(p, s)
    for p in range(PARTS):
        copies[p].wait_recv()
        sent.append(copies[p])
        at = ds(offsets[p], part)
        copies[p] = send(full.at[at], full.at[at], core_sems.at[1, p], core)
    for p in range(PARTS):
        copies[p].wait_recv()
        sent.append(copies[p])
    store = pltpu.make_async_copy(full, out_ref, local_sem.at[2])
    store.start()
    for copy in sent:
        copy.wait_send()
    store.wait()


def sum_everywhere(one, two, small):
    rows = lax.axis_size("rows")
    total, width = one.shape[0] + two.shape[0], one.shape[1]
    stages = len(bits_of(rows)[1])
    part = total // 2 // PARTS
    anywhere = pl.BlockSpec(memory_space=pl.ANY)
    vmem = pl.BlockSpec(memory_space=pltpu.VMEM)
    return pl.pallas_call(
        partial(reduce_kernel, rows),
        out_shape=[jax.ShapeDtypeStruct((total, width), bf16), jax.ShapeDtypeStruct(small.shape, f32)],
        in_specs=[anywhere, anywhere, vmem],
        out_specs=[anywhere, vmem],
        scratch_shapes=[
            pltpu.VMEM((total, width), bf16),
            pltpu.VMEM((total, width), bf16),
            pltpu.VMEM((total // 2, width), bf16),
            pltpu.VMEM((PARTS, part, width), bf16),
            pltpu.VMEM((stages + 2,) + small.shape, f32),
            pltpu.VMEM((stages + 1,) + small.shape, f32),
            pltpu.SemaphoreType.DMA((2, PARTS, stages, 2)),
            pltpu.SemaphoreType.DMA((2, PARTS, 2)),
            pltpu.SemaphoreType.DMA((stages + 1, 2)),
            pltpu.SemaphoreType.DMA((3,)),
        ],
        compiler_params=pltpu.CompilerParams(
            collective_id=0, has_side_effects=True, vmem_limit_bytes=40 * MIB
        ),
        cost_estimate=pl.CostEstimate(flops=total * width * 2, bytes_accessed=total * width * 4, transcendentals=0),
        name="sum_everywhere",
    )(one, two, small)


def place_kernel(me_ref, got_ref, _, out_ref):
    out_ref[...] = got_ref[...].astype(out_ref.dtype)


def put_in_place(me, got, target, place):
    width = got.shape[1]
    return call(
        place_kernel,
        "place_half",
        (place.phase,),
        [pl.BlockSpec((TILE, width), lambda t, me: (t, 0)), pl.BlockSpec(memory_space=pl.ANY)],
        pl.BlockSpec((TILE, width), lambda t, me: ((1 - me[0]) * place.phase + t, 0)),
        jax.ShapeDtypeStruct(target.shape, target.dtype),
        [],
        0,
        got.size * 6,
        32,
        aliases={2: 0},
    )(me, got, target)


def swap(value):
    return lax.ppermute(value, "seq", [(0, 1), (1, 0)])


def after(value, *others):
    return lax.optimization_barrier((value,) + others)[0]


def row_local(
    block_input, segment_ids, norm1_gain, norm1_shift, qkv_weight, qv_bias, proj_weight, proj_bias,
    norm2_gain, norm2_shift, fc_weight, fc_bias, out_weight, out_bias, out_cotangent,
):
    held, half_len, width = block_input.shape
    rows, length = held // 2, 2 * half_len
    tokens = rows * length
    place = Place(rows, half_len)
    side = lax.axis_index("seq").astype(jnp.int32)
    me = side[None]

    def outgoing(value, row):
        return lax.dynamic_index_in_dim(value, (1 - side) * rows + row, 0, keepdims=False)

    mine = lax.dynamic_slice_in_dim(segment_ids, side * rows, rows, 0)
    other = swap(lax.dynamic_slice_in_dim(segment_ids, (1 - side) * rows, rows, 0))
    x_parts = [swap(after(outgoing(block_input, 0), other))]

    segments = jnp.concatenate((jnp.where(side == 0, mine, other), jnp.where(side == 0, other, mine)), axis=1)
    slot = jnp.arange(length, dtype=jnp.int32)[None]
    ends = [jnp.sum((segments <= doc).astype(jnp.int32), axis=1, keepdims=True) for doc in range(2)]
    start = jnp.where(
        segments == 0, 0, jnp.where(segments == 1, ends[0], jnp.where(segments == 2, ends[1], slot))
    )
    low = start[:, ::BLOCK] // BLOCK
    blocks = length // BLOCK
    high = jnp.sum((low[:, None, :] <= jnp.arange(blocks)[None, :, None]).astype(jnp.int32), axis=2) - 1
    start = start[:, None, :]
    low = low.reshape(-1)
    high = high.reshape(-1)

    x = block_input.reshape(held * half_len, width)
    cot = out_cotangent.reshape(held * half_len, width)
    bias = jnp.concatenate((qv_bias[:width], jnp.zeros((width,), f32), qv_bias[width:]))[:, None]
    params = (norm1_gain[None], norm1_shift[None], jnp.transpose(qkv_weight), bias)
    qkv = project_qkv(me, x, params, place, 0, place.phase, False, (), ())
    attended = ()
    for row in range(rows):
        if row + 1 < rows:
            x_parts.append(swap(after(outgoing(block_input, row + 1), x_parts[row], qkv[0])))
        qkv = project_qkv(
            me, x_parts[row], params, place, place.phase + row * place.per, place.per, True, qkv, attended[:1]
        )
        attended = attend(low, start, *qkv, row, length, attended)
        if row + 2 == rows:
            cot_out = lax.dynamic_slice_in_dim(out_cotangent, (1 - side) * rows, rows, 0)
            cot_got = swap(after(cot_out, x_parts[row + 1], attended[1])).reshape(tokens // 2, width)
    att, lse = attended
    x_got = jnp.concatenate(x_parts, axis=0)

    y, y_sent, grad_middle, grad_att, delta, dfc, dout, dproj, small_two, dfcb = feed_forward(
        me, x, x_got, cot, cot_got, att, place, proj_weight, proj_bias, norm2_gain, norm2_shift, fc_weight, fc_bias,
        out_weight, out_bias
    )
    dfc, dout = lax.psum((dfc, dout), ("rows", "seq"))
    y_got = swap(y_sent)
    dq, dk, dv = attend_back(high, start, *qkv, grad_att, lse, delta, rows)
    dx, dx_sent, small_one = qkv_input_back(me, x, x_got, place, norm1_gain, qkv_weight, dq, dk, dv, grad_middle)
    dx_got = swap(dx_sent)
    dqkv, small_qv = qkv_weight_back(me, x, x_got, place, norm1_gain, norm1_shift, after(dq, dx_sent), dk, dv)
    small = jnp.sum(jnp.concatenate((small_two, small_one), axis=0).reshape(-1, 8, width), axis=1)
    small = jnp.concatenate(
        (small, jnp.sum(small_qv, axis=2), jnp.sum(dfcb, axis=0).reshape(-1, width)), axis=0
    )
    lines = small.shape[0]
    small = jnp.pad(small, ((0, -lines % 8), (0, 0)))
    late, small = sum_everywhere(dqkv, dproj, small)
    late = late.astype(f32)
    dqkv = jnp.concatenate([late[i * width : (i + 1) * width] for i in range(3)], axis=1)
    layer_output = put_in_place(me, y_got, y, place).reshape(held, half_len, width)
    input_grad = put_in_place(me, dx_got, dx, place).reshape(held, half_len, width)

    return (
        layer_output,
        input_grad,
        small[4],
        small[5],
        dqkv,
        small[6:8].reshape(-1),
        late[3 * width :],
        small[3],
        small[0],
        small[1],
        dfc.astype(f32),
        small[8:lines].reshape(-1),
        dout.astype(f32),
        small[2],
    )


def solution(mesh):
    rows_spec = P("rows", "seq", None)
    in_specs = (rows_spec, P("rows", "seq")) + (P(),) * 12 + (rows_spec,)
    out_specs = (rows_spec, rows_spec) + (P(),) * 12
    body = row_local if mesh.shape["seq"] == 2 else local
    return jax.shard_map(body, mesh=mesh, in_specs=in_specs, out_specs=out_specs, check_vma=False)
```

```python
from functools import partial, reduce

import jax
import jax.numpy as jnp
from jax import lax
from jax.experimental import pallas as pl
from jax.experimental.pallas import tpu as pltpu
from jax.sharding import PartitionSpec as P

HEADS = 12
HEAD_DIM = 64


BRANCH = 12 ** (-0.5)
EPSILON = 1e-05
PADDING = 3.0
NEGATIVE = -1e30
block_keys = 256


def layer_norm(values, scale_gain, shift_bias):
    center = values - jnp.mean(values, axis=-1, keepdims=True)
    variance = jnp.mean(center * center, axis=-1, keepdims=True)
    return center * lax.rsqrt(variance + EPSILON) * scale_gain + shift_bias


def allowed_pairs(query_segments, key_segments, query_slots, key_slots):
    same_doc = query_segments[:, :, None] == key_segments[:, None, :]
    causal = key_slots[None, None, :] <= query_slots[None, :, None]
    itself = key_slots[None, None, :] == query_slots[None, :, None]
    unpadded = key_segments[:, None, :] != PADDING
    return (same_doc & causal & (unpadded | itself))[:, None]


def split_heads(block_rows):
    return block_rows.reshape(block_rows.shape[0], block_rows.shape[1], HEADS, HEAD_DIM)


def fold_blocks(block_step, running, piece_tuple):
    piece_len = piece_tuple[0].shape[1]

    def one_block(block_index, held_state):
        offset = block_index * block_keys
        sub_tuple = tuple(
            (lax.dynamic_slice_in_dim(member, offset, block_keys, 1) for member in piece_tuple)
        )
        return block_step(held_state, sub_tuple, offset)

    return lax.fori_loop(0, piece_len // block_keys, one_block, running)


def keep_same(running):
    return running


def local(
    block_input,
    segment_ids,
    norm1_gain,
    norm1_shift,
    qkv_weight,
    qv_bias,
    proj_weight,
    proj_bias,
    norm2_gain,
    norm2_shift,
    fc_weight,
    fc_bias,
    out_weight,
    out_bias,
    out_cotangent,
):
    row_count, local_len, model_width = block_input.shape
    tokens = row_count * local_len
    full_len = local_len * lax.axis_size("seq")
    my_first = lax.axis_index("seq") * local_len
    query_slots = my_first + jnp.arange(local_len)
    my_segments = segment_ids.astype(jnp.bfloat16)
    my_seg_float = segment_ids.astype(jnp.float32)
    score_scale = HEAD_DIM ** (-0.5)
    inputs = block_input.astype(jnp.float32).reshape(tokens, model_width)
    normed_one = layer_norm(inputs, norm1_gain, norm1_shift).astype(jnp.bfloat16)
    mixed_qkv = jnp.dot(normed_one, qkv_weight, preferred_element_type=jnp.float32)
    query_flat = (
        (mixed_qkv[:, :model_width] + qv_bias[:model_width])
        .astype(jnp.bfloat16)
        .reshape(row_count, local_len, model_width)
    )
    key_rows = (
        mixed_qkv[:, model_width : 2 * model_width]
        .astype(jnp.bfloat16)
        .reshape(row_count, local_len, model_width)
    )
    value_rows = (
        (mixed_qkv[:, 2 * model_width :] + qv_bias[model_width:])
        .astype(jnp.bfloat16)
        .reshape(row_count, local_len, model_width)
    )
    queries = split_heads(query_flat)

    def attend_block(running, sub_tuple, first_slot):
        key_piece, value_piece, seg_piece = sub_tuple
        piece_len = key_piece.shape[1]
        key_slots = first_slot + jnp.arange(piece_len)
        seg_float = seg_piece.astype(jnp.float32)
        skipped = (first_slot > my_first + local_len - 1) | (
            jnp.max(seg_float) < jnp.min(my_seg_float)
        )

        def attend_update(state):
            running_max, running_sum, running_out = state
            scores = (
                jnp.einsum(
                    "rqhd,rkhd->rhqk",
                    queries,
                    split_heads(key_piece),
                    preferred_element_type=jnp.float32,
                )
                * score_scale
            )
            allowed = allowed_pairs(my_seg_float, seg_float, query_slots, key_slots)
            masked = jnp.where(allowed, scores, NEGATIVE)
            new_max = jnp.maximum(running_max, jnp.max(masked, axis=-1))
            prob_block = jnp.where(allowed, jnp.exp(scores - new_max[..., None]), 0.0)
            factor = jnp.exp(running_max - new_max)
            new_sum = running_sum * factor + jnp.sum(prob_block, axis=-1)
            added_part = jnp.einsum(
                "rhqk,rkhd->rqhd",
                prob_block.astype(jnp.bfloat16),
                split_heads(value_piece),
                preferred_element_type=jnp.float32,
            )
            new_out = running_out * jnp.transpose(factor, (0, 2, 1))[..., None] + added_part
            return (new_max, new_sum, new_out)

        return lax.cond(skipped, keep_same, attend_update, running)

    start_state = (
        jnp.full((row_count, HEADS, local_len), NEGATIVE, jnp.float32),
        jnp.zeros((row_count, HEADS, local_len), jnp.float32),
        jnp.zeros((row_count, local_len, HEADS, HEAD_DIM), jnp.float32),
    )
    running_max, running_sum, running_out = fold_blocks(
        attend_block,
        start_state,
        (
            lax.all_gather(key_rows, "seq", axis=1, tiled=True),
            lax.all_gather(value_rows, "seq", axis=1, tiled=True),
            lax.all_gather(my_segments, "seq", axis=1, tiled=True),
        ),
    )
    log_total = running_max + jnp.log(running_sum)
    attended_heads = running_out / jnp.transpose(running_sum, (0, 2, 1))[..., None]
    attended_low = attended_heads.reshape(tokens, model_width).astype(jnp.bfloat16)
    branch_one = jnp.dot(attended_low, proj_weight, preferred_element_type=jnp.float32) + proj_bias
    middle = inputs + BRANCH * branch_one
    normed_two = layer_norm(middle, norm2_gain, norm2_shift).astype(jnp.bfloat16)
    hidden_pre = jnp.dot(normed_two, fc_weight, preferred_element_type=jnp.float32) + fc_bias
    hidden_act = jax.nn.gelu(hidden_pre, approximate=True).astype(jnp.bfloat16)
    branch_two = jnp.dot(hidden_act, out_weight, preferred_element_type=jnp.float32) + out_bias
    layer_output = (
        (middle + BRANCH * branch_two)
        .astype(jnp.bfloat16)
        .reshape(row_count, local_len, model_width)
    )
    flat_cot = out_cotangent.reshape(tokens, model_width).astype(jnp.float32)
    grad_two = (BRANCH * flat_cot).astype(jnp.bfloat16)
    grad_out_weight = jnp.einsum(
        "tf,td->fd", hidden_act, grad_two, preferred_element_type=jnp.float32
    )
    grad_out_bias = jnp.sum(grad_two.astype(jnp.float32), axis=0)
    grad_act = jnp.einsum("td,fd->tf", grad_two, out_weight, preferred_element_type=jnp.float32)
    gelu_value, gelu_pull = jax.vjp(partial(jax.nn.gelu, approximate=True), hidden_pre)
    grad_pre = gelu_pull(grad_act)[0].astype(jnp.bfloat16)
    grad_fc_weight = jnp.einsum(
        "td,tf->df", normed_two, grad_pre, preferred_element_type=jnp.float32
    )
    grad_fc_bias = jnp.sum(grad_pre.astype(jnp.float32), axis=0)
    grad_normed_two = jnp.einsum(
        "tf,df->td", grad_pre, fc_weight, preferred_element_type=jnp.float32
    )
    norm_value, norm_pull = jax.vjp(layer_norm, middle, norm2_gain, norm2_shift)
    grad_inner, grad_norm2_gain, grad_norm2_shift = norm_pull(grad_normed_two)
    grad_middle = flat_cot + grad_inner
    grad_one = (BRANCH * grad_middle).astype(jnp.bfloat16)
    grad_proj_weight = jnp.einsum(
        "td,te->de", attended_low, grad_one, preferred_element_type=jnp.float32
    )
    grad_proj_bias = jnp.sum(grad_one.astype(jnp.float32), axis=0)
    grad_attended_flat = (
        jnp.einsum("te,de->td", grad_one, proj_weight, preferred_element_type=jnp.float32)
        .astype(jnp.bfloat16)
        .reshape(row_count, local_len, model_width)
    )
    grad_attended = split_heads(grad_attended_flat)
    grad_delta = jnp.einsum("rqhd,rqhd->rhq", grad_attended.astype(jnp.float32), attended_heads)

    def back_block(running, sub_tuple, first_slot):
        key_piece, value_piece, seg_piece = sub_tuple
        piece_len = key_piece.shape[1]
        key_slots = first_slot + jnp.arange(piece_len)
        seg_float = seg_piece.astype(jnp.float32)
        skipped = (first_slot > my_first + local_len - 1) | (
            jnp.max(seg_float) < jnp.min(my_seg_float)
        )

        def back_update(state):
            grad_query, grad_full = state
            key_heads = split_heads(key_piece)
            value_heads = split_heads(value_piece)
            scores = (
                jnp.einsum(
                    "rqhd,rkhd->rhqk", queries, key_heads, preferred_element_type=jnp.float32
                )
                * score_scale
            )
            allowed = allowed_pairs(my_seg_float, seg_float, query_slots, key_slots)
            prob_block = jnp.where(allowed, jnp.exp(scores - log_total[..., None]), 0.0)
            grad_probs = jnp.einsum(
                "rqhd,rkhd->rhqk", grad_attended, value_heads, preferred_element_type=jnp.float32
            )
            grad_scores = (score_scale * prob_block * (grad_probs - grad_delta[..., None])).astype(
                jnp.bfloat16
            )
            new_query = grad_query + jnp.einsum(
                "rhqk,rkhd->rqhd", grad_scores, key_heads, preferred_element_type=jnp.float32
            )
            grad_keys = jnp.einsum(
                "rhqk,rqhd->rkhd", grad_scores, queries, preferred_element_type=jnp.float32
            ).reshape(row_count, piece_len, model_width)
            grad_values = jnp.einsum(
                "rhqk,rqhd->rkhd",
                prob_block.astype(jnp.bfloat16),
                grad_attended,
                preferred_element_type=jnp.float32,
            ).reshape(row_count, piece_len, model_width)
            held_part = lax.dynamic_slice_in_dim(grad_full, first_slot, piece_len, 2)
            new_full = lax.dynamic_update_slice_in_dim(
                grad_full, held_part + jnp.stack((grad_keys, grad_values)), first_slot, 2
            )
            return (new_query, new_full)

        return lax.cond(skipped, keep_same, back_update, running)

    back_start = (
        jnp.zeros((row_count, local_len, HEADS, HEAD_DIM), jnp.float32),
        jnp.zeros((2, row_count, full_len, model_width), jnp.float32),
    )
    grad_query, grad_full = fold_blocks(
        back_block,
        back_start,
        (
            lax.all_gather(key_rows, "seq", axis=1, tiled=True),
            lax.all_gather(value_rows, "seq", axis=1, tiled=True),
            lax.all_gather(my_segments, "seq", axis=1, tiled=True),
        ),
    )
    grad_pairs = lax.psum_scatter(
        grad_full.astype(jnp.bfloat16), "seq", scatter_dimension=2, tiled=True
    ).astype(jnp.float32)
    grad_query_low = grad_query.reshape(row_count, local_len, model_width).astype(jnp.bfloat16)
    grad_key_low = grad_pairs[0].astype(jnp.bfloat16)
    grad_value_low = grad_pairs[1].astype(jnp.bfloat16)
    grad_qkv_low = jnp.concatenate((grad_query_low, grad_key_low, grad_value_low), axis=-1).reshape(
        tokens, 3 * model_width
    )
    grad_qkv_weight = jnp.einsum(
        "td,te->de", normed_one, grad_qkv_low, preferred_element_type=jnp.float32
    )
    grad_qv_bias = jnp.concatenate(
        (
            jnp.sum(grad_query_low.astype(jnp.float32), axis=(0, 1)),
            jnp.sum(grad_value_low.astype(jnp.float32), axis=(0, 1)),
        )
    )
    grad_normed_one = jnp.einsum(
        "te,de->td", grad_qkv_low, qkv_weight, preferred_element_type=jnp.float32
    )
    first_value, first_pull = jax.vjp(layer_norm, inputs, norm1_gain, norm1_shift)
    grad_first, grad_norm1_gain, grad_norm1_shift = first_pull(grad_normed_one)
    input_grad = (grad_middle + grad_first).reshape(row_count, local_len, model_width)
    local_grads = (
        grad_norm1_gain,
        grad_norm1_shift,
        grad_qkv_weight,
        grad_qv_bias,
        grad_proj_weight,
        grad_proj_bias,
        grad_norm2_gain,
        grad_norm2_shift,
        grad_fc_weight,
        grad_fc_bias,
        grad_out_weight,
        grad_out_bias,
    )
    shares = (
        lax.psum_scatter(
            local_grads[0].astype(jnp.bfloat16), "rows", scatter_dimension=0, tiled=True
        ).astype(jnp.float32),
        lax.psum_scatter(
            local_grads[1].astype(jnp.bfloat16), "rows", scatter_dimension=0, tiled=True
        ).astype(jnp.float32),
        lax.psum_scatter(
            local_grads[2].astype(jnp.bfloat16), "rows", scatter_dimension=0, tiled=True
        ).astype(jnp.float32),
        lax.psum_scatter(
            local_grads[3].astype(jnp.bfloat16), "rows", scatter_dimension=0, tiled=True
        ).astype(jnp.float32),
        lax.psum_scatter(
            local_grads[4].astype(jnp.bfloat16), "rows", scatter_dimension=0, tiled=True
        ).astype(jnp.float32),
        lax.psum_scatter(
            local_grads[5].astype(jnp.bfloat16), "rows", scatter_dimension=0, tiled=True
        ).astype(jnp.float32),
        lax.psum_scatter(
            local_grads[6].astype(jnp.bfloat16), "rows", scatter_dimension=0, tiled=True
        ).astype(jnp.float32),
        lax.psum_scatter(
            local_grads[7].astype(jnp.bfloat16), "rows", scatter_dimension=0, tiled=True
        ).astype(jnp.float32),
        lax.psum_scatter(
            local_grads[8].astype(jnp.bfloat16), "rows", scatter_dimension=0, tiled=True
        ).astype(jnp.float32),
        lax.psum_scatter(
            local_grads[9].astype(jnp.bfloat16), "rows", scatter_dimension=0, tiled=True
        ).astype(jnp.float32),
        lax.psum_scatter(
            local_grads[10].astype(jnp.bfloat16), "rows", scatter_dimension=0, tiled=True
        ).astype(jnp.float32),
        lax.psum_scatter(
            local_grads[11].astype(jnp.bfloat16), "rows", scatter_dimension=0, tiled=True
        ).astype(jnp.float32),
    )
    shares = (
        lax.psum(shares[0].astype(jnp.bfloat16), "seq").astype(jnp.float32),
        lax.psum(shares[1].astype(jnp.bfloat16), "seq").astype(jnp.float32),
        lax.psum(shares[2].astype(jnp.bfloat16), "seq").astype(jnp.float32),
        lax.psum(shares[3].astype(jnp.bfloat16), "seq").astype(jnp.float32),
        lax.psum(shares[4].astype(jnp.bfloat16), "seq").astype(jnp.float32),
        lax.psum(shares[5].astype(jnp.bfloat16), "seq").astype(jnp.float32),
        lax.psum(shares[6].astype(jnp.bfloat16), "seq").astype(jnp.float32),
        lax.psum(shares[7].astype(jnp.bfloat16), "seq").astype(jnp.float32),
        lax.psum(shares[8].astype(jnp.bfloat16), "seq").astype(jnp.float32),
        lax.psum(shares[9].astype(jnp.bfloat16), "seq").astype(jnp.float32),
        lax.psum(shares[10].astype(jnp.bfloat16), "seq").astype(jnp.float32),
        lax.psum(shares[11].astype(jnp.bfloat16), "seq").astype(jnp.float32),
    )
    totals = (
        lax.all_gather(shares[0].astype(jnp.bfloat16), "rows", axis=0, tiled=True).astype(
            jnp.float32
        ),
        lax.all_gather(shares[1].astype(jnp.bfloat16), "rows", axis=0, tiled=True).astype(
            jnp.float32
        ),
        lax.all_gather(shares[2].astype(jnp.bfloat16), "rows", axis=0, tiled=True).astype(
            jnp.float32
        ),
        lax.all_gather(shares[3].astype(jnp.bfloat16), "rows", axis=0, tiled=True).astype(
            jnp.float32
        ),
        lax.all_gather(shares[4].astype(jnp.bfloat16), "rows", axis=0, tiled=True).astype(
            jnp.float32
        ),
        lax.all_gather(shares[5].astype(jnp.bfloat16), "rows", axis=0, tiled=True).astype(
            jnp.float32
        ),
        lax.all_gather(shares[6].astype(jnp.bfloat16), "rows", axis=0, tiled=True).astype(
            jnp.float32
        ),
        lax.all_gather(shares[7].astype(jnp.bfloat16), "rows", axis=0, tiled=True).astype(
            jnp.float32
        ),
        lax.all_gather(shares[8].astype(jnp.bfloat16), "rows", axis=0, tiled=True).astype(
            jnp.float32
        ),
        lax.all_gather(shares[9].astype(jnp.bfloat16), "rows", axis=0, tiled=True).astype(
            jnp.float32
        ),
        lax.all_gather(shares[10].astype(jnp.bfloat16), "rows", axis=0, tiled=True).astype(
            jnp.float32
        ),
        lax.all_gather(shares[11].astype(jnp.bfloat16), "rows", axis=0, tiled=True).astype(
            jnp.float32
        ),
    )
    return (layer_output, input_grad) + tuple(totals)


MIB = 1 << 20
LOG2E = 1.4426950408889634
GELU_C = 0.7978845608028654
GELU_A = 0.044715
BLOCK = 256
f32 = jnp.float32
bf16 = jnp.bfloat16


def dot_nn(a, b):
    return lax.dot_general(a, b, (((1,), (0,)), ((), ())), preferred_element_type=f32)


def dot_tn(a, b):
    return lax.dot_general(a, b, (((0,), (0,)), ((), ())), preferred_element_type=f32)


def dot_nt(a, b):
    return lax.dot_general(a, b, (((1,), (1,)), ((), ())), preferred_element_type=f32)


def norm_parts(values):
    center = values - jnp.mean(values, axis=-1, keepdims=True)
    variance = jnp.mean(center * center, axis=-1, keepdims=True)
    inverse = lax.rsqrt(variance + EPSILON)
    return center * inverse, inverse


def row_sums(values):
    rows, cols = values.shape
    return jnp.sum(values.reshape(rows // 8, 8, cols), axis=0)


def whole(shape):
    return pl.BlockSpec(shape, lambda *_: (0,) * len(shape), pipeline_mode=pl.Buffered(1))


def call(
    kernel, name, grid, in_specs, out_specs, out_shape, scratch, flops, moved, vmem, prefetch=1, aliases=None
):
    return pl.pallas_call(
        kernel,
        out_shape=out_shape,
        grid_spec=pltpu.PrefetchScalarGridSpec(
            num_scalar_prefetch=prefetch,
            grid=grid,
            in_specs=in_specs,
            out_specs=out_specs,
            scratch_shapes=scratch,
        ),
        compiler_params=pltpu.CompilerParams(vmem_limit_bytes=vmem * MIB),
        cost_estimate=pl.CostEstimate(flops=flops, bytes_accessed=moved, transcendentals=0),
        input_output_aliases=aliases or {},
        name=name,
    )


TILE = 512
LIMIT = 2.0**100


class Place:
    def __init__(self, rows, half_len):
        self.rows, self.per = rows, half_len // TILE
        self.phase = rows * self.per
        self.steps = 2 * self.phase

    def own(self, t, me):
        return me[0] * self.phase + jnp.minimum(t, self.phase - 1), 0

    def got(self, t, me):
        return jnp.maximum(t - self.phase, 0), 0

    def slot(self, t, me):
        late = t // self.phase
        half = jnp.where(late == 0, me[0], 1 - me[0])
        at = t - late * self.phase
        return (at // self.per) * 2 * self.per + half * self.per + at % self.per

    def turned(self, t, me):
        return 0, self.slot(t, me)

    def back(self, t, me):
        return (1 - me[0]) * self.phase + t, 0


def either(step, phase, own_ref, got_ref):
    return jnp.where(step < phase, own_ref[...], got_ref[...])


def qkv_kernel(me_ref, x_ref, gain_ref, shift_ref, w_ref, bias_ref, *refs):
    width = x_ref.shape[1]
    hat, _ = norm_parts(x_ref[...].astype(f32))
    normed = (hat * gain_ref[...] + shift_ref[...]).astype(bf16)
    for i, ref in enumerate(refs[-3:]):
        part = dot_nt(w_ref[i * width : (i + 1) * width, :], normed)
        if i != 1:
            part = part + bias_ref[i * width : (i + 1) * width, :]
        ref[...] = part.astype(bf16)


def project_qkv(me, x, params, place, first, count, got, earlier, after):
    width = x.shape[1]
    tokens = place.steps * TILE
    index = (lambda t, me: (t, 0)) if got else (lambda t, me: place.own(t + first, me))
    turned = pl.BlockSpec((width, TILE), lambda t, me: place.turned(t + first, me))
    anywhere = pl.BlockSpec(memory_space=pl.ANY)
    extra = list(earlier) + list(after)
    return call(
        qkv_kernel,
        "qkv_forward",
        (count,),
        [pl.BlockSpec((TILE, width), index)]
        + [whole(p.shape) for p in params]
        + [anywhere] * len(extra),
        [turned] * 3,
        [jax.ShapeDtypeStruct((width, tokens), bf16)] * 3,
        [],
        2 * count * TILE * width * 3 * width,
        count * TILE * width * 8 + width * width * 6,
        60,
        aliases={6 + i: i for i in range(len(earlier))},
    )(me, x, *params, *extra)


def attend_kernel(low_ref, start_ref, qt_ref, kt_ref, vt_ref, *refs, row, first, blocks):
    att_ref, lse_ref, acc, base, bias = refs[-5:]
    width, length = qt_ref.shape
    heads = width // HEAD_DIM
    pad = HEAD_DIM + 16
    scale = HEAD_DIM**-0.5 * LOG2E
    slots = lax.broadcasted_iota(jnp.int32, (BLOCK, BLOCK), 0)
    query_iota = lax.broadcasted_iota(jnp.int32, (BLOCK, BLOCK), 1)
    ones = jnp.ones((16, BLOCK), bf16)

    def at(i):
        return pl.ds(pl.multiple_of(i * BLOCK, BLOCK), BLOCK)

    def head_rows(h):
        return slice(h * HEAD_DIM, (h + 1) * HEAD_DIM)

    def acc_rows(h):
        return slice(h * pad, (h + 1) * pad)

    def total(h):
        return acc[h * pad + HEAD_DIM : h * pad + HEAD_DIM + 1, :]

    def score(h, qb, kb):
        return dot_tn(kt_ref[head_rows(h), at(kb)], qt_ref[head_rows(h), at(qb - first)])

    def weigh(h, kb, probs):
        return dot_nn(jnp.concatenate((vt_ref[head_rows(h), at(kb)], ones), axis=0), probs)

    def set_bias(qb, kb):
        allowed = (slots >= start_ref[0, :, at(qb - first)] - kb * BLOCK) & (
            slots + (kb - qb) * BLOCK <= query_iota
        )
        bias[...] = jnp.where(allowed, 0.0, NEGATIVE)

    def query_block(qb, carry):
        low = low_ref[row * blocks + qb]
        for h in range(heads):
            own = qt_ref[head_rows(h), at(qb - first)].astype(f32) * kt_ref[head_rows(h), at(qb)].astype(f32)
            base[h : h + 1, :] = jnp.sum(own, axis=0, keepdims=True) * scale
        acc[...] = jnp.zeros_like(acc)

        def fast(kb, carry):
            set_bias(qb, kb)

            def finish(h, probs):
                acc[acc_rows(h), :] += weigh(h, kb, probs)

            ahead = [score(h, qb, kb) for h in range(min(3, heads))]
            waiting = []
            for h in range(heads):
                scores = ahead.pop(0)
                if h + 3 < heads:
                    ahead.append(score(h + 3, qb, kb))
                probs = jnp.exp2(scores * scale + (bias[...] - base[h : h + 1, :]))
                waiting.append((h, probs.astype(bf16)))
                if len(waiting) > 1:
                    finish(*waiting.pop(0))
            finish(*waiting[0])
            return carry

        lax.fori_loop(low, qb + 1, fast, 0)
        largest = reduce(jnp.maximum, [total(h) for h in range(heads)])

        @pl.when(jnp.logical_not(jnp.max(largest) < LIMIT))
        def _():
            base[...] = jnp.full_like(base, NEGATIVE)
            acc[...] = jnp.zeros_like(acc)

            def safe(kb, carry):
                set_bias(qb, kb)
                for h in range(heads):
                    scores = score(h, qb, kb) * scale + bias[...]
                    old = base[h : h + 1, :]
                    top = jnp.maximum(old, jnp.max(scores, axis=0, keepdims=True))
                    base[h : h + 1, :] = top
                    probs = jnp.exp2(scores - top).astype(bf16)
                    acc[acc_rows(h), :] = acc[acc_rows(h), :] * jnp.exp2(old - top) + weigh(h, kb, probs)
                return carry

            lax.fori_loop(low, qb + 1, safe, 0)

        for h in range(heads):
            out = acc[h * pad : h * pad + HEAD_DIM, :]
            att_ref[head_rows(h), at(qb - first)] = (out / total(h)).astype(bf16)
            lse_ref[h // 2, h % 2 : h % 2 + 1, at(qb - first)] = base[h : h + 1, :] + jnp.log2(total(h))
        return carry

    lax.fori_loop(first, first + length // BLOCK, query_block, 0)


def attend(low, start, qt, kt, vt, row, length, part, parts, earlier):
    width, tokens = qt.shape
    heads = width // HEAD_DIM
    span = length // parts
    seen = span * (part + 1)
    column = row * parts + part
    queries = pl.BlockSpec((width, span), lambda i, low: (0, column))
    keys = pl.BlockSpec((width, seen), lambda i, low: (0, row * length // seen))
    lined = pl.BlockSpec((heads // 2, 2, span), lambda i, low: (0, 0, column))
    return call(
        partial(attend_kernel, row=row, first=part * span // BLOCK, blocks=length // BLOCK),
        "attention_forward",
        (1,),
        [pl.BlockSpec((1, 1, span), lambda i, low: (row, 0, part)), queries, keys, keys]
        + [pl.BlockSpec(memory_space=pl.ANY)] * len(earlier),
        [queries, lined],
        [
            jax.ShapeDtypeStruct((width, tokens), bf16),
            jax.ShapeDtypeStruct((heads // 2, 2, tokens), f32),
        ],
        [
            pltpu.VMEM((heads * (HEAD_DIM + 16), BLOCK), f32),
            pltpu.VMEM((16, BLOCK), f32),
            pltpu.VMEM((BLOCK, BLOCK), f32),
        ],
        2 * span * seen * width,
        length * width * 8,
        60,
        aliases={5 + i: i for i in range(len(earlier))},
    )(low, start, qt, kt, vt, *earlier)


def attend_back_kernel(
    high_ref, start_ref, qt_ref, kt_ref, vt_ref, dot_ref, lse_ref, delta_ref,
    dqt_ref, dkt_ref, dvt_ref, dq, dk, dv, bias,
):
    row = pl.program_id(0)
    width, length = qt_ref.shape
    heads = width // HEAD_DIM
    blocks = length // BLOCK
    scale = HEAD_DIM**-0.5 * LOG2E
    slots = lax.broadcasted_iota(jnp.int32, (BLOCK, BLOCK), 0)
    query_iota = lax.broadcasted_iota(jnp.int32, (BLOCK, BLOCK), 1)
    dq[...] = jnp.zeros_like(dq)

    def at(i):
        return pl.ds(pl.multiple_of(i * BLOCK, BLOCK), BLOCK)

    def key_block(kb, carry):
        k_at = at(kb)

        def visit(qb, first):
            q_at = at(qb)
            allowed = slots >= start_ref[0, :, q_at] - kb * BLOCK
            if first:
                allowed = allowed & (slots <= query_iota)
            bias[...] = jnp.where(allowed, 0.0, NEGATIVE)

            def begin(h):
                rows = slice(h * HEAD_DIM, (h + 1) * HEAD_DIM)
                return (
                    dot_tn(kt_ref[rows, k_at], qt_ref[rows, q_at]),
                    dot_tn(vt_ref[rows, k_at], dot_ref[rows, q_at]),
                )

            def finish(h, probs, grad_scores):
                rows = slice(h * HEAD_DIM, (h + 1) * HEAD_DIM)
                dv_new = dot_nt(dot_ref[rows, q_at], probs)
                dk_new = dot_nt(qt_ref[rows, q_at], grad_scores)
                dv[rows, :] = dv_new if first else dv[rows, :] + dv_new
                dk[rows, :] = dk_new if first else dk[rows, :] + dk_new
                dq[rows, q_at] += dot_nn(kt_ref[rows, k_at], grad_scores)

            ahead = [begin(0)]
            waiting = []
            for h in range(heads):
                scores, grad_probs = ahead.pop(0)
                if h + 1 < heads:
                    ahead.append(begin(h + 1))
                line = (h // 2, slice(h % 2, h % 2 + 1), q_at)
                probs = jnp.exp2(scores * scale + (bias[...] - lse_ref[line]))
                grad_scores = (probs * (grad_probs - delta_ref[line])).astype(bf16)
                waiting.append((h, probs.astype(bf16), grad_scores))
                if len(waiting) > 1:
                    finish(*waiting.pop(0))
            finish(*waiting[0])

        visit(kb, True)

        def later(qb, carry):
            visit(qb, False)
            return carry

        lax.fori_loop(kb + 1, high_ref[row * blocks + kb] + 1, later, 0)
        dkt_ref[:, k_at] = (dk[...] * HEAD_DIM**-0.5).astype(bf16)
        dvt_ref[:, k_at] = dv[...].astype(bf16)
        return carry

    lax.fori_loop(0, blocks, key_block, 0)
    dqt_ref[...] = (dq[...] * HEAD_DIM**-0.5).astype(bf16)


def attend_back(high, start, qt, kt, vt, dot, lse, delta, rows):
    width, tokens = qt.shape
    length = tokens // rows
    heads = width // HEAD_DIM
    turned = pl.BlockSpec((width, length), lambda r, high: (0, r))
    lined = pl.BlockSpec((heads // 2, 2, length), lambda r, high: (0, 0, r))
    return call(
        attend_back_kernel,
        "attention_backward",
        (rows,),
        [pl.BlockSpec((1, 1, length), lambda r, high: (r, 0, 0)), turned, turned, turned, turned, lined, lined],
        [turned] * 3,
        [jax.ShapeDtypeStruct((width, tokens), bf16)] * 3,
        [
            pltpu.VMEM((width, length), f32),
            pltpu.VMEM((width, BLOCK), f32),
            pltpu.VMEM((width, BLOCK), f32),
            pltpu.VMEM((BLOCK, BLOCK), f32),
        ],
        5 * tokens * length * width,
        tokens * width * 14,
        62,
    )(high, start, qt, kt, vt, dot, lse, delta)


def mlp_kernel(
    me_ref, x_ref, xg_ref, cot_ref, cotg_ref, att_ref, proj_ref, projb_ref, gain_ref, shift_ref, fc_ref, fcb_ref,
    out_ref, outb_ref,
    kept_ref, sent_ref, gm_ref, do_ref, delta_ref, dfc_ref, dout_ref, dproj_ref, small_ref, dfcb_ref,
    dfc, doutt, dproj, sums, dfcb, stage, sem,
):
    step = pl.program_id(0)
    steps = pl.num_programs(0)
    phase = steps // 2
    tile, width = x_ref.shape
    hidden = fc_ref.shape[1]
    chunk = 768

    @pl.when(step == 0)
    def _():
        dfc[...] = jnp.zeros_like(dfc)
        doutt[...] = jnp.zeros_like(doutt)
        dproj[...] = jnp.zeros_like(dproj)
        sums[...] = jnp.zeros_like(sums)
        dfcb[...] = jnp.zeros_like(dfcb)

    att_t = att_ref[...]
    x = either(step, phase, x_ref, xg_ref).astype(f32)
    middle = x + BRANCH * (dot_tn(att_t, proj_ref[...]) + projb_ref[...])
    hat, inverse = norm_parts(middle)
    normed = (hat * gain_ref[...] + shift_ref[...]).astype(bf16)
    normed_t = jnp.transpose(normed)
    cot = either(step, phase, cot_ref, cotg_ref).astype(f32)
    grad_two = (BRANCH * cot).astype(bf16)
    grad_two_t = jnp.transpose(grad_two)
    branch = jnp.zeros((tile, width), f32)
    grad_normed = jnp.zeros((tile, width), f32)
    for at in range(0, hidden, chunk):
        cols = slice(at, at + chunk)
        pre = dot_nn(normed, fc_ref[:, cols]) + fcb_ref[:, cols]
        grad_act = dot_nt(grad_two, out_ref[cols, :])
        square = pre * pre
        half = 0.5 + 0.5 * jnp.tanh(pre * (GELU_C + GELU_C * GELU_A * square))
        act = pre * half
        slope = half + act * (1.0 - half) * (2.0 * GELU_C + 6.0 * GELU_C * GELU_A * square)
        act = act.astype(bf16)
        grad_pre = (grad_act * slope).astype(bf16)
        branch += dot_nn(act, out_ref[cols, :])
        grad_normed += dot_nt(grad_pre, fc_ref[:, cols])
        dfc[:, cols] += dot_nn(normed_t, grad_pre)
        doutt[:, cols] += dot_nn(grad_two_t, act)
        dfcb[:, cols] += row_sums(grad_pre.astype(f32))
    y = (middle + BRANCH * (branch + outb_ref[...])).astype(bf16)

    @pl.when(step < phase)
    def _():
        kept_ref[...] = y

    @pl.when(step >= phase)
    def _():
        sent_ref[...] = y

    scaled = grad_normed * gain_ref[...]
    mean_one = jnp.mean(scaled, axis=-1, keepdims=True)
    mean_two = jnp.mean(scaled * hat, axis=-1, keepdims=True)
    grad_middle = cot + inverse * (scaled - mean_one - hat * mean_two)
    gm_ref[...] = grad_middle.astype(bf16)
    grad_one = (BRANCH * grad_middle).astype(bf16)
    dproj[...] += dot_nn(att_t, grad_one)
    grad_att = dot_nt(proj_ref[...], grad_one).astype(bf16)
    do_ref[...] = grad_att
    product = grad_att.astype(f32) * att_t.astype(f32)
    for h in range(width // HEAD_DIM):
        part = product[h * HEAD_DIM : (h + 1) * HEAD_DIM, :]
        delta_ref[h // 2, h % 2 : h % 2 + 1, :] = jnp.sum(part, axis=0, keepdims=True)
    sums[0:8, :] += row_sums(grad_normed * hat)
    sums[8:16, :] += row_sums(grad_normed)
    sums[16:24, :] += row_sums(grad_two.astype(f32))
    sums[24:32, :] += row_sums(grad_one.astype(f32))

    @pl.when(step == steps - 1)
    def _():
        for at in range(0, hidden, chunk):
            cols = slice(at, at + chunk)
            stage[...] = dfc[:, cols].astype(bf16)
            copy = pltpu.make_async_copy(stage, dfc_ref.at[:, cols], sem)
            copy.start()
            copy.wait()
            stage[...] = jnp.transpose(doutt[:, cols].astype(bf16))
            copy = pltpu.make_async_copy(stage, dout_ref.at[cols, :], sem)
            copy.start()
            copy.wait()
        dproj_ref[...] = dproj[...].astype(bf16)
        small_ref[...] = sums[...]
        dfcb_ref[...] = dfcb[...]


def feed_forward(
    me, x, x_got, cot, cot_got, att, place, proj_weight, proj_bias, gain, shift, fc_weight, fc_bias, out_weight, out_bias
):
    width, tokens = att.shape
    hidden = fc_weight.shape[1]
    heads = width // HEAD_DIM
    own = pl.BlockSpec((TILE, width), place.own)
    got = pl.BlockSpec((TILE, width), place.got)
    turned = pl.BlockSpec((width, TILE), place.turned)
    plain = pl.BlockSpec((TILE, width), lambda t, me: (t, 0))
    anywhere = pl.BlockSpec(memory_space=pl.ANY)
    return call(
        mlp_kernel,
        "feed_forward",
        (place.steps,),
        [own, got, own, got, turned, whole((width, width)), whole((1, width)), whole((1, width)), whole((1, width)),
         whole(fc_weight.shape), whole((1, hidden)), whole(out_weight.shape), whole((1, width))],
        [own, got, plain, turned,
         pl.BlockSpec((heads // 2, 2, TILE), lambda t, me: (0, 0, place.slot(t, me))),
         anywhere, anywhere, whole((width, width)), whole((32, width)), whole((8, hidden))],
        [
            jax.ShapeDtypeStruct((tokens, width), bf16),
            jax.ShapeDtypeStruct((tokens // 2, width), bf16),
            jax.ShapeDtypeStruct((tokens, width), bf16),
            jax.ShapeDtypeStruct((width, tokens), bf16),
            jax.ShapeDtypeStruct((heads // 2, 2, tokens), f32),
            jax.ShapeDtypeStruct((width, hidden), bf16),
            jax.ShapeDtypeStruct((hidden, width), bf16),
            jax.ShapeDtypeStruct((width, width), bf16),
            jax.ShapeDtypeStruct((32, width), f32),
            jax.ShapeDtypeStruct((8, hidden), f32),
        ],
        [
            pltpu.VMEM((width, hidden), f32),
            pltpu.VMEM((width, hidden), f32),
            pltpu.VMEM((width, width), f32),
            pltpu.VMEM((32, width), f32),
            pltpu.VMEM((8, hidden), f32),
            pltpu.VMEM((width, width), bf16),
            pltpu.SemaphoreType.DMA,
        ],
        2 * tokens * width * (3 * width + 6 * hidden),
        tokens * width * 14,
        63,
    )(me, x, x_got, cot, cot_got, att, proj_weight, proj_bias[None], gain[None], shift[None], fc_weight, fc_bias[None],
      out_weight, out_bias[None])


def qkv_back_kernel(
    me_ref, x_ref, xg_ref, gain_ref, shift_ref, w_ref, dq_ref, dk_ref, dv_ref, gm_ref,
    kept_ref, sent_ref, dw_ref, small_ref, bias_ref, acc, sums, bias_sums,
):
    step = pl.program_id(0)
    steps = pl.num_programs(0)
    width = x_ref.shape[1]
    refs = (dq_ref, dk_ref, dv_ref)

    @pl.when(step == 0)
    def _():
        acc[...] = jnp.zeros_like(acc)
        sums[...] = jnp.zeros_like(sums)
        bias_sums[...] = jnp.zeros_like(bias_sums)

    hat, inverse = norm_parts(either(step, steps // 2, x_ref, xg_ref).astype(f32))
    normed_t = jnp.transpose((hat * gain_ref[...] + shift_ref[...]).astype(bf16))
    grad_t = sum(dot_nn(w_ref[:, i * width : (i + 1) * width], ref[...]) for i, ref in enumerate(refs))
    for i, ref in enumerate(refs):
        acc[i * width : (i + 1) * width, :] += dot_nt(normed_t, ref[...])
    grad_normed = jnp.transpose(grad_t)
    scaled = grad_normed * gain_ref[...]
    mean_one = jnp.mean(scaled, axis=-1, keepdims=True)
    mean_two = jnp.mean(scaled * hat, axis=-1, keepdims=True)
    grad_x = gm_ref[...].astype(f32) + inverse * (scaled - mean_one - hat * mean_two)
    sums[0:8, :] += row_sums(grad_normed * hat)
    sums[8:16, :] += row_sums(grad_normed)
    for i, ref in enumerate((dq_ref, dv_ref)):
        part = ref[...].astype(f32)
        bias_sums[i] += sum(part[:, j : j + 128] for j in range(0, part.shape[1], 128))

    @pl.when(step < steps // 2)
    def _():
        kept_ref[...] = grad_x

    @pl.when(step >= steps // 2)
    def _():
        sent_ref[...] = grad_x.astype(bf16)

    @pl.when(step == steps - 1)
    def _():
        dw_ref[...] = acc[...].astype(bf16)
        small_ref[...] = sums[...]
        bias_ref[...] = bias_sums[...]


def qkv_back(me, x, x_got, place, gain, shift, weight, dq, dk, dv, grad_middle):
    width, tokens = dq.shape
    own = pl.BlockSpec((TILE, width), place.own)
    got = pl.BlockSpec((TILE, width), place.got)
    turned = pl.BlockSpec((width, TILE), place.turned)
    return call(
        qkv_back_kernel,
        "qkv_backward",
        (place.steps,),
        [own, got, whole((1, width)), whole((1, width)), whole(weight.shape), turned, turned, turned,
         pl.BlockSpec((TILE, width), lambda t, me: (t, 0))],
        [own, got, whole((3 * width, width)), whole((16, width)), whole((2, width, 128))],
        [
            jax.ShapeDtypeStruct((tokens, width), f32),
            jax.ShapeDtypeStruct((tokens // 2, width), bf16),
            jax.ShapeDtypeStruct((3 * width, width), bf16),
            jax.ShapeDtypeStruct((16, width), f32),
            jax.ShapeDtypeStruct((2, width, 128), f32),
        ],
        [
            pltpu.VMEM((3 * width, width), f32),
            pltpu.VMEM((16, width), f32),
            pltpu.VMEM((2, width, 128), f32),
        ],
        4 * tokens * width * 3 * width,
        tokens * width * 20,
        62,
    )(me, x, x_got, gain[None], shift[None], weight, dq, dk, dv, grad_middle)


MESH = pl.DeviceIdType.MESH
PARTS = 6


def bits_of(rows):
    bits = [("rows", 1 << i) for i in range(rows.bit_length() - 1)]
    return bits[0], bits[1:] + [("seq", 1)], bits[2:] + bits[1:2] + [("seq", 1)]


def bit_value(bit):
    axis, weight = bit
    return lax.rem(lax.div(lax.axis_index(axis), weight), 2)


def partner(bit):
    axis, weight = bit
    return {axis: lax.axis_index(axis) + weight * (1 - 2 * bit_value(bit))}


def reduce_kernel(
    rows, one_ref, two_ref, small_ref, out_ref, two_out_ref, small_out_ref,
    buf, full, core_recv, recv, lines, line_recv, sems, core_sems, line_sems, local_sem,
):
    core, order_a, order_b = bits_of(rows)
    stages = len(order_a)
    total = buf.shape[0]
    part = total // 2 // PARTS
    orders = [order_b if p == 1 else order_a for p in range(PARTS)]

    barrier = pltpu.get_barrier_semaphore()
    for bit in [core] + order_a:
        pl.semaphore_signal(barrier, inc=1, device_id=partner(bit), device_id_type=MESH)
    split, depth = one_ref.shape[0], two_ref.shape[0]
    loads = [
        pltpu.make_async_copy(one_ref, buf.at[pl.ds(0, split)], local_sem.at[0]),
        pltpu.make_async_copy(two_ref, buf.at[pl.ds(split, depth)], local_sem.at[1]),
    ]
    for load in loads:
        load.start()
    lines[0] = small_ref[...]
    for load in loads:
        load.wait()
    pl.semaphore_wait(barrier, stages + 1)

    def ds(start, size):
        return pl.ds(pl.multiple_of(start, 16), size)

    def send(source, target, pair, bit):
        copy = pltpu.make_async_remote_copy(
            src_ref=source,
            dst_ref=target,
            send_sem=pair.at[0],
            recv_sem=pair.at[1],
            device_id=partner(bit),
            device_id_type=MESH,
        )
        copy.start()
        return copy

    line_bits = [core] + order_a

    def line_send(k):
        return send(lines.at[k], line_recv.at[k], line_sems.at[k], line_bits[k])

    def line_next(k, copy):
        copy.wait_recv()
        lines[k + 1] = lines[k] + line_recv[k]
        return copy

    sent = []
    mine = bit_value(core)
    copies = []
    for p in range(PARTS):
        other = (1 - mine) * (total // 2) + p * part
        copies.append(send(buf.at[ds(other, part)], core_recv.at[pl.ds(p * part, part)], core_sems.at[0, p], core))
    line = line_send(0)
    offsets = []
    for p in range(PARTS):
        copies[p].wait_recv()
        sent.append(copies[p])
        at = mine * (total // 2) + p * part
        offsets.append(at)
        buf[ds(at, part), :] = (
            buf[ds(at, part), :].astype(f32) + core_recv[p * part : (p + 1) * part, :].astype(f32)
        ).astype(bf16)
        copies[p] = None

    def halve(p, s):
        half = part >> (s + 1)
        bit = orders[p][s]
        value = bit_value(bit)
        base = part - (part >> s)
        copy = send(
            buf.at[ds(offsets[p] + (1 - value) * half, half)],
            recv.at[p, pl.ds(base, half)],
            sems.at[0, p, s],
            bit,
        )
        offsets[p] = offsets[p] + value * half
        return copy

    def settle(p, s, copy):
        half = part >> (s + 1)
        base = part - (part >> s)
        copy.wait_recv()
        sent.append(copy)
        rows_at = ds(offsets[p], half)
        total_now = buf[rows_at, :].astype(f32) + recv[p, base : base + half, :].astype(f32)
        return rows_at, total_now.astype(bf16)

    copies = [halve(p, 0) for p in range(PARTS)]
    line = line_next(0, line)
    sent.append(line)
    line = line_send(1)
    for s in range(1, stages):
        for p in range(PARTS):
            at, value = settle(p, s - 1, copies[p])
            buf[at, :] = value
            copies[p] = halve(p, s)
        line = line_next(s, line)
        sent.append(line)
        line = line_send(s + 1)

    def double(p, s):
        size = part >> (s + 1)
        bit = orders[p][s]
        at = ds(offsets[p], size)
        copy = send(full.at[at], full.at[at], sems.at[1, p, s], bit)
        offsets[p] = offsets[p] - bit_value(bit) * size
        return copy

    for p in range(PARTS):
        at, value = settle(p, stages - 1, copies[p])
        full[at, :] = value
        copies[p] = double(p, stages - 1)
    line = line_next(stages, line)
    sent.append(line)
    small_out_ref[...] = lines[stages + 1]
    for s in reversed(range(stages - 1)):
        for p in range(PARTS):
            copies[p].wait_recv()
            sent.append(copies[p])
            copies[p] = double(p, s)
    for p in range(PARTS):
        copies[p].wait_recv()
        sent.append(copies[p])
        at = ds(offsets[p], part)
        copies[p] = send(full.at[at], full.at[at], core_sems.at[1, p], core)
    for p in range(PARTS):
        copies[p].wait_recv()
        sent.append(copies[p])
    wide = full.shape[1]
    stores = []
    for i in range(total // depth):
        here = full.at[i * depth : (i + 1) * depth, :]
        there = out_ref.at[:, i * wide : (i + 1) * wide] if i * depth < split else two_out_ref
        stores.append(pltpu.make_async_copy(here, there, local_sem.at[2 + i]))
        stores[-1].start()
    for copy in sent:
        copy.wait_send()
    for store in stores:
        store.wait()


def sum_everywhere(one, two, small):
    rows = lax.axis_size("rows")
    depth, width = two.shape
    total = one.shape[0] + depth
    stages = len(bits_of(rows)[1])
    part = total // 2 // PARTS
    anywhere = pl.BlockSpec(memory_space=pl.ANY)
    vmem = pl.BlockSpec(memory_space=pltpu.VMEM)
    return pl.pallas_call(
        partial(reduce_kernel, rows),
        out_shape=[
            jax.ShapeDtypeStruct((depth, one.shape[0] // depth * width), bf16),
            jax.ShapeDtypeStruct(two.shape, bf16),
            jax.ShapeDtypeStruct(small.shape, f32),
        ],
        in_specs=[anywhere, anywhere, vmem],
        out_specs=[anywhere, anywhere, vmem],
        scratch_shapes=[
            pltpu.VMEM((total, width), bf16),
            pltpu.VMEM((total, width), bf16),
            pltpu.VMEM((total // 2, width), bf16),
            pltpu.VMEM((PARTS, part, width), bf16),
            pltpu.VMEM((stages + 2,) + small.shape, f32),
            pltpu.VMEM((stages + 1,) + small.shape, f32),
            pltpu.SemaphoreType.DMA((2, PARTS, stages, 2)),
            pltpu.SemaphoreType.DMA((2, PARTS, 2)),
            pltpu.SemaphoreType.DMA((stages + 1, 2)),
            pltpu.SemaphoreType.DMA((2 + total // depth,)),
        ],
        compiler_params=pltpu.CompilerParams(
            collective_id=0, has_side_effects=True, vmem_limit_bytes=40 * MIB
        ),
        cost_estimate=pl.CostEstimate(flops=total * width * 2, bytes_accessed=total * width * 4, transcendentals=0),
        name="sum_everywhere",
    )(one, two, small)


def place_kernel(me_ref, got_ref, _, out_ref):
    out_ref[...] = got_ref[...].astype(out_ref.dtype)


def put_in_place(me, got, target, place):
    width = got.shape[1]
    return call(
        place_kernel,
        "place_half",
        (place.phase,),
        [pl.BlockSpec((TILE, width), lambda t, me: (t, 0)), pl.BlockSpec(memory_space=pl.ANY)],
        pl.BlockSpec((TILE, width), place.back),
        jax.ShapeDtypeStruct(target.shape, target.dtype),
        [],
        0,
        got.size * 6,
        32,
        aliases={2: 0},
    )(me, got, target)


def swap(value):
    return lax.ppermute(value, "seq", [(0, 1), (1, 0)])


def after(value, *others):
    return lax.optimization_barrier((value,) + others)[0]


def row_local(
    block_input, segment_ids, norm1_gain, norm1_shift, qkv_weight, qv_bias, proj_weight, proj_bias,
    norm2_gain, norm2_shift, fc_weight, fc_bias, out_weight, out_bias, out_cotangent,
):
    held, half_len, width = block_input.shape
    rows, length = held // 2, 2 * half_len
    tokens = rows * length
    place = Place(rows, half_len)
    side = lax.axis_index("seq").astype(jnp.int32)
    first_side = side == 0

    def outgoing(value, row):
        return lax.dynamic_index_in_dim(value, row, 0, keepdims=False)

    me = side[None]
    left_rows = [(1 - side) * rows + r for r in range(rows)]
    x_out = outgoing(block_input, left_rows[0])
    x_parts = [swap(x_out)]
    mine = lax.dynamic_slice_in_dim(segment_ids, side * rows, rows, 0)
    other = swap(after(lax.dynamic_slice_in_dim(segment_ids, (1 - side) * rows, rows, 0), x_out))

    segments = jnp.concatenate((jnp.where(first_side, mine, other), jnp.where(first_side, other, mine)), axis=1)
    slot = jnp.arange(length, dtype=jnp.int32)[None]
    ends = [jnp.sum((segments <= doc).astype(jnp.int32), axis=1, keepdims=True) for doc in range(2)]
    start = jnp.where(
        segments == 0, 0, jnp.where(segments == 1, ends[0], jnp.where(segments == 2, ends[1], slot))
    )
    low = start[:, ::BLOCK] // BLOCK
    blocks = length // BLOCK
    high = jnp.sum((low[:, None, :] <= jnp.arange(blocks)[None, :, None]).astype(jnp.int32), axis=2) - 1
    start = start[:, None, :]
    low = low.reshape(-1)
    high = high.reshape(-1)

    x = block_input.reshape(held * half_len, width)
    cot = out_cotangent.reshape(held * half_len, width)
    bias = jnp.concatenate((qv_bias[:width], jnp.zeros((width,), f32), qv_bias[width:]))[:, None]
    params = (norm1_gain[None], norm1_shift[None], jnp.transpose(qkv_weight), bias)
    qkv = project_qkv(me, x, params, place, 0, place.phase, False, (), ())
    attended = ()
    for row in range(rows):
        if row + 1 < rows:
            x_parts.append(swap(after(outgoing(block_input, left_rows[row + 1]), x_parts[row], qkv[0])))
        qkv = project_qkv(
            me, x_parts[row], params, place, place.phase + row * place.per, place.per, True, qkv, attended[:1]
        )
        parts = 2 if row + 2 == rows else 1
        for part in range(parts):
            attended = attend(low, start, *qkv, row, length, part, parts, attended)
            if part + 1 < parts:
                cot_out = jnp.concatenate([outgoing(out_cotangent, left_rows[r]) for r in range(rows)], axis=0)
                cot_got = swap(after(cot_out, x_parts[row + 1], attended[1]))
    att, lse = attended
    x_got = jnp.concatenate(x_parts, axis=0)

    y, y_sent, grad_middle, grad_att, delta, dfc, dout, dproj, small_two, dfcb = feed_forward(
        me, x, x_got, cot, cot_got, att, place, proj_weight, proj_bias, norm2_gain, norm2_shift, fc_weight, fc_bias,
        out_weight, out_bias
    )
    dfc, dout = lax.psum((dfc, dout), ("rows", "seq"))
    y_got = swap(y_sent)
    dq, dk, dv = attend_back(high, start, *qkv, grad_att, lse, delta, rows)
    y = put_in_place(me, y_got, y, place)
    dq = after(dq, y)
    dx, dx_sent, dqkv, small_one, small_qv = qkv_back(
        me, x, x_got, place, norm1_gain, norm1_shift, qkv_weight, dq, dk, dv, grad_middle
    )
    dx_got = swap(dx_sent)
    small = jnp.sum(jnp.concatenate((small_two, small_one), axis=0).reshape(-1, 8, width), axis=1)
    small = jnp.concatenate(
        (small, jnp.sum(small_qv, axis=2), jnp.sum(dfcb, axis=0).reshape(-1, width)), axis=0
    )
    lines = small.shape[0]
    small = jnp.pad(small, ((0, -lines % 8), (0, 0)))
    dqkv, dproj, small = sum_everywhere(dqkv, dproj, small)
    layer_output = y.reshape(held, half_len, width)
    input_grad = put_in_place(me, dx_got, dx, place).reshape(held, half_len, width)

    return (
        layer_output,
        input_grad,
        small[4],
        small[5],
        dqkv.astype(f32),
        small[6:8].reshape(-1),
        dproj.astype(f32),
        small[3],
        small[0],
        small[1],
        dfc.astype(f32),
        small[8:lines].reshape(-1),
        dout.astype(f32),
        small[2],
    )


def solution(mesh):
    rows_spec = P("rows", "seq", None)
    in_specs = (rows_spec, P("rows", "seq")) + (P(),) * 12 + (rows_spec,)
    out_specs = (rows_spec, rows_spec) + (P(),) * 12
    body = row_local if mesh.shape["seq"] == 2 else local
    return jax.shard_map(body, mesh=mesh, in_specs=in_specs, out_specs=out_specs, check_vma=False)
```

```python
from functools import partial, reduce

import jax
import jax.numpy as jnp
from jax import lax
from jax.experimental import pallas as pl
from jax.experimental.pallas import tpu as pltpu
from jax.sharding import PartitionSpec as P

HEADS = 12
HEAD_DIM = 64


BRANCH = 12 ** (-0.5)
EPSILON = 1e-05
PADDING = 3.0
NEGATIVE = -1e30
block_keys = 256


def layer_norm(values, scale_gain, shift_bias):
    center = values - jnp.mean(values, axis=-1, keepdims=True)
    variance = jnp.mean(center * center, axis=-1, keepdims=True)
    return center * lax.rsqrt(variance + EPSILON) * scale_gain + shift_bias


def allowed_pairs(query_segments, key_segments, query_slots, key_slots):
    same_doc = query_segments[:, :, None] == key_segments[:, None, :]
    causal = key_slots[None, None, :] <= query_slots[None, :, None]
    itself = key_slots[None, None, :] == query_slots[None, :, None]
    unpadded = key_segments[:, None, :] != PADDING
    return (same_doc & causal & (unpadded | itself))[:, None]


def split_heads(block_rows):
    return block_rows.reshape(block_rows.shape[0], block_rows.shape[1], HEADS, HEAD_DIM)


def fold_blocks(block_step, running, piece_tuple):
    piece_len = piece_tuple[0].shape[1]

    def one_block(block_index, held_state):
        offset = block_index * block_keys
        sub_tuple = tuple(
            (lax.dynamic_slice_in_dim(member, offset, block_keys, 1) for member in piece_tuple)
        )
        return block_step(held_state, sub_tuple, offset)

    return lax.fori_loop(0, piece_len // block_keys, one_block, running)


def keep_same(running):
    return running


def local(
    block_input,
    segment_ids,
    norm1_gain,
    norm1_shift,
    qkv_weight,
    qv_bias,
    proj_weight,
    proj_bias,
    norm2_gain,
    norm2_shift,
    fc_weight,
    fc_bias,
    out_weight,
    out_bias,
    out_cotangent,
):
    row_count, local_len, model_width = block_input.shape
    tokens = row_count * local_len
    full_len = local_len * lax.axis_size("seq")
    my_first = lax.axis_index("seq") * local_len
    query_slots = my_first + jnp.arange(local_len)
    my_segments = segment_ids.astype(jnp.bfloat16)
    my_seg_float = segment_ids.astype(jnp.float32)
    score_scale = HEAD_DIM ** (-0.5)
    inputs = block_input.astype(jnp.float32).reshape(tokens, model_width)
    normed_one = layer_norm(inputs, norm1_gain, norm1_shift).astype(jnp.bfloat16)
    mixed_qkv = jnp.dot(normed_one, qkv_weight, preferred_element_type=jnp.float32)
    query_flat = (
        (mixed_qkv[:, :model_width] + qv_bias[:model_width])
        .astype(jnp.bfloat16)
        .reshape(row_count, local_len, model_width)
    )
    key_rows = (
        mixed_qkv[:, model_width : 2 * model_width]
        .astype(jnp.bfloat16)
        .reshape(row_count, local_len, model_width)
    )
    value_rows = (
        (mixed_qkv[:, 2 * model_width :] + qv_bias[model_width:])
        .astype(jnp.bfloat16)
        .reshape(row_count, local_len, model_width)
    )
    queries = split_heads(query_flat)

    def attend_block(running, sub_tuple, first_slot):
        key_piece, value_piece, seg_piece = sub_tuple
        piece_len = key_piece.shape[1]
        key_slots = first_slot + jnp.arange(piece_len)
        seg_float = seg_piece.astype(jnp.float32)
        skipped = (first_slot > my_first + local_len - 1) | (
            jnp.max(seg_float) < jnp.min(my_seg_float)
        )

        def attend_update(state):
            running_max, running_sum, running_out = state
            scores = (
                jnp.einsum(
                    "rqhd,rkhd->rhqk",
                    queries,
                    split_heads(key_piece),
                    preferred_element_type=jnp.float32,
                )
                * score_scale
            )
            allowed = allowed_pairs(my_seg_float, seg_float, query_slots, key_slots)
            masked = jnp.where(allowed, scores, NEGATIVE)
            new_max = jnp.maximum(running_max, jnp.max(masked, axis=-1))
            prob_block = jnp.where(allowed, jnp.exp(scores - new_max[..., None]), 0.0)
            factor = jnp.exp(running_max - new_max)
            new_sum = running_sum * factor + jnp.sum(prob_block, axis=-1)
            added_part = jnp.einsum(
                "rhqk,rkhd->rqhd",
                prob_block.astype(jnp.bfloat16),
                split_heads(value_piece),
                preferred_element_type=jnp.float32,
            )
            new_out = running_out * jnp.transpose(factor, (0, 2, 1))[..., None] + added_part
            return (new_max, new_sum, new_out)

        return lax.cond(skipped, keep_same, attend_update, running)

    start_state = (
        jnp.full((row_count, HEADS, local_len), NEGATIVE, jnp.float32),
        jnp.zeros((row_count, HEADS, local_len), jnp.float32),
        jnp.zeros((row_count, local_len, HEADS, HEAD_DIM), jnp.float32),
    )
    running_max, running_sum, running_out = fold_blocks(
        attend_block,
        start_state,
        (
            lax.all_gather(key_rows, "seq", axis=1, tiled=True),
            lax.all_gather(value_rows, "seq", axis=1, tiled=True),
            lax.all_gather(my_segments, "seq", axis=1, tiled=True),
        ),
    )
    log_total = running_max + jnp.log(running_sum)
    attended_heads = running_out / jnp.transpose(running_sum, (0, 2, 1))[..., None]
    attended_low = attended_heads.reshape(tokens, model_width).astype(jnp.bfloat16)
    branch_one = jnp.dot(attended_low, proj_weight, preferred_element_type=jnp.float32) + proj_bias
    middle = inputs + BRANCH * branch_one
    normed_two = layer_norm(middle, norm2_gain, norm2_shift).astype(jnp.bfloat16)
    hidden_pre = jnp.dot(normed_two, fc_weight, preferred_element_type=jnp.float32) + fc_bias
    hidden_act = jax.nn.gelu(hidden_pre, approximate=True).astype(jnp.bfloat16)
    branch_two = jnp.dot(hidden_act, out_weight, preferred_element_type=jnp.float32) + out_bias
    layer_output = (
        (middle + BRANCH * branch_two)
        .astype(jnp.bfloat16)
        .reshape(row_count, local_len, model_width)
    )
    flat_cot = out_cotangent.reshape(tokens, model_width).astype(jnp.float32)
    grad_two = (BRANCH * flat_cot).astype(jnp.bfloat16)
    grad_out_weight = jnp.einsum(
        "tf,td->fd", hidden_act, grad_two, preferred_element_type=jnp.float32
    )
    grad_out_bias = jnp.sum(grad_two.astype(jnp.float32), axis=0)
    grad_act = jnp.einsum("td,fd->tf", grad_two, out_weight, preferred_element_type=jnp.float32)
    gelu_value, gelu_pull = jax.vjp(partial(jax.nn.gelu, approximate=True), hidden_pre)
    grad_pre = gelu_pull(grad_act)[0].astype(jnp.bfloat16)
    grad_fc_weight = jnp.einsum(
        "td,tf->df", normed_two, grad_pre, preferred_element_type=jnp.float32
    )
    grad_fc_bias = jnp.sum(grad_pre.astype(jnp.float32), axis=0)
    grad_normed_two = jnp.einsum(
        "tf,df->td", grad_pre, fc_weight, preferred_element_type=jnp.float32
    )
    norm_value, norm_pull = jax.vjp(layer_norm, middle, norm2_gain, norm2_shift)
    grad_inner, grad_norm2_gain, grad_norm2_shift = norm_pull(grad_normed_two)
    grad_middle = flat_cot + grad_inner
    grad_one = (BRANCH * grad_middle).astype(jnp.bfloat16)
    grad_proj_weight = jnp.einsum(
        "td,te->de", attended_low, grad_one, preferred_element_type=jnp.float32
    )
    grad_proj_bias = jnp.sum(grad_one.astype(jnp.float32), axis=0)
    grad_attended_flat = (
        jnp.einsum("te,de->td", grad_one, proj_weight, preferred_element_type=jnp.float32)
        .astype(jnp.bfloat16)
        .reshape(row_count, local_len, model_width)
    )
    grad_attended = split_heads(grad_attended_flat)
    grad_delta = jnp.einsum("rqhd,rqhd->rhq", grad_attended.astype(jnp.float32), attended_heads)

    def back_block(running, sub_tuple, first_slot):
        key_piece, value_piece, seg_piece = sub_tuple
        piece_len = key_piece.shape[1]
        key_slots = first_slot + jnp.arange(piece_len)
        seg_float = seg_piece.astype(jnp.float32)
        skipped = (first_slot > my_first + local_len - 1) | (
            jnp.max(seg_float) < jnp.min(my_seg_float)
        )

        def back_update(state):
            grad_query, grad_full = state
            key_heads = split_heads(key_piece)
            value_heads = split_heads(value_piece)
            scores = (
                jnp.einsum(
                    "rqhd,rkhd->rhqk", queries, key_heads, preferred_element_type=jnp.float32
                )
                * score_scale
            )
            allowed = allowed_pairs(my_seg_float, seg_float, query_slots, key_slots)
            prob_block = jnp.where(allowed, jnp.exp(scores - log_total[..., None]), 0.0)
            grad_probs = jnp.einsum(
                "rqhd,rkhd->rhqk", grad_attended, value_heads, preferred_element_type=jnp.float32
            )
            grad_scores = (score_scale * prob_block * (grad_probs - grad_delta[..., None])).astype(
                jnp.bfloat16
            )
            new_query = grad_query + jnp.einsum(
                "rhqk,rkhd->rqhd", grad_scores, key_heads, preferred_element_type=jnp.float32
            )
            grad_keys = jnp.einsum(
                "rhqk,rqhd->rkhd", grad_scores, queries, preferred_element_type=jnp.float32
            ).reshape(row_count, piece_len, model_width)
            grad_values = jnp.einsum(
                "rhqk,rqhd->rkhd",
                prob_block.astype(jnp.bfloat16),
                grad_attended,
                preferred_element_type=jnp.float32,
            ).reshape(row_count, piece_len, model_width)
            held_part = lax.dynamic_slice_in_dim(grad_full, first_slot, piece_len, 2)
            new_full = lax.dynamic_update_slice_in_dim(
                grad_full, held_part + jnp.stack((grad_keys, grad_values)), first_slot, 2
            )
            return (new_query, new_full)

        return lax.cond(skipped, keep_same, back_update, running)

    back_start = (
        jnp.zeros((row_count, local_len, HEADS, HEAD_DIM), jnp.float32),
        jnp.zeros((2, row_count, full_len, model_width), jnp.float32),
    )
    grad_query, grad_full = fold_blocks(
        back_block,
        back_start,
        (
            lax.all_gather(key_rows, "seq", axis=1, tiled=True),
            lax.all_gather(value_rows, "seq", axis=1, tiled=True),
            lax.all_gather(my_segments, "seq", axis=1, tiled=True),
        ),
    )
    grad_pairs = lax.psum_scatter(
        grad_full.astype(jnp.bfloat16), "seq", scatter_dimension=2, tiled=True
    ).astype(jnp.float32)
    grad_query_low = grad_query.reshape(row_count, local_len, model_width).astype(jnp.bfloat16)
    grad_key_low = grad_pairs[0].astype(jnp.bfloat16)
    grad_value_low = grad_pairs[1].astype(jnp.bfloat16)
    grad_qkv_low = jnp.concatenate((grad_query_low, grad_key_low, grad_value_low), axis=-1).reshape(
        tokens, 3 * model_width
    )
    grad_qkv_weight = jnp.einsum(
        "td,te->de", normed_one, grad_qkv_low, preferred_element_type=jnp.float32
    )
    grad_qv_bias = jnp.concatenate(
        (
            jnp.sum(grad_query_low.astype(jnp.float32), axis=(0, 1)),
            jnp.sum(grad_value_low.astype(jnp.float32), axis=(0, 1)),
        )
    )
    grad_normed_one = jnp.einsum(
        "te,de->td", grad_qkv_low, qkv_weight, preferred_element_type=jnp.float32
    )
    first_value, first_pull = jax.vjp(layer_norm, inputs, norm1_gain, norm1_shift)
    grad_first, grad_norm1_gain, grad_norm1_shift = first_pull(grad_normed_one)
    input_grad = (grad_middle + grad_first).reshape(row_count, local_len, model_width)
    local_grads = (
        grad_norm1_gain,
        grad_norm1_shift,
        grad_qkv_weight,
        grad_qv_bias,
        grad_proj_weight,
        grad_proj_bias,
        grad_norm2_gain,
        grad_norm2_shift,
        grad_fc_weight,
        grad_fc_bias,
        grad_out_weight,
        grad_out_bias,
    )
    shares = (
        lax.psum_scatter(
            local_grads[0].astype(jnp.bfloat16), "rows", scatter_dimension=0, tiled=True
        ).astype(jnp.float32),
        lax.psum_scatter(
            local_grads[1].astype(jnp.bfloat16), "rows", scatter_dimension=0, tiled=True
        ).astype(jnp.float32),
        lax.psum_scatter(
            local_grads[2].astype(jnp.bfloat16), "rows", scatter_dimension=0, tiled=True
        ).astype(jnp.float32),
        lax.psum_scatter(
            local_grads[3].astype(jnp.bfloat16), "rows", scatter_dimension=0, tiled=True
        ).astype(jnp.float32),
        lax.psum_scatter(
            local_grads[4].astype(jnp.bfloat16), "rows", scatter_dimension=0, tiled=True
        ).astype(jnp.float32),
        lax.psum_scatter(
            local_grads[5].astype(jnp.bfloat16), "rows", scatter_dimension=0, tiled=True
        ).astype(jnp.float32),
        lax.psum_scatter(
            local_grads[6].astype(jnp.bfloat16), "rows", scatter_dimension=0, tiled=True
        ).astype(jnp.float32),
        lax.psum_scatter(
            local_grads[7].astype(jnp.bfloat16), "rows", scatter_dimension=0, tiled=True
        ).astype(jnp.float32),
        lax.psum_scatter(
            local_grads[8].astype(jnp.bfloat16), "rows", scatter_dimension=0, tiled=True
        ).astype(jnp.float32),
        lax.psum_scatter(
            local_grads[9].astype(jnp.bfloat16), "rows", scatter_dimension=0, tiled=True
        ).astype(jnp.float32),
        lax.psum_scatter(
            local_grads[10].astype(jnp.bfloat16), "rows", scatter_dimension=0, tiled=True
        ).astype(jnp.float32),
        lax.psum_scatter(
            local_grads[11].astype(jnp.bfloat16), "rows", scatter_dimension=0, tiled=True
        ).astype(jnp.float32),
    )
    shares = (
        lax.psum(shares[0].astype(jnp.bfloat16), "seq").astype(jnp.float32),
        lax.psum(shares[1].astype(jnp.bfloat16), "seq").astype(jnp.float32),
        lax.psum(shares[2].astype(jnp.bfloat16), "seq").astype(jnp.float32),
        lax.psum(shares[3].astype(jnp.bfloat16), "seq").astype(jnp.float32),
        lax.psum(shares[4].astype(jnp.bfloat16), "seq").astype(jnp.float32),
        lax.psum(shares[5].astype(jnp.bfloat16), "seq").astype(jnp.float32),
        lax.psum(shares[6].astype(jnp.bfloat16), "seq").astype(jnp.float32),
        lax.psum(shares[7].astype(jnp.bfloat16), "seq").astype(jnp.float32),
        lax.psum(shares[8].astype(jnp.bfloat16), "seq").astype(jnp.float32),
        lax.psum(shares[9].astype(jnp.bfloat16), "seq").astype(jnp.float32),
        lax.psum(shares[10].astype(jnp.bfloat16), "seq").astype(jnp.float32),
        lax.psum(shares[11].astype(jnp.bfloat16), "seq").astype(jnp.float32),
    )
    totals = (
        lax.all_gather(shares[0].astype(jnp.bfloat16), "rows", axis=0, tiled=True).astype(
            jnp.float32
        ),
        lax.all_gather(shares[1].astype(jnp.bfloat16), "rows", axis=0, tiled=True).astype(
            jnp.float32
        ),
        lax.all_gather(shares[2].astype(jnp.bfloat16), "rows", axis=0, tiled=True).astype(
            jnp.float32
        ),
        lax.all_gather(shares[3].astype(jnp.bfloat16), "rows", axis=0, tiled=True).astype(
            jnp.float32
        ),
        lax.all_gather(shares[4].astype(jnp.bfloat16), "rows", axis=0, tiled=True).astype(
            jnp.float32
        ),
        lax.all_gather(shares[5].astype(jnp.bfloat16), "rows", axis=0, tiled=True).astype(
            jnp.float32
        ),
        lax.all_gather(shares[6].astype(jnp.bfloat16), "rows", axis=0, tiled=True).astype(
            jnp.float32
        ),
        lax.all_gather(shares[7].astype(jnp.bfloat16), "rows", axis=0, tiled=True).astype(
            jnp.float32
        ),
        lax.all_gather(shares[8].astype(jnp.bfloat16), "rows", axis=0, tiled=True).astype(
            jnp.float32
        ),
        lax.all_gather(shares[9].astype(jnp.bfloat16), "rows", axis=0, tiled=True).astype(
            jnp.float32
        ),
        lax.all_gather(shares[10].astype(jnp.bfloat16), "rows", axis=0, tiled=True).astype(
            jnp.float32
        ),
        lax.all_gather(shares[11].astype(jnp.bfloat16), "rows", axis=0, tiled=True).astype(
            jnp.float32
        ),
    )
    return (layer_output, input_grad) + tuple(totals)


MIB = 1 << 20
LOG2E = 1.4426950408889634
GELU_C = 0.7978845608028654
GELU_A = 0.044715
BLOCK = 256
f32 = jnp.float32
bf16 = jnp.bfloat16


def dot_nn(a, b):
    return lax.dot_general(a, b, (((1,), (0,)), ((), ())), preferred_element_type=f32)


def dot_tn(a, b):
    return lax.dot_general(a, b, (((0,), (0,)), ((), ())), preferred_element_type=f32)


def dot_nt(a, b):
    return lax.dot_general(a, b, (((1,), (1,)), ((), ())), preferred_element_type=f32)


def norm_parts(values):
    center = values - jnp.mean(values, axis=-1, keepdims=True)
    variance = jnp.mean(center * center, axis=-1, keepdims=True)
    inverse = lax.rsqrt(variance + EPSILON)
    return center * inverse, inverse


def row_sums(values):
    rows, cols = values.shape
    return jnp.sum(values.reshape(rows // 8, 8, cols), axis=0)


def whole(shape):
    return pl.BlockSpec(shape, lambda *_: (0,) * len(shape), pipeline_mode=pl.Buffered(1))


def call(
    kernel, name, grid, in_specs, out_specs, out_shape, scratch, flops, moved, vmem, prefetch=1, aliases=None
):
    return pl.pallas_call(
        kernel,
        out_shape=out_shape,
        grid_spec=pltpu.PrefetchScalarGridSpec(
            num_scalar_prefetch=prefetch,
            grid=grid,
            in_specs=in_specs,
            out_specs=out_specs,
            scratch_shapes=scratch,
        ),
        compiler_params=pltpu.CompilerParams(vmem_limit_bytes=vmem * MIB),
        cost_estimate=pl.CostEstimate(flops=flops, bytes_accessed=moved, transcendentals=0),
        input_output_aliases=aliases or {},
        name=name,
    )


TILE = 512
LIMIT = 2.0**100


class Place:
    def __init__(self, rows, half_len):
        self.rows, self.per = rows, half_len // TILE
        self.phase = rows * self.per
        self.steps = 2 * self.phase

    def own(self, t, me):
        return me[0] * self.phase + jnp.minimum(t, self.phase - 1), 0

    def got(self, t, me):
        return jnp.maximum(t - self.phase, 0), 0

    def slot(self, t, me):
        late = t // self.phase
        half = jnp.where(late == 0, me[0], 1 - me[0])
        at = t - late * self.phase
        return (at // self.per) * 2 * self.per + half * self.per + at % self.per

    def turned(self, t, me):
        return 0, self.slot(t, me)

    def back(self, t, me):
        return (1 - me[0]) * self.phase + t, 0


def either(step, phase, own_ref, got_ref):
    return jnp.where(step < phase, own_ref[...], got_ref[...])


def qkv_kernel(me_ref, x_ref, gain_ref, shift_ref, w_ref, bias_ref, *refs):
    width = x_ref.shape[1]
    hat, _ = norm_parts(x_ref[...].astype(f32))
    normed = (hat * gain_ref[...] + shift_ref[...]).astype(bf16)
    for i, ref in enumerate(refs[-3:]):
        part = dot_nt(w_ref[i * width : (i + 1) * width, :], normed)
        if i != 1:
            part = part + bias_ref[i * width : (i + 1) * width, :]
        ref[...] = part.astype(bf16)


def project_qkv(me, x, params, place, first, count, got, earlier, after):
    width = x.shape[1]
    tokens = place.steps * TILE
    index = (lambda t, me: (t, 0)) if got else (lambda t, me: place.own(t + first, me))
    turned = pl.BlockSpec((width, TILE), lambda t, me: place.turned(t + first, me))
    anywhere = pl.BlockSpec(memory_space=pl.ANY)
    extra = list(earlier) + list(after)
    return call(
        qkv_kernel,
        "qkv_forward",
        (count,),
        [pl.BlockSpec((TILE, width), index)]
        + [whole(p.shape) for p in params]
        + [anywhere] * len(extra),
        [turned] * 3,
        [jax.ShapeDtypeStruct((width, tokens), bf16)] * 3,
        [],
        2 * count * TILE * width * 3 * width,
        count * TILE * width * 8 + width * width * 6,
        60,
        aliases={6 + i: i for i in range(len(earlier))},
    )(me, x, *params, *extra)


def attend_kernel(low_ref, start_ref, qt_ref, kt_ref, vt_ref, *refs, row, first, blocks):
    att_ref, lse_ref, acc, base, bias = refs[-5:]
    width, length = qt_ref.shape
    heads = width // HEAD_DIM
    pad = HEAD_DIM + 16
    scale = HEAD_DIM**-0.5 * LOG2E
    slots = lax.broadcasted_iota(jnp.int32, (BLOCK, BLOCK), 0)
    query_iota = lax.broadcasted_iota(jnp.int32, (BLOCK, BLOCK), 1)
    ones = jnp.ones((16, BLOCK), bf16)

    def at(i):
        return pl.ds(pl.multiple_of(i * BLOCK, BLOCK), BLOCK)

    def head_rows(h):
        return slice(h * HEAD_DIM, (h + 1) * HEAD_DIM)

    def acc_rows(h):
        return slice(h * pad, (h + 1) * pad)

    def total(h):
        return acc[h * pad + HEAD_DIM : h * pad + HEAD_DIM + 1, :]

    def score(h, qb, kb):
        return dot_tn(kt_ref[head_rows(h), at(kb)], qt_ref[head_rows(h), at(qb - first)])

    def weigh(h, kb, probs):
        return dot_nn(jnp.concatenate((vt_ref[head_rows(h), at(kb)], ones), axis=0), probs)

    def set_bias(qb, kb):
        allowed = (slots >= start_ref[0, :, at(qb - first)] - kb * BLOCK) & (
            slots + (kb - qb) * BLOCK <= query_iota
        )
        bias[...] = jnp.where(allowed, 0.0, NEGATIVE)

    def query_block(qb, carry):
        low = low_ref[row * blocks + qb]
        for h in range(heads):
            own = qt_ref[head_rows(h), at(qb - first)].astype(f32) * kt_ref[head_rows(h), at(qb)].astype(f32)
            base[h : h + 1, :] = jnp.sum(own, axis=0, keepdims=True) * scale
        acc[...] = jnp.zeros_like(acc)

        def fast(kb, carry):
            set_bias(qb, kb)

            def finish(h, probs):
                acc[acc_rows(h), :] += weigh(h, kb, probs)

            ahead = [score(h, qb, kb) for h in range(min(3, heads))]
            waiting = []
            for h in range(heads):
                scores = ahead.pop(0)
                if h + 3 < heads:
                    ahead.append(score(h + 3, qb, kb))
                probs = jnp.exp2(scores * scale + (bias[...] - base[h : h + 1, :]))
                waiting.append((h, probs.astype(bf16)))
                if len(waiting) > 1:
                    finish(*waiting.pop(0))
            finish(*waiting[0])
            return carry

        lax.fori_loop(low, qb + 1, fast, 0)
        largest = reduce(jnp.maximum, [total(h) for h in range(heads)])

        @pl.when(jnp.logical_not(jnp.max(largest) < LIMIT))
        def _():
            base[...] = jnp.full_like(base, NEGATIVE)
            acc[...] = jnp.zeros_like(acc)

            def safe(kb, carry):
                set_bias(qb, kb)
                for h in range(heads):
                    scores = score(h, qb, kb) * scale + bias[...]
                    old = base[h : h + 1, :]
                    top = jnp.maximum(old, jnp.max(scores, axis=0, keepdims=True))
                    base[h : h + 1, :] = top
                    probs = jnp.exp2(scores - top).astype(bf16)
                    acc[acc_rows(h), :] = acc[acc_rows(h), :] * jnp.exp2(old - top) + weigh(h, kb, probs)
                return carry

            lax.fori_loop(low, qb + 1, safe, 0)

        for h in range(heads):
            out = acc[h * pad : h * pad + HEAD_DIM, :]
            att_ref[head_rows(h), at(qb - first)] = (out / total(h)).astype(bf16)
            lse_ref[h // 2, h % 2 : h % 2 + 1, at(qb - first)] = base[h : h + 1, :] + jnp.log2(total(h))
        return carry

    lax.fori_loop(first, first + length // BLOCK, query_block, 0)


def attend(low, start, qt, kt, vt, row, length, part, parts, earlier):
    width, tokens = qt.shape
    heads = width // HEAD_DIM
    span = length // parts
    seen = span * (part + 1)
    column = row * parts + part
    queries = pl.BlockSpec((width, span), lambda i, low: (0, column))
    keys = pl.BlockSpec((width, seen), lambda i, low: (0, row * length // seen))
    lined = pl.BlockSpec((heads // 2, 2, span), lambda i, low: (0, 0, column))
    return call(
        partial(attend_kernel, row=row, first=part * span // BLOCK, blocks=length // BLOCK),
        "attention_forward",
        (1,),
        [pl.BlockSpec((1, 1, span), lambda i, low: (row, 0, part)), queries, keys, keys]
        + [pl.BlockSpec(memory_space=pl.ANY)] * len(earlier),
        [queries, lined],
        [
            jax.ShapeDtypeStruct((width, tokens), bf16),
            jax.ShapeDtypeStruct((heads // 2, 2, tokens), f32),
        ],
        [
            pltpu.VMEM((heads * (HEAD_DIM + 16), BLOCK), f32),
            pltpu.VMEM((16, BLOCK), f32),
            pltpu.VMEM((BLOCK, BLOCK), f32),
        ],
        2 * span * seen * width,
        length * width * 8,
        60,
        aliases={5 + i: i for i in range(len(earlier))},
    )(low, start, qt, kt, vt, *earlier)


def attend_back_kernel(
    high_ref, start_ref, qt_ref, kt_ref, vt_ref, dot_ref, lse_ref, delta_ref,
    dqt_ref, dkt_ref, dvt_ref, dq, dk, dv, bias,
):
    row = pl.program_id(0)
    width, length = qt_ref.shape
    heads = width // HEAD_DIM
    blocks = length // BLOCK
    scale = HEAD_DIM**-0.5 * LOG2E
    slots = lax.broadcasted_iota(jnp.int32, (BLOCK, BLOCK), 0)
    query_iota = lax.broadcasted_iota(jnp.int32, (BLOCK, BLOCK), 1)
    dq[...] = jnp.zeros_like(dq)

    def at(i):
        return pl.ds(pl.multiple_of(i * BLOCK, BLOCK), BLOCK)

    def key_block(kb, carry):
        k_at = at(kb)

        def visit(qb, first):
            q_at = at(qb)
            allowed = slots >= start_ref[0, :, q_at] - kb * BLOCK
            if first:
                allowed = allowed & (slots <= query_iota)
            bias[...] = jnp.where(allowed, 0.0, NEGATIVE)

            def begin(h):
                rows = slice(h * HEAD_DIM, (h + 1) * HEAD_DIM)
                return (
                    dot_tn(kt_ref[rows, k_at], qt_ref[rows, q_at]),
                    dot_tn(vt_ref[rows, k_at], dot_ref[rows, q_at]),
                )

            def finish(h, probs, grad_scores):
                rows = slice(h * HEAD_DIM, (h + 1) * HEAD_DIM)
                dv_new = dot_nt(dot_ref[rows, q_at], probs)
                dk_new = dot_nt(qt_ref[rows, q_at], grad_scores)
                dv[rows, :] = dv_new if first else dv[rows, :] + dv_new
                dk[rows, :] = dk_new if first else dk[rows, :] + dk_new
                dq[rows, q_at] += dot_nn(kt_ref[rows, k_at], grad_scores)

            ahead = [begin(0)]
            waiting = []
            for h in range(heads):
                scores, grad_probs = ahead.pop(0)
                if h + 1 < heads:
                    ahead.append(begin(h + 1))
                line = (h // 2, slice(h % 2, h % 2 + 1), q_at)
                probs = jnp.exp2(scores * scale + (bias[...] - lse_ref[line]))
                grad_scores = (probs * (grad_probs - delta_ref[line])).astype(bf16)
                waiting.append((h, probs.astype(bf16), grad_scores))
                if len(waiting) > 1:
                    finish(*waiting.pop(0))
            finish(*waiting[0])

        visit(kb, True)

        def later(qb, carry):
            visit(qb, False)
            return carry

        lax.fori_loop(kb + 1, high_ref[row * blocks + kb] + 1, later, 0)
        dkt_ref[:, k_at] = (dk[...] * HEAD_DIM**-0.5).astype(bf16)
        dvt_ref[:, k_at] = dv[...].astype(bf16)
        return carry

    lax.fori_loop(0, blocks, key_block, 0)
    dqt_ref[...] = (dq[...] * HEAD_DIM**-0.5).astype(bf16)


def attend_back(high, start, qt, kt, vt, dot, lse, delta, rows):
    width, tokens = qt.shape
    length = tokens // rows
    heads = width // HEAD_DIM
    turned = pl.BlockSpec((width, length), lambda r, high: (0, r))
    lined = pl.BlockSpec((heads // 2, 2, length), lambda r, high: (0, 0, r))
    return call(
        attend_back_kernel,
        "attention_backward",
        (rows,),
        [pl.BlockSpec((1, 1, length), lambda r, high: (r, 0, 0)), turned, turned, turned, turned, lined, lined],
        [turned] * 3,
        [jax.ShapeDtypeStruct((width, tokens), bf16)] * 3,
        [
            pltpu.VMEM((width, length), f32),
            pltpu.VMEM((width, BLOCK), f32),
            pltpu.VMEM((width, BLOCK), f32),
            pltpu.VMEM((BLOCK, BLOCK), f32),
        ],
        5 * tokens * length * width,
        tokens * width * 14,
        62,
    )(high, start, qt, kt, vt, dot, lse, delta)


def mlp_kernel(
    me_ref, x_ref, xg_ref, cot_ref, cotg_ref, att_ref, proj_ref, projb_ref, gain_ref, shift_ref, fc_ref, fcb_ref,
    out_ref, outb_ref,
    kept_ref, sent_ref, gm_ref, do_ref, delta_ref, dfc_ref, dout_ref, dproj_ref, small_ref, dfcb_ref,
    dfc, doutt, dproj, sums, dfcb, stage, stage_t, sem,
):
    step = pl.program_id(0)
    steps = pl.num_programs(0)
    phase = steps // 2
    tile, width = x_ref.shape
    hidden = fc_ref.shape[1]
    chunk = width

    @pl.when(step == 0)
    def _():
        dfc[...] = jnp.zeros_like(dfc)
        doutt[...] = jnp.zeros_like(doutt)
        dproj[...] = jnp.zeros_like(dproj)
        sums[...] = jnp.zeros_like(sums)
        dfcb[...] = jnp.zeros_like(dfcb)

    att_t = att_ref[...]
    x = either(step, phase, x_ref, xg_ref).astype(f32)
    middle = x + BRANCH * (dot_tn(att_t, proj_ref[...]) + projb_ref[...])
    hat, inverse = norm_parts(middle)
    normed = (hat * gain_ref[...] + shift_ref[...]).astype(bf16)
    normed_t = jnp.transpose(normed)
    cot = either(step, phase, cot_ref, cotg_ref).astype(f32)
    grad_two = (BRANCH * cot).astype(bf16)
    grad_two_t = jnp.transpose(grad_two)
    branch = jnp.zeros((tile, width), f32)
    grad_normed = jnp.zeros((tile, width), f32)
    for at in range(0, hidden, chunk):
        cols = slice(at, at + chunk)
        pre = dot_nn(normed, fc_ref[:, cols]) + fcb_ref[:, cols]
        grad_act = dot_nt(grad_two, out_ref[cols, :])
        square = pre * pre
        half = 0.5 + 0.5 * jnp.tanh(pre * (GELU_C + GELU_C * GELU_A * square))
        act = pre * half
        slope = half + act * (1.0 - half) * (2.0 * GELU_C + 6.0 * GELU_C * GELU_A * square)
        act = act.astype(bf16)
        grad_pre = (grad_act * slope).astype(bf16)
        branch += dot_nn(act, out_ref[cols, :])
        grad_normed += dot_nt(grad_pre, fc_ref[:, cols])
        dfc[:, cols] += dot_nn(normed_t, grad_pre)
        doutt[:, cols] += dot_nn(grad_two_t, act)
        dfcb[:, cols] += row_sums(grad_pre.astype(f32))
    y = (middle + BRANCH * (branch + outb_ref[...])).astype(bf16)

    scaled = grad_normed * gain_ref[...]
    mean_one = jnp.mean(scaled, axis=-1, keepdims=True)
    mean_two = jnp.mean(scaled * hat, axis=-1, keepdims=True)
    grad_middle = cot + inverse * (scaled - mean_one - hat * mean_two)
    gm_ref[...] = grad_middle.astype(bf16)
    grad_one = (BRANCH * grad_middle).astype(bf16)
    dproj[...] += dot_nn(att_t, grad_one)
    grad_att = dot_nt(proj_ref[...], grad_one).astype(bf16)
    do_ref[...] = grad_att
    product = grad_att.astype(f32) * att_t.astype(f32)
    for h in range(width // HEAD_DIM):
        part = product[h * HEAD_DIM : (h + 1) * HEAD_DIM, :]
        delta_ref[h // 2, h % 2 : h % 2 + 1, :] = jnp.sum(part, axis=0, keepdims=True)
    sums[0:8, :] += row_sums(grad_normed * hat)
    sums[8:16, :] += row_sums(grad_normed)
    sums[16:24, :] += row_sums(grad_two.astype(f32))
    sums[24:32, :] += row_sums(grad_one.astype(f32))

    @pl.when(step < phase)
    def _():
        kept_ref[...] = y

    @pl.when(step >= phase)
    def _():
        sent_ref[...] = y

    @pl.when(step == steps - 1)
    def _():
        copies = []
        piece = stage_t.shape[0]
        for i, at in enumerate(range(0, hidden, piece)):
            cols = slice(at, at + piece)
            if i > 0:
                copies[-2].wait()
            stage[...] = dfc[:, cols].astype(bf16)
            copies.append(pltpu.make_async_copy(stage, dfc_ref.at[:, cols], sem.at[0]))
            copies[-1].start()
            if i > 0:
                copies[-2].wait()
            stage_t[...] = jnp.transpose(doutt[:, cols].astype(bf16))
            copies.append(pltpu.make_async_copy(stage_t, dout_ref.at[cols, :], sem.at[1]))
            copies[-1].start()
        for copy in copies[-2:]:
            copy.wait()
        dproj_ref[...] = dproj[...].astype(bf16)
        small_ref[...] = sums[...]
        dfcb_ref[...] = dfcb[...]


def feed_forward(
    me, x, x_got, cot, cot_got, att, place, proj_weight, proj_bias, gain, shift, fc_weight, fc_bias, out_weight, out_bias
):
    width, tokens = att.shape
    hidden = fc_weight.shape[1]
    heads = width // HEAD_DIM
    own = pl.BlockSpec((TILE, width), place.own)
    got = pl.BlockSpec((TILE, width), place.got)
    turned = pl.BlockSpec((width, TILE), place.turned)
    plain = pl.BlockSpec((TILE, width), lambda t, me: (t, 0))
    anywhere = pl.BlockSpec(memory_space=pl.ANY)
    return call(
        mlp_kernel,
        "feed_forward",
        (place.steps,),
        [own, got, own, got, turned, whole((width, width)), whole((1, width)), whole((1, width)), whole((1, width)),
         whole(fc_weight.shape), whole((1, hidden)), whole(out_weight.shape), whole((1, width))],
        [own, got, plain, turned,
         pl.BlockSpec((heads // 2, 2, TILE), lambda t, me: (0, 0, place.slot(t, me))),
         anywhere, anywhere, whole((width, width)), whole((32, width)), whole((8, hidden))],
        [
            jax.ShapeDtypeStruct((tokens, width), bf16),
            jax.ShapeDtypeStruct((tokens // 2, width), bf16),
            jax.ShapeDtypeStruct((tokens, width), bf16),
            jax.ShapeDtypeStruct((width, tokens), bf16),
            jax.ShapeDtypeStruct((heads // 2, 2, tokens), f32),
            jax.ShapeDtypeStruct((width, hidden), bf16),
            jax.ShapeDtypeStruct((hidden, width), bf16),
            jax.ShapeDtypeStruct((width, width), bf16),
            jax.ShapeDtypeStruct((32, width), f32),
            jax.ShapeDtypeStruct((8, hidden), f32),
        ],
        [
            pltpu.VMEM((width, hidden), f32),
            pltpu.VMEM((width, hidden), f32),
            pltpu.VMEM((width, width), f32),
            pltpu.VMEM((32, width), f32),
            pltpu.VMEM((8, hidden), f32),
            pltpu.VMEM((width, width // 2), bf16),
            pltpu.VMEM((width // 2, width), bf16),
            pltpu.SemaphoreType.DMA((2,)),
        ],
        2 * tokens * width * (3 * width + 6 * hidden),
        tokens * width * 14,
        63,
    )(me, x, x_got, cot, cot_got, att, proj_weight, proj_bias[None], gain[None], shift[None], fc_weight, fc_bias[None],
      out_weight, out_bias[None])


def qkv_back_kernel(
    me_ref, x_ref, xg_ref, gain_ref, shift_ref, w_ref, dq_ref, dk_ref, dv_ref, gm_ref,
    kept_ref, sent_ref, dw_ref, small_ref, bias_ref, acc, sums, bias_sums,
):
    step = pl.program_id(0)
    steps = pl.num_programs(0)
    width = x_ref.shape[1]
    refs = (dq_ref, dk_ref, dv_ref)

    @pl.when(step == 0)
    def _():
        acc[...] = jnp.zeros_like(acc)
        sums[...] = jnp.zeros_like(sums)
        bias_sums[...] = jnp.zeros_like(bias_sums)

    hat, inverse = norm_parts(either(step, steps // 2, x_ref, xg_ref).astype(f32))
    normed_t = jnp.transpose((hat * gain_ref[...] + shift_ref[...]).astype(bf16))
    grad_t = sum(dot_nn(w_ref[:, i * width : (i + 1) * width], ref[...]) for i, ref in enumerate(refs))
    for i, ref in enumerate(refs):
        acc[i * width : (i + 1) * width, :] += dot_nt(normed_t, ref[...])
    grad_normed = jnp.transpose(grad_t)
    scaled = grad_normed * gain_ref[...]
    mean_one = jnp.mean(scaled, axis=-1, keepdims=True)
    mean_two = jnp.mean(scaled * hat, axis=-1, keepdims=True)
    grad_x = gm_ref[...].astype(f32) + inverse * (scaled - mean_one - hat * mean_two)
    sums[0:8, :] += row_sums(grad_normed * hat)
    sums[8:16, :] += row_sums(grad_normed)
    for i, ref in enumerate((dq_ref, dv_ref)):
        part = ref[...].astype(f32)
        bias_sums[i] += sum(part[:, j : j + 128] for j in range(0, part.shape[1], 128))

    @pl.when(step < steps // 2)
    def _():
        kept_ref[...] = grad_x

    @pl.when(step >= steps // 2)
    def _():
        sent_ref[...] = grad_x.astype(bf16)

    @pl.when(step == steps - 1)
    def _():
        dw_ref[...] = acc[...].astype(bf16)
        small_ref[...] = sums[...]
        bias_ref[...] = bias_sums[...]


def qkv_back(me, x, x_got, place, gain, shift, weight, dq, dk, dv, grad_middle):
    width, tokens = dq.shape
    own = pl.BlockSpec((TILE, width), place.own)
    got = pl.BlockSpec((TILE, width), place.got)
    turned = pl.BlockSpec((width, TILE), place.turned)
    return call(
        qkv_back_kernel,
        "qkv_backward",
        (place.steps,),
        [own, got, whole((1, width)), whole((1, width)), whole(weight.shape), turned, turned, turned,
         pl.BlockSpec((TILE, width), lambda t, me: (t, 0))],
        [own, got, whole((3 * width, width)), whole((16, width)), whole((2, width, 128))],
        [
            jax.ShapeDtypeStruct((tokens, width), f32),
            jax.ShapeDtypeStruct((tokens // 2, width), bf16),
            jax.ShapeDtypeStruct((3 * width, width), bf16),
            jax.ShapeDtypeStruct((16, width), f32),
            jax.ShapeDtypeStruct((2, width, 128), f32),
        ],
        [
            pltpu.VMEM((3 * width, width), f32),
            pltpu.VMEM((16, width), f32),
            pltpu.VMEM((2, width, 128), f32),
        ],
        4 * tokens * width * 3 * width,
        tokens * width * 20,
        62,
    )(me, x, x_got, gain[None], shift[None], weight, dq, dk, dv, grad_middle)


MESH = pl.DeviceIdType.MESH
PARTS = 6


def bits_of(rows):
    bits = [("rows", 1 << i) for i in range(rows.bit_length() - 1)]
    return bits[0], bits[1:] + [("seq", 1)], bits[2:] + bits[1:2] + [("seq", 1)]


def bit_value(bit):
    axis, weight = bit
    return lax.rem(lax.div(lax.axis_index(axis), weight), 2)


def partner(bit):
    axis, weight = bit
    return {axis: lax.axis_index(axis) + weight * (1 - 2 * bit_value(bit))}


def reduce_kernel(
    rows, one_ref, two_ref, second_ref, first_ref, qv_ref, hidden_ref, out_ref, two_out_ref, small_out_ref,
    buf, full, core_recv, recv, lines, line_recv, sems, core_sems, line_sems, local_sem,
):
    core, order_a, order_b = bits_of(rows)
    stages = len(order_a)
    total = buf.shape[0]
    part = total // 2 // PARTS
    orders = [order_b if p == 1 else order_a for p in range(PARTS)]

    barrier = pltpu.get_barrier_semaphore()
    for bit in [core] + order_a:
        pl.semaphore_signal(barrier, inc=1, device_id=partner(bit), device_id_type=MESH)
    split, depth = one_ref.shape[0], two_ref.shape[0]
    loads = [
        pltpu.make_async_copy(one_ref, buf.at[pl.ds(0, split)], local_sem.at[0]),
        pltpu.make_async_copy(two_ref, buf.at[pl.ds(split, depth)], local_sem.at[1]),
    ]
    for load in loads:
        load.start()
    width = buf.shape[1]
    values = [second_ref[i : i + 8, :] for i in range(0, second_ref.shape[0], 8)]
    values += [first_ref[i : i + 8, :] for i in range(0, first_ref.shape[0], 8)]
    values += [jnp.transpose(qv_ref[i]) for i in range(qv_ref.shape[0])]
    values += [hidden_ref[:, i : i + width] for i in range(0, hidden_ref.shape[1], width)]
    lines[0] = jnp.zeros(lines.shape[1:], f32)
    for i, value in enumerate(values):
        lines[0, i : i + 1, :] = jnp.sum(value, axis=0, keepdims=True)
    for load in loads:
        load.wait()
    pl.semaphore_wait(barrier, stages + 1)

    def ds(start, size):
        return pl.ds(pl.multiple_of(start, 16), size)

    def send(source, target, pair, bit):
        copy = pltpu.make_async_remote_copy(
            src_ref=source,
            dst_ref=target,
            send_sem=pair.at[0],
            recv_sem=pair.at[1],
            device_id=partner(bit),
            device_id_type=MESH,
        )
        copy.start()
        return copy

    line_bits = [core] + order_a

    def line_send(k):
        return send(lines.at[k], line_recv.at[k], line_sems.at[k], line_bits[k])

    def line_next(k, copy):
        copy.wait_recv()
        lines[k + 1] = lines[k] + line_recv[k]
        return copy

    sent = []
    mine = bit_value(core)
    copies = []
    for p in range(PARTS):
        other = (1 - mine) * (total // 2) + p * part
        copies.append(send(buf.at[ds(other, part)], core_recv.at[pl.ds(p * part, part)], core_sems.at[0, p], core))
    line = line_send(0)
    offsets = []
    for p in range(PARTS):
        copies[p].wait_recv()
        sent.append(copies[p])
        at = mine * (total // 2) + p * part
        offsets.append(at)
        buf[ds(at, part), :] = (
            buf[ds(at, part), :].astype(f32) + core_recv[p * part : (p + 1) * part, :].astype(f32)
        ).astype(bf16)
        copies[p] = None

    def halve(p, s):
        half = part >> (s + 1)
        bit = orders[p][s]
        value = bit_value(bit)
        base = part - (part >> s)
        copy = send(
            buf.at[ds(offsets[p] + (1 - value) * half, half)],
            recv.at[p, pl.ds(base, half)],
            sems.at[0, p, s],
            bit,
        )
        offsets[p] = offsets[p] + value * half
        return copy

    def settle(p, s, copy):
        half = part >> (s + 1)
        base = part - (part >> s)
        copy.wait_recv()
        sent.append(copy)
        rows_at = ds(offsets[p], half)
        total_now = buf[rows_at, :].astype(f32) + recv[p, base : base + half, :].astype(f32)
        return rows_at, total_now.astype(bf16)

    copies = [halve(p, 0) for p in range(PARTS)]
    line = line_next(0, line)
    sent.append(line)
    line = line_send(1)
    for s in range(1, stages):
        for p in range(PARTS):
            at, value = settle(p, s - 1, copies[p])
            buf[at, :] = value
            copies[p] = halve(p, s)
        line = line_next(s, line)
        sent.append(line)
        line = line_send(s + 1)

    def double(p, s):
        size = part >> (s + 1)
        bit = orders[p][s]
        at = ds(offsets[p], size)
        copy = send(full.at[at], full.at[at], sems.at[1, p, s], bit)
        offsets[p] = offsets[p] - bit_value(bit) * size
        return copy

    for p in range(PARTS):
        at, value = settle(p, stages - 1, copies[p])
        full[at, :] = value
        copies[p] = double(p, stages - 1)
    line = line_next(stages, line)
    sent.append(line)
    small_out_ref[...] = lines[stages + 1]
    for s in reversed(range(stages - 1)):
        for p in range(PARTS):
            copies[p].wait_recv()
            sent.append(copies[p])
            copies[p] = double(p, s)
    for p in range(PARTS):
        copies[p].wait_recv()
        sent.append(copies[p])
        at = ds(offsets[p], part)
        copies[p] = send(full.at[at], full.at[at], core_sems.at[1, p], core)
    for p in range(PARTS):
        copies[p].wait_recv()
        sent.append(copies[p])
    wide = full.shape[1]
    stores = []
    for i in range(total // depth):
        here = full.at[i * depth : (i + 1) * depth, :]
        there = out_ref.at[:, i * wide : (i + 1) * wide] if i * depth < split else two_out_ref
        stores.append(pltpu.make_async_copy(here, there, local_sem.at[2 + i]))
        stores[-1].start()
    for copy in sent:
        copy.wait_send()
    for store in stores:
        store.wait()


def sum_everywhere(one, two, second, first, qv, hidden):
    rows = lax.axis_size("rows")
    depth, width = two.shape
    total = one.shape[0] + depth
    stages = len(bits_of(rows)[1])
    part = total // 2 // PARTS
    count = (second.shape[0] + first.shape[0] + hidden.size // width) // 8 + qv.shape[0]
    small = jax.ShapeDtypeStruct((count + -count % 8, width), f32)
    anywhere = pl.BlockSpec(memory_space=pl.ANY)
    vmem = pl.BlockSpec(memory_space=pltpu.VMEM)
    return pl.pallas_call(
        partial(reduce_kernel, rows),
        out_shape=[
            jax.ShapeDtypeStruct((depth, one.shape[0] // depth * width), bf16),
            jax.ShapeDtypeStruct(two.shape, bf16),
            small,
        ],
        in_specs=[anywhere, anywhere, vmem, vmem, vmem, vmem],
        out_specs=[anywhere, anywhere, vmem],
        scratch_shapes=[
            pltpu.VMEM((total, width), bf16),
            pltpu.VMEM((total, width), bf16),
            pltpu.VMEM((total // 2, width), bf16),
            pltpu.VMEM((PARTS, part, width), bf16),
            pltpu.VMEM((stages + 2,) + small.shape, f32),
            pltpu.VMEM((stages + 1,) + small.shape, f32),
            pltpu.SemaphoreType.DMA((2, PARTS, stages, 2)),
            pltpu.SemaphoreType.DMA((2, PARTS, 2)),
            pltpu.SemaphoreType.DMA((stages + 1, 2)),
            pltpu.SemaphoreType.DMA((2 + total // depth,)),
        ],
        compiler_params=pltpu.CompilerParams(
            collective_id=0, has_side_effects=True, vmem_limit_bytes=60 * MIB
        ),
        cost_estimate=pl.CostEstimate(flops=total * width * 2, bytes_accessed=total * width * 4, transcendentals=0),
        name="sum_everywhere",
    )(one, two, second, first, qv, hidden)


def place_kernel(me_ref, got_ref, _, out_ref):
    out_ref[...] = got_ref[...].astype(out_ref.dtype)


def put_in_place(me, got, target, place):
    width = got.shape[1]
    return call(
        place_kernel,
        "place_half",
        (place.phase,),
        [pl.BlockSpec((TILE, width), lambda t, me: (t, 0)), pl.BlockSpec(memory_space=pl.ANY)],
        pl.BlockSpec((TILE, width), place.back),
        jax.ShapeDtypeStruct(target.shape, target.dtype),
        [],
        0,
        got.size * 6,
        32,
        aliases={2: 0},
    )(me, got, target)


def swap(value):
    return lax.ppermute(value, "seq", [(0, 1), (1, 0)])


def after(value, *others):
    return lax.optimization_barrier((value,) + others)[0]


def row_local(
    block_input, segment_ids, norm1_gain, norm1_shift, qkv_weight, qv_bias, proj_weight, proj_bias,
    norm2_gain, norm2_shift, fc_weight, fc_bias, out_weight, out_bias, out_cotangent,
):
    held, half_len, width = block_input.shape
    rows, length = held // 2, 2 * half_len
    tokens = rows * length
    place = Place(rows, half_len)
    side = lax.axis_index("seq").astype(jnp.int32)
    first_side = side == 0

    def outgoing(value, row):
        return lax.dynamic_index_in_dim(value, row, 0, keepdims=False)

    me = side[None]
    left_rows = [(1 - side) * rows + r for r in range(rows)]
    x_out = outgoing(block_input, left_rows[0])
    x_parts = [swap(x_out)]
    mine = lax.dynamic_slice_in_dim(segment_ids, side * rows, rows, 0)
    other = swap(after(lax.dynamic_slice_in_dim(segment_ids, (1 - side) * rows, rows, 0), x_out))

    segments = jnp.concatenate((jnp.where(first_side, mine, other), jnp.where(first_side, other, mine)), axis=1)
    slot = jnp.arange(length, dtype=jnp.int32)[None]
    ends = [jnp.sum((segments <= doc).astype(jnp.int32), axis=1, keepdims=True) for doc in range(2)]
    start = jnp.where(
        segments == 0, 0, jnp.where(segments == 1, ends[0], jnp.where(segments == 2, ends[1], slot))
    )
    low = start[:, ::BLOCK] // BLOCK
    blocks = length // BLOCK
    high = jnp.sum((low[:, None, :] <= jnp.arange(blocks)[None, :, None]).astype(jnp.int32), axis=2) - 1
    start = start[:, None, :]
    low = low.reshape(-1)
    high = high.reshape(-1)

    x = block_input.reshape(held * half_len, width)
    cot = out_cotangent.reshape(held * half_len, width)
    bias = jnp.concatenate((qv_bias[:width], jnp.zeros((width,), f32), qv_bias[width:]))[:, None]
    params = (norm1_gain[None], norm1_shift[None], jnp.transpose(qkv_weight), bias)
    qkv = project_qkv(me, x, params, place, 0, place.phase, False, (), ())
    attended = ()
    for row in range(rows):
        if row + 1 < rows:
            x_parts.append(swap(after(outgoing(block_input, left_rows[row + 1]), x_parts[row], qkv[0])))
        qkv = project_qkv(
            me, x_parts[row], params, place, place.phase + row * place.per, place.per, True, qkv, attended[:1]
        )
        parts = 2 if row + 2 == rows else 1
        for part in range(parts):
            attended = attend(low, start, *qkv, row, length, part, parts, attended)
            if part + 1 < parts:
                cot_out = lax.dynamic_slice_in_dim(out_cotangent, left_rows[0], rows, 0)
                cot_got = swap(after(cot_out, x_parts[row + 1], attended[1])).reshape(tokens // 2, width)
    att, lse = attended
    x_got = jnp.concatenate(x_parts, axis=0)

    y, y_sent, grad_middle, grad_att, delta, dfc, dout, dproj, small_two, dfcb = feed_forward(
        me, x, x_got, cot, cot_got, att, place, proj_weight, proj_bias, norm2_gain, norm2_shift, fc_weight, fc_bias,
        out_weight, out_bias
    )
    dfc, dout = lax.psum((dfc, dout), ("rows", "seq"))
    y_got = swap(y_sent)
    dq, dk, dv = attend_back(high, start, *qkv, grad_att, lse, delta, rows)
    y = put_in_place(me, y_got, y, place)
    dq = after(dq, y)
    dx, dx_sent, dqkv, small_one, small_qv = qkv_back(
        me, x, x_got, place, norm1_gain, norm1_shift, qkv_weight, dq, dk, dv, grad_middle
    )
    dx_got = swap(dx_sent)
    dqkv, dproj, small = sum_everywhere(dqkv, dproj, small_two, small_one, small_qv, dfcb)
    layer_output = y.reshape(held, half_len, width)
    input_grad = put_in_place(me, dx_got, dx, place).reshape(held, half_len, width)

    return (
        layer_output,
        input_grad,
        small[4],
        small[5],
        dqkv.astype(f32),
        small[6:8].reshape(-1),
        dproj.astype(f32),
        small[3],
        small[0],
        small[1],
        dfc.astype(f32),
        small[8 : 8 + dfcb.shape[1] // width].reshape(-1),
        dout.astype(f32),
        small[2],
    )


def solution(mesh):
    rows_spec = P("rows", "seq", None)
    in_specs = (rows_spec, P("rows", "seq")) + (P(),) * 12 + (rows_spec,)
    out_specs = (rows_spec, rows_spec) + (P(),) * 12
    body = row_local if mesh.shape["seq"] == 2 else local
    return jax.shard_map(body, mesh=mesh, in_specs=in_specs, out_specs=out_specs, check_vma=False)
```
